128 devices in a mesh: gx: 16 (over y, z), gy: 8 (over x, core).
Axes of the slice: x: 4, y: 4, z: 4, core: 2. Of those that a mesh axis runs over, the one named last changes fastest.
Arguments:
- obs_rows: float32 [262144, 128], P(('gx', 'gy')), may hold values from -6 to 6
- obs_tile: int32 [262144, 1], P(('gx', 'gy')), may hold values from 0 to 127; in each aligned block of 2048 rows (0 to 2047, 2048 to 4095, ...) at most 32 rows name the same one
- obs_cell: int32 [262144], P(('gx', 'gy')), may hold values from 0 to 2047
- land_sea: int32 [64, 128, 2048], P(None, 'gy', 'gx'), may hold values 0 or 1
- zonal_rate: float32 [64, 128, 2048], P(None, 'gy', 'gx'), may hold values from 0.03 to 0.24
- meridional_rate: float32 [64, 128, 2048], P(None, 'gy', 'gx'), may hold values from 0.03 to 0.24
Outputs:
- increment: float32 [2, 64, 128, 2048], P(None, None, 'gy', 'gx')
The draws below stay inside these ranges and needn't reach their ends.
Inputs may be any that keep to these rules, and one draw needn't show every extreme that they name: `obs_tile`: in the rows of one device, at most 32 observations name the same tile, a bound that some block reaches.
All inputs are finite; a program needn't handle non-finite values. No bound on the sum of `land_sea` on one device may be relied on, other than what follows from the above.
Results may differ from the reference program's by a relative error of at most 0.00002.
Values sent between devices are 32-bit elements; how exact they have to be, the bound alone decides.
No kernel may reach another device: no remote copies, remote signals or barrier semaphores. Data moves between devices by JAX's collectives and lax.ppermute only.
A program may use at most 64 MiB of HBM per device.

```python
import math
import jax
import jax.numpy as jnp
import numpy as np

VAR = 2
LEV = 64
LAT_DEV = 16
LON_DEV = 128
OBS_DEV = 2048
ITERS = 4
ROW = 128
NLAT = 128
NLON = 2048
OBS = 262144
CAP = 32
N_GY = 8
DEVICES = 128


def touch_ends(result, stream_key, least, high):
    place = [jax.random.randint(jax.random.fold_in(stream_key, axis), (), 0, length) for axis, length in enumerate(result.shape)]
    widest = result.shape.index(max(result.shape))
    next_to = place[:widest] + [(place[widest] + 1) % result.shape[widest]] + place[widest + 1:]
    return result.at[tuple(place)].set(least).at[tuple(next_to)].set(high)


def block_scale(rng, extent, shards, least, top_value):
    def one(dim, parts):
        steps = jax.random.uniform(jax.random.fold_in(jax.random.fold_in(rng, 6), dim), (parts,), jnp.float32, least / len(shards), top_value / len(shards))
        return jnp.repeat(jnp.exp(steps), extent[dim] // parts).reshape((-1,) + (1,) * (len(extent) - dim - 1))

    level = one(*shards[0])
    for cut in shards[1:]:
        level = level * one(*cut)
    return level


def routed_block(stream_key, own, number, rows, number_of, top, limit, slope):
    order = jax.random.permutation(stream_key, number_of)
    packed, common = portions_of(number_of, rows * top, limit, slope, True), portions_of(number_of, rows * top, limit, slope, False)
    places = jnp.arange(number_of)

    def named(lengths, offset_by):
        used = int((lengths > 0).sum())
        fixed = max(1, used // 4)
        passed = fixed + (places - fixed + offset_by * (used - fixed)) % max(1, number_of - fixed)
        return jnp.zeros((number_of,), jnp.int32).at[order[jnp.where(places < fixed, places, passed)]].set(jnp.asarray(lengths, jnp.int32))

    lengths = jnp.where(number % 4 == 0, named(packed, number // 4), named(common, number - number // 4 - 1))
    mixed = jax.random.permutation(jax.random.fold_in(own, 3), number_of)
    source_of, taker = mixed[0:number_of // 2 * 2:2], mixed[1:number_of // 2 * 2:2]
    margin = jnp.minimum(lengths[source_of] - 1, limit - lengths[taker]) // 2
    margin = jnp.where((source_of == order[0]) | (taker == order[0]) | (lengths[taker] == 0), 0, jnp.maximum(margin, 0))
    passed = jax.random.randint(jax.random.fold_in(own, 4), (number_of // 2,), 0, 1 << 20) % (margin + 1)
    lengths = lengths.at[source_of].add(-passed).at[taker].add(passed)
    labels = jnp.searchsorted(jnp.cumsum(lengths), jnp.arange(rows * top), side="right").astype(jnp.int32)
    listing = labels.reshape(top, rows).T
    listing = listing[jax.random.permutation(jax.random.fold_in(own, 1), rows)]
    offset_by = jax.random.randint(jax.random.fold_in(own, 2), (rows, 1), 0, top)
    return jnp.take_along_axis(listing, (jnp.arange(top)[None, :] + offset_by) % top, axis=1)


def portions_of(count, total, reach, skew, full):
    loads = [(1 << 20) // math.isqrt(grade ** skew) + 1 for grade in range(1, count + 1)]
    largest = reach if full else min(reach, max(-(-total // count), total * loads[0] // sum(loads)))
    least = 1 if total - largest >= count - 1 else 0
    given, surplus = [largest] + [least] * (count - 1), total - largest - least * (count - 1)
    while surplus > 0:
        free = [i for i in range(1, count) if given[i] < largest] or [i for i in range(1, count) if given[i] < reach]
        whole, budget = sum([loads[i] for i in free]), surplus
        for i in free:
            extra = min(reach - given[i], max(1, budget * loads[i] // whole), surplus)
            given[i] = given[i] + extra
            surplus = surplus - extra
    return np.array(given)


def normal_values(stream_key, dims, spread, most, cuts=(), kind=jnp.bfloat16):
    gain = block_scale(stream_key, dims, cuts, -0.22, 0.18) if cuts else 1.0
    array = jax.random.normal(stream_key, dims, jnp.float32) * spread * gain
    return jnp.minimum(jnp.maximum(array, -most), most).astype(kind)


def setup_inputs(seed: int = 0) -> dict:
    splits = jax.random.split(jax.random.key(seed), 7)
    obs_rows = normal_values(splits[0], (OBS, ROW), 1.0, 6.0, ((0, 128),), jnp.float32)
    obs_tile_keys = jax.random.split(jax.random.fold_in(splits[1], 1), OBS // OBS_DEV)
    obs_tile_turns = jax.random.permutation(jax.random.fold_in(splits[1], 3), OBS // OBS_DEV)
    obs_tile = jax.vmap(lambda own, number: routed_block(jax.random.fold_in(splits[1], 2), own, number, OBS_DEV, DEVICES, 1, CAP, 2))(obs_tile_keys, obs_tile_turns).reshape((OBS, 1))
    obs_cell = touch_ends(jax.random.randint(splits[2], (OBS,), 0, LAT_DEV * LON_DEV), jax.random.fold_in(splits[2], 1), 0, (LAT_DEV * LON_DEV) - 1).astype(jnp.int32)
    land_sea = touch_ends((jax.random.randint(splits[3], (LEV, NLAT, NLON), 0, 10) < 7).astype(jnp.int32), jax.random.fold_in(splits[3], 1), 0, 1)
    zonal_rate = jnp.clip(jnp.exp(math.log(0.24) - 2.0794415 * jax.random.uniform(splits[4], (LEV, NLAT, NLON), jnp.float32) ** block_scale(splits[4], (LEV, NLAT, NLON), ((1, 8), (2, 16)), -0.2, 0.2)), 0.03, 0.24)
    meridional_rate = jnp.clip(jnp.exp(math.log(0.24) - 2.0794415 * jax.random.uniform(splits[5], (LEV, NLAT, NLON), jnp.float32) ** block_scale(splits[5], (LEV, NLAT, NLON), ((1, 8), (2, 16)), -0.2, 0.2)), 0.03, 0.24)
    return dict(obs_rows=obs_rows, obs_tile=obs_tile, obs_cell=obs_cell, land_sea=land_sea, zonal_rate=zonal_rate, meridional_rate=meridional_rate)


def reference(obs_rows, obs_tile, obs_cell, land_sea, zonal_rate, meridional_rate):
    target = obs_tile[:, 0]
    row_global = (target % N_GY) * LAT_DEV + obs_cell // LON_DEV
    col_global = (target // N_GY) * LON_DEV + obs_cell % LON_DEV
    columns = jnp.zeros((NLAT * NLON, ROW), jnp.float32).at[row_global * NLON + col_global].add(obs_rows)
    ocean = land_sea.astype(jnp.float32)
    state = columns.T.reshape(VAR, LEV, NLAT, NLON) * ocean
    east_face = zonal_rate * ocean * jnp.roll(ocean, -1, 2)
    open_rows = (jnp.arange(NLAT) != NLAT - 1).astype(jnp.float32)
    north_face = meridional_rate * ocean * jnp.roll(ocean, -1, 1) * open_rows[:, None]
    for _step in range(ITERS):
        flux_east = east_face * (jnp.roll(state, -1, 3) - state)
        flux_north = north_face * (jnp.roll(state, -1, 2) - state)
        state = state + flux_east - jnp.roll(flux_east, 1, 3) + flux_north - jnp.roll(flux_north, 1, 2)
    return state
```

```python
import functools

import jax
import jax.numpy as jnp
from jax import lax
from jax.experimental import pallas as pl
from jax.experimental.pallas import tpu as pltpu
from jax.sharding import PartitionSpec as P

ITERS = 4
LANES = 128
SUB = 8
ACCS = 4
VMEM = pl.BlockSpec(memory_space=pltpu.VMEM)


def ring(axis, step):
    count = lax.axis_size(axis)
    return [(i, (i + step) % count) for i in range(count)]


def from_both(low_edge, high_edge, axis):
    return (
        lax.ppermute(high_edge, axis, ring(axis, 1)),
        lax.ppermute(low_edge, axis, ring(axis, -1)),
    )


def rates_kernel(land_ref, zonal_ref, merid_ref, out_ref):
    lat_cells, lon_cells = land_ref.shape[1:]
    for lat in range(lat_cells):
        ocean = land_ref[:, lat, :].astype(jnp.float32)
        both = jnp.concatenate(
            [zonal_ref[:, lat, :] * ocean, merid_ref[:, lat, :] * ocean], axis=0
        )
        out_ref[pl.ds(lat * lon_cells, lon_cells), :] = both.T


def pack_kernel(cap, cells, tile_ref, cell_ref, rows_ref, out_ref, slot_vmem, slot_smem, sem):
    groups = tile_ref.shape[0]
    tiles = out_ref.shape[0] // (cap + 1)
    f32, bf16 = jnp.float32, jnp.bfloat16
    down = lax.broadcasted_iota(jnp.int32, (tiles, LANES), 0)
    row_of = lax.broadcasted_iota(jnp.int32, (LANES, LANES), 0)
    col_of = lax.broadcasted_iota(jnp.int32, (LANES, LANES), 1)
    earlier = (row_of < col_of).astype(bf16)
    place = row_of % cap
    taken = jnp.zeros((tiles, 1), f32)
    high = jnp.zeros((tiles, LANES), f32)
    low = jnp.zeros((tiles, LANES), f32)
    across = (((1,), (1,)), ((), ()))
    for g in range(groups):
        tile = tile_ref[pl.ds(g, 1), :]
        code = cell_ref[pl.ds(g, 1), :] + 1
        hit = (down == tile).astype(f32)
        hit16 = hit.astype(bf16)
        before = jnp.dot(hit16, earlier, preferred_element_type=f32) + taken
        pos = jnp.sum(hit * before, axis=0, keepdims=True).astype(jnp.int32)
        taken = taken + jnp.sum(hit, axis=1, keepdims=True)
        slot_vmem[pl.ds(g, 1), :] = tile * (cap + 1) + pos
        here = place == pos
        top = jnp.where(here, (code >> 6).astype(f32), 0.0).astype(bf16)
        rest = jnp.where(here, (code & 63).astype(f32), 0.0).astype(bf16)
        high += lax.dot_general(hit16, top, across, preferred_element_type=f32)
        low += lax.dot_general(hit16, rest, across, preferred_element_type=f32)
    copy = pltpu.make_async_copy(slot_vmem, slot_smem, sem)
    copy.start()
    code = high * 64.0 + low
    out_ref[pl.ds(cap, tiles, stride=cap + 1), :] = jnp.where(
        code == 0.0, jnp.float32(cells), code - 1.0
    )
    copy.wait()

    @pl.loop(0, groups)
    def _(g):
        base = pl.multiple_of(g * LANES, LANES)
        for u in range(LANES):
            out_ref[pl.ds(slot_smem[g, u], 1), :] = rows_ref[pl.ds(base + u, 1), :]


def land_kernel(cap, got_ref, rates_ref, out_ref, cell_vmem, cell_smem, sem, *accs):
    block = cap + 1
    sources = got_ref.shape[0] // block
    per = LANES // cap
    lane = lax.broadcasted_iota(jnp.int32, (sources // per, LANES), 1)
    found = jnp.zeros((sources // per, LANES), jnp.float32)
    for j in range(per):
        part = got_ref[pl.ds(block * j + cap, sources // per, stride=block * per), :]
        found = jnp.where(lane // cap == j, part, found)
    cell_vmem[...] = found.astype(jnp.int32)
    copy = pltpu.make_async_copy(cell_vmem, cell_smem, sem)
    copy.start()
    for acc in accs:
        acc[...] = jnp.zeros_like(acc)
    copy.wait()

    @pl.loop(0, sources // per)
    def _(m):
        base = m * (block * per)
        for j in range(per):
            for p in range(cap):
                acc = accs[p % len(accs)]
                at = pl.ds(cell_smem[m, j * cap + p], 1)
                acc[at, :] += got_ref[pl.ds(base + j * block + p, 1), :]

    step = 64

    @pl.loop(0, out_ref.shape[0] // step)
    def _(i):
        at = pl.ds(pl.multiple_of(i * step, step), step)
        total = accs[0][at, :]
        for acc in accs[1:]:
            total += acc[at, :]
        out_ref[at, :] = jnp.where(rates_ref[at, :] > 0.0, total, 0.0)


def diffuse_kernel(
    lat_cells, lon_cells, total_rows, first_ref,
    state_ref, s_low, s_high, s_west, s_east,
    rates_ref, r_low, r_high, r_west, r_east,
    out_ref, even, odd, east_face, north_face,
):
    rim = ITERS
    rows = lat_cells + 2 * rim
    width = lon_cells + 2 * SUB

    def widen(dest, main, low, high, west, east):
        for r in range(rows):
            if r < rim:
                line = low[pl.ds(r * lon_cells, lon_cells), :]
            elif r < rim + lat_cells:
                line = main[pl.ds((r - rim) * lon_cells, lon_cells), :]
            else:
                line = high[pl.ds((r - rim - lat_cells) * lon_cells, lon_cells), :]
            dest[r, pl.ds(SUB, lon_cells), :] = line
            dest[r, pl.ds(SUB - rim, rim), :] = west[pl.ds(r * rim, rim), :]
            dest[r, pl.ds(SUB + lon_cells, rim), :] = east[pl.ds(r * rim, rim), :]

    widen(even, state_ref, s_low, s_high, s_west, s_east)
    widen(odd, rates_ref, r_low, r_high, r_west, r_east)
    half = LANES // 2
    zonal_lane = lax.broadcasted_iota(jnp.int32, (width, LANES), 1) < half

    @pl.loop(0, rows - 1)
    def _(r):
        here = odd[r]
        ocean_east = pltpu.roll(here, width - 1, 0) > 0.0
        ocean_north = odd[r + 1] > 0.0
        swapped = pltpu.roll(here, half, 1)
        row = lax.rem(first_ref[0] + r - rim + total_rows, total_rows)
        east_face[r] = jnp.where(ocean_east, jnp.where(zonal_lane, here, swapped), 0.0)
        north_face[r] = jnp.where(
            ocean_north & (row != total_rows - 1), jnp.where(zonal_lane, swapped, here), 0.0
        )

    for step in range(ITERS):
        old, new = (even, odd) if step % 2 == 0 else (odd, even)

        def line(r, south):
            s = old[r]
            flux_east = east_face[r] * (pltpu.roll(s, width - 1, 0) - s)
            flux_north = north_face[r] * (old[r + 1] - s)
            s = s + flux_east - pltpu.roll(flux_east, 1, 0) + flux_north - south
            if step < ITERS - 1:
                new[r] = s
            else:
                out_ref[:, r - rim, :] = s[SUB : SUB + lon_cells].T
            return flux_north

        south = north_face[step] * (old[step + 1] - old[step])
        if step < ITERS - 1:
            lax.fori_loop(step + 1, rows - 1 - step, line, south)
        else:
            for r in range(rim, rim + lat_cells):
                south = line(r, south)


def params(limit=48 << 20):
    return pltpu.CompilerParams(vmem_limit_bytes=limit)


def on_device(obs_rows, obs_tile, obs_cell, land_sea, zonal_rate, meridional_rate):
    count_x = lax.axis_size("gx")
    count_y = lax.axis_size("gy")
    devices = count_x * count_y
    owned, row_width = obs_rows.shape
    cap = 2 * owned // devices
    levels, lat_cells, lon_cells = land_sea.shape
    cells = lat_cells * lon_cells
    variables = row_width // levels
    rim = ITERS
    f32, i32 = jnp.float32, jnp.int32
    groups = owned // LANES
    sent = devices * (cap + 1)

    rates = pl.pallas_call(
        rates_kernel,
        out_shape=jax.ShapeDtypeStruct((cells, LANES), f32),
        in_specs=[VMEM] * 3,
        out_specs=VMEM,
        compiler_params=params(),
        cost_estimate=pl.CostEstimate(flops=4 << 20, bytes_accessed=3 << 20, transcendentals=0),
    )(land_sea, zonal_rate, meridional_rate)

    packed = pl.pallas_call(
        functools.partial(pack_kernel, cap, cells),
        out_shape=jax.ShapeDtypeStruct((sent, LANES), f32),
        in_specs=[VMEM] * 3,
        out_specs=VMEM,
        scratch_shapes=[
            pltpu.VMEM((groups, LANES), i32),
            pltpu.SMEM((groups, LANES), i32),
            pltpu.SemaphoreType.DMA,
        ],
        compiler_params=params(),
    )(obs_tile.reshape(groups, LANES), obs_cell.reshape(groups, LANES), obs_rows)
    got = lax.all_to_all(
        packed.reshape(sent, 1, LANES), ("gx", "gy"), split_axis=0, concat_axis=0, tiled=True
    ).reshape(sent, LANES)

    state = pl.pallas_call(
        functools.partial(land_kernel, cap),
        out_shape=jax.ShapeDtypeStruct((cells, LANES), f32),
        in_specs=[VMEM] * 2,
        out_specs=VMEM,
        scratch_shapes=[
            pltpu.VMEM((devices * cap // LANES, LANES), i32),
            pltpu.SMEM((devices * cap // LANES, LANES), i32),
            pltpu.SemaphoreType.DMA,
        ]
        + [pltpu.VMEM((cells + SUB, LANES), f32)] * ACCS,
        compiler_params=params(),
    )(got, rates)

    def halos(block):
        edge = rim * lon_cells
        low, high = from_both(block[:edge], block[cells - edge :], "gy")
        tall = [
            t.reshape(-1, lon_cells, LANES) for t in (low, block, high)
        ]
        first = jnp.concatenate([t[:, :rim] for t in tall]).reshape(-1, LANES)
        last = jnp.concatenate([t[:, lon_cells - rim :] for t in tall]).reshape(-1, LANES)
        west, east = from_both(first, last, "gx")
        return block, low, high, west, east

    wide = (lat_cells + 2 * rim, lon_cells + 2 * SUB, LANES)
    out = pl.pallas_call(
        functools.partial(diffuse_kernel, lat_cells, lon_cells, lat_cells * count_y),
        out_shape=jax.ShapeDtypeStruct((row_width, lat_cells, lon_cells), f32),
        in_specs=[pl.BlockSpec(memory_space=pltpu.SMEM)] + [VMEM] * 10,
        out_specs=VMEM,
        scratch_shapes=[pltpu.VMEM(wide, f32)] * 4,
        compiler_params=params(),
    )((lax.axis_index("gy") * lat_cells).astype(i32).reshape(1), *halos(state), *halos(rates))
    return out.reshape(variables, levels, lat_cells, lon_cells)


def solution(mesh):
    placed = (
        P(("gx", "gy"), None),
        P(("gx", "gy"), None),
        P(("gx", "gy")),
        P(None, "gy", "gx"),
        P(None, "gy", "gx"),
        P(None, "gy", "gx"),
    )
    return jax.shard_map(
        on_device, mesh=mesh, in_specs=placed, out_specs=P(None, None, "gy", "gx"), check_vma=False
    )
```

```python
import functools

import jax
import jax.numpy as jnp
from jax import lax
from jax.experimental import pallas as pl
from jax.experimental.pallas import tpu as pltpu
from jax.sharding import PartitionSpec as P

ITERS = 4
LANES = 128
SUB = 8
ACCS = 4
VMEM = pl.BlockSpec(memory_space=pltpu.VMEM)
ANY = pl.BlockSpec(memory_space=pl.ANY)


def ring(axis, step):
    count = lax.axis_size(axis)
    return [(i, (i + step) % count) for i in range(count)]


def from_both(low_edge, high_edge, axis):
    return (
        lax.ppermute(high_edge, axis, ring(axis, 1)),
        lax.ppermute(low_edge, axis, ring(axis, -1)),
    )


def fetch(pairs, sems):
    copies = [pltpu.make_async_copy(a, b, sems.at[i]) for i, (a, b) in enumerate(pairs)]
    for copy in copies:
        copy.start()
    return copies


def rates_kernel(land_hbm, zonal_hbm, merid_hbm, out_ref, land_ref, zonal_ref, merid_ref, sems):
    lat_cells, lon_cells = land_ref.shape[1:]
    for copy in fetch(
        [(land_hbm, land_ref), (zonal_hbm, zonal_ref), (merid_hbm, merid_ref)], sems
    ):
        copy.wait()
    for lat in range(lat_cells):
        ocean = land_ref[:, lat, :].astype(jnp.float32)
        both = jnp.concatenate(
            [zonal_ref[:, lat, :] * ocean, merid_ref[:, lat, :] * ocean], axis=0
        )
        out_ref[pl.ds(lat * lon_cells, lon_cells), :] = both.T


def pack_kernel(
    cap, cells, tile_hbm, cell_hbm, rows_hbm, out_ref,
    tile_ref, cell_ref, rows_ref, slot_vmem, slot_smem, sem, sems,
):
    copies = fetch([(tile_hbm, tile_ref), (cell_hbm, cell_ref), (rows_hbm, rows_ref)], sems)
    copies[0].wait()
    copies[1].wait()
    groups = tile_ref.shape[0]
    tiles = out_ref.shape[0] // (cap + 1)
    f32, bf16 = jnp.float32, jnp.bfloat16
    down = lax.broadcasted_iota(jnp.int32, (tiles, LANES), 0)
    row_of = lax.broadcasted_iota(jnp.int32, (LANES, LANES), 0)
    col_of = lax.broadcasted_iota(jnp.int32, (LANES, LANES), 1)
    earlier = (row_of < col_of).astype(bf16)
    place = row_of % cap
    taken = jnp.zeros((tiles, 1), f32)
    high = jnp.zeros((tiles, LANES), f32)
    low = jnp.zeros((tiles, LANES), f32)
    across = (((1,), (1,)), ((), ()))
    for g in range(groups):
        tile = tile_ref[pl.ds(g, 1), :]
        code = cell_ref[pl.ds(g, 1), :] + 1
        hit = (down == tile).astype(f32)
        hit16 = hit.astype(bf16)
        before = jnp.dot(hit16, earlier, preferred_element_type=f32) + taken
        pos = jnp.sum(hit * before, axis=0, keepdims=True).astype(jnp.int32)
        taken = taken + jnp.sum(hit, axis=1, keepdims=True)
        slot_vmem[pl.ds(g, 1), :] = tile * (cap + 1) + pos
        here = place == pos
        top = jnp.where(here, (code >> 6).astype(f32), 0.0).astype(bf16)
        rest = jnp.where(here, (code & 63).astype(f32), 0.0).astype(bf16)
        high += lax.dot_general(hit16, top, across, preferred_element_type=f32)
        low += lax.dot_general(hit16, rest, across, preferred_element_type=f32)
    copy = pltpu.make_async_copy(slot_vmem, slot_smem, sem)
    copy.start()
    code = high * 64.0 + low
    out_ref[pl.ds(cap, tiles, stride=cap + 1), :] = jnp.where(
        code == 0.0, jnp.float32(cells), code - 1.0
    )
    copies[2].wait()
    copy.wait()

    @pl.loop(0, groups)
    def _(g):
        base = pl.multiple_of(g * LANES, LANES)
        for u in range(LANES):
            out_ref[pl.ds(slot_smem[g, u], 1), :] = rows_ref[pl.ds(base + u, 1), :]


def land_kernel(cap, got_ref, rates_ref, out_ref, cell_vmem, cell_smem, sem, *accs):
    block = cap + 1
    sources = got_ref.shape[0] // block
    per = LANES // cap
    lane = lax.broadcasted_iota(jnp.int32, (sources // per, LANES), 1)
    found = jnp.zeros((sources // per, LANES), jnp.float32)
    for j in range(per):
        part = got_ref[pl.ds(block * j + cap, sources // per, stride=block * per), :]
        found = jnp.where(lane // cap == j, part, found)
    cell_vmem[...] = found.astype(jnp.int32)
    copy = pltpu.make_async_copy(cell_vmem, cell_smem, sem)
    copy.start()
    for acc in accs:
        acc[...] = jnp.zeros_like(acc)
    copy.wait()

    @pl.loop(0, sources // per)
    def _(m):
        base = m * (block * per)
        for j in range(per):
            for p in range(cap):
                acc = accs[p % len(accs)]
                at = pl.ds(cell_smem[m, j * cap + p], 1)
                acc[at, :] += got_ref[pl.ds(base + j * block + p, 1), :]

    step = 64

    @pl.loop(0, out_ref.shape[0] // step)
    def _(i):
        at = pl.ds(pl.multiple_of(i * step, step), step)
        total = accs[0][at, :]
        for acc in accs[1:]:
            total += acc[at, :]
        out_ref[at, :] = jnp.where(rates_ref[at, :] > 0.0, total, 0.0)


def diffuse_kernel(
    lat_cells, lon_cells, total_rows, first_ref,
    state_ref, s_low, s_high, s_west, s_east,
    rates_ref, r_low, r_high, r_west, r_east,
    out_ref, even, odd, east_face, north_face,
):
    rim = ITERS
    rows = lat_cells + 2 * rim
    width = lon_cells + 2 * SUB

    def widen(dest, main, low, high, west, east):
        for r in range(rows):
            if r < rim:
                line = low[pl.ds(r * lon_cells, lon_cells), :]
            elif r < rim + lat_cells:
                line = main[pl.ds((r - rim) * lon_cells, lon_cells), :]
            else:
                line = high[pl.ds((r - rim - lat_cells) * lon_cells, lon_cells), :]
            dest[r, pl.ds(SUB, lon_cells), :] = line
            dest[r, pl.ds(SUB - rim, rim), :] = west[pl.ds(r * rim, rim), :]
            dest[r, pl.ds(SUB + lon_cells, rim), :] = east[pl.ds(r * rim, rim), :]

    widen(even, state_ref, s_low, s_high, s_west, s_east)
    widen(odd, rates_ref, r_low, r_high, r_west, r_east)
    half = LANES // 2
    zonal_lane = lax.broadcasted_iota(jnp.int32, (width, LANES), 1) < half

    @pl.loop(0, rows - 1)
    def _(r):
        here = odd[r]
        ocean_east = pltpu.roll(here, width - 1, 0) > 0.0
        ocean_north = odd[r + 1] > 0.0
        swapped = pltpu.roll(here, half, 1)
        row = lax.rem(first_ref[0] + r - rim + total_rows, total_rows)
        east_face[r] = jnp.where(ocean_east, jnp.where(zonal_lane, here, swapped), 0.0)
        north_face[r] = jnp.where(
            ocean_north & (row != total_rows - 1), jnp.where(zonal_lane, swapped, here), 0.0
        )

    for step in range(ITERS):
        old, new = (even, odd) if step % 2 == 0 else (odd, even)

        def line(r, south):
            s = old[r]
            flux_east = east_face[r] * (pltpu.roll(s, width - 1, 0) - s)
            flux_north = north_face[r] * (old[r + 1] - s)
            s = s + flux_east - pltpu.roll(flux_east, 1, 0) + flux_north - south
            if step < ITERS - 1:
                new[r] = s
            else:
                out_ref[:, r - rim, :] = s[SUB : SUB + lon_cells].T
            return flux_north

        south = north_face[step] * (old[step + 1] - old[step])
        if step < ITERS - 1:
            lax.fori_loop(step + 1, rows - 1 - step, line, south)
        else:
            for r in range(rim, rim + lat_cells):
                south = line(r, south)


def params(limit):
    return pltpu.CompilerParams(vmem_limit_bytes=limit)


def on_device(obs_rows, obs_tile, obs_cell, land_sea, zonal_rate, meridional_rate):
    count_x = lax.axis_size("gx")
    count_y = lax.axis_size("gy")
    devices = count_x * count_y
    owned, row_width = obs_rows.shape
    cap = 2 * owned // devices
    levels, lat_cells, lon_cells = land_sea.shape
    cells = lat_cells * lon_cells
    variables = row_width // levels
    rim = ITERS
    f32, i32 = jnp.float32, jnp.int32
    groups = owned // LANES
    sent = devices * (cap + 1)

    rates = pl.pallas_call(
        rates_kernel,
        out_shape=jax.ShapeDtypeStruct((cells, LANES), f32),
        in_specs=[ANY] * 3,
        out_specs=VMEM,
        scratch_shapes=[
            pltpu.VMEM(land_sea.shape, i32),
            pltpu.VMEM(land_sea.shape, f32),
            pltpu.VMEM(land_sea.shape, f32),
            pltpu.SemaphoreType.DMA((3,)),
        ],
        compiler_params=params(4 << 20),
    )(land_sea, zonal_rate, meridional_rate)
    edge = rim * lon_cells

    def lat_halo(block):
        return from_both(block[:edge], block[cells - edge :], "gy")

    def lon_halo(block, low, high):
        tall = [t.reshape(-1, lon_cells, LANES) for t in (low, block, high)]
        first = jnp.concatenate([t[:, :rim] for t in tall]).reshape(-1, LANES)
        last = jnp.concatenate([t[:, lon_cells - rim :] for t in tall]).reshape(-1, LANES)
        return from_both(first, last, "gx")

    rates, obs_tile = lax.optimization_barrier((rates, obs_tile))
    rates_lat = lat_halo(rates)
    packed = pl.pallas_call(
        functools.partial(pack_kernel, cap, cells),
        out_shape=jax.ShapeDtypeStruct((sent, LANES), f32),
        in_specs=[ANY] * 3,
        out_specs=VMEM,
        scratch_shapes=[
            pltpu.VMEM((groups, LANES), i32),
            pltpu.VMEM((groups, LANES), i32),
            pltpu.VMEM((owned, LANES), f32),
            pltpu.VMEM((groups, LANES), i32),
            pltpu.SMEM((groups, LANES), i32),
            pltpu.SemaphoreType.DMA,
            pltpu.SemaphoreType.DMA((3,)),
        ],
        compiler_params=params(8 << 20),
    )(obs_tile.reshape(groups, LANES), obs_cell.reshape(groups, LANES), obs_rows)
    packed, rates_lat = lax.optimization_barrier((packed, rates_lat))
    rates_lon = lon_halo(rates, *rates_lat)
    got = lax.all_to_all(
        packed.reshape(sent, 1, LANES), ("gx", "gy"), split_axis=0, concat_axis=0, tiled=True
    ).reshape(sent, LANES)

    state = pl.pallas_call(
        functools.partial(land_kernel, cap),
        out_shape=jax.ShapeDtypeStruct((cells, LANES), f32),
        in_specs=[VMEM] * 2,
        out_specs=VMEM,
        scratch_shapes=[
            pltpu.VMEM((devices * cap // LANES, LANES), i32),
            pltpu.SMEM((devices * cap // LANES, LANES), i32),
            pltpu.SemaphoreType.DMA,
        ]
        + [pltpu.VMEM((cells + SUB, LANES), f32)] * ACCS,
        compiler_params=params(8 << 20),
    )(got, rates)

    state_lat = lat_halo(state)
    state_lon = lon_halo(state, *state_lat)
    wide = (lat_cells + 2 * rim, lon_cells + 2 * SUB, LANES)
    out = pl.pallas_call(
        functools.partial(diffuse_kernel, lat_cells, lon_cells, lat_cells * count_y),
        out_shape=jax.ShapeDtypeStruct((row_width, lat_cells, lon_cells), f32),
        in_specs=[pl.BlockSpec(memory_space=pltpu.SMEM)] + [VMEM] * 10,
        out_specs=VMEM,
        scratch_shapes=[pltpu.VMEM(wide, f32)] * 4,
        compiler_params=params(12 << 20),
    )((lax.axis_index("gy") * lat_cells).astype(i32).reshape(1), state, *state_lat, *state_lon, rates, *rates_lat, *rates_lon)
    return out.reshape(variables, levels, lat_cells, lon_cells)


def solution(mesh):
    placed = (
        P(("gx", "gy"), None),
        P(("gx", "gy"), None),
        P(("gx", "gy")),
        P(None, "gy", "gx"),
        P(None, "gy", "gx"),
        P(None, "gy", "gx"),
    )
    return jax.shard_map(
        on_device, mesh=mesh, in_specs=placed, out_specs=P(None, None, "gy", "gx"), check_vma=False
    )
```

```python
import functools

import jax
import jax.numpy as jnp
from jax import lax
from jax.experimental import pallas as pl
from jax.experimental.pallas import tpu as pltpu
from jax.sharding import PartitionSpec as P

ITERS = 4
LANES = 128
SUB = 8
ACCS = 4
OUT_PARTS = 8
VMEM = pl.BlockSpec(memory_space=pltpu.VMEM)
HBM = pl.BlockSpec(memory_space=pltpu.HBM)


def ring(axis, step):
    count = lax.axis_size(axis)
    return [(i, (i + step) % count) for i in range(count)]


def from_both(low_edge, high_edge, axis):
    return (
        lax.ppermute(high_edge, axis, ring(axis, 1)),
        lax.ppermute(low_edge, axis, ring(axis, -1)),
    )


def fetch(pairs, sems):
    copies = [pltpu.make_async_copy(a, b, sems.at[i]) for i, (a, b) in enumerate(pairs)]
    for copy in copies:
        copy.start()
    return copies


def rates_kernel(land_hbm, zonal_hbm, merid_hbm, out_ref, land_ref, zonal_ref, merid_ref, sems):
    lat_cells, lon_cells = land_ref.shape[1:]
    for copy in fetch(
        [(land_hbm, land_ref), (zonal_hbm, zonal_ref), (merid_hbm, merid_ref)], sems
    ):
        copy.wait()
    for lat in range(lat_cells):
        ocean = land_ref[:, lat, :].astype(jnp.float32)
        both = jnp.concatenate(
            [zonal_ref[:, lat, :] * ocean, merid_ref[:, lat, :] * ocean], axis=0
        )
        out_ref[pl.ds(lat * lon_cells, lon_cells), :] = both.T


def pack_kernel(
    cap, cells, tile_hbm, cell_hbm, rows_hbm, out_hbm,
    tile_ref, cell_ref, rows_ref, out_ref, slot_vmem, slot_smem, sem, sems, out_sems,
):
    copies = fetch([(tile_hbm, tile_ref), (cell_hbm, cell_ref), (rows_hbm, rows_ref)], sems)
    copies[0].wait()
    copies[1].wait()
    groups = tile_ref.shape[0]
    tiles = out_ref.shape[0] // (cap + 1)
    f32, bf16 = jnp.float32, jnp.bfloat16
    down = lax.broadcasted_iota(jnp.int32, (tiles, LANES), 0)
    row_of = lax.broadcasted_iota(jnp.int32, (LANES, LANES), 0)
    col_of = lax.broadcasted_iota(jnp.int32, (LANES, LANES), 1)
    earlier = (row_of < col_of).astype(bf16)
    place = row_of % cap
    taken = jnp.zeros((tiles, 1), f32)
    high = jnp.zeros((tiles, LANES), f32)
    low = jnp.zeros((tiles, LANES), f32)
    across = (((1,), (1,)), ((), ()))
    for g in range(groups):
        tile = tile_ref[pl.ds(g, 1), :]
        code = cell_ref[pl.ds(g, 1), :] + 1
        hit = (down == tile).astype(f32)
        hit16 = hit.astype(bf16)
        before = jnp.dot(hit16, earlier, preferred_element_type=f32) + taken
        pos = jnp.sum(hit * before, axis=0, keepdims=True).astype(jnp.int32)
        taken = taken + jnp.sum(hit, axis=1, keepdims=True)
        slot_vmem[pl.ds(g, 1), :] = tile * (cap + 1) + pos
        here = place == pos
        top = jnp.where(here, (code >> 6).astype(f32), 0.0).astype(bf16)
        rest = jnp.where(here, (code & 63).astype(f32), 0.0).astype(bf16)
        high += lax.dot_general(hit16, top, across, preferred_element_type=f32)
        low += lax.dot_general(hit16, rest, across, preferred_element_type=f32)
    copy = pltpu.make_async_copy(slot_vmem, slot_smem, sem)
    copy.start()
    code = high * 64.0 + low
    out_ref[pl.ds(cap, tiles, stride=cap + 1), :] = jnp.where(
        code == 0.0, jnp.float32(cells), code - 1.0
    )
    copies[2].wait()
    copy.wait()

    @pl.loop(0, groups)
    def _(g):
        base = pl.multiple_of(g * LANES, LANES)
        for u in range(LANES):
            out_ref[pl.ds(slot_smem[g, u], 1), :] = rows_ref[pl.ds(base + u, 1), :]

    part = out_ref.shape[0] // OUT_PARTS
    spans = [pl.ds(i * part, part) for i in range(OUT_PARTS)]
    for copy in fetch([(out_ref.at[at], out_hbm.at[at]) for at in spans], out_sems):
        copy.wait()


def arrived_kernel(
    cap, edge, corner, got_ref, rates_ref, west_ref, east_ref, cell_ref, first_ref, last_ref
):
    block = cap + 1
    sources = got_ref.shape[0] // block
    per = LANES // cap
    lane = lax.broadcasted_iota(jnp.int32, (sources // per, LANES), 1)
    found = jnp.zeros((sources // per, LANES), jnp.float32)
    for j in range(per):
        part = got_ref[pl.ds(block * j + cap, sources // per, stride=block * per), :]
        found = jnp.where(lane // cap == j, part, found)
    cell_ref[...] = found.astype(jnp.int32)
    first_ref[pl.ds(0, edge), :] = rates_ref[pl.ds(0, edge), :]
    last_ref[pl.ds(0, edge), :] = rates_ref[pl.ds(rates_ref.shape[0] - edge, edge), :]
    for i, ref in enumerate((west_ref, east_ref)):
        at = pl.ds(edge + i * corner, corner)
        first_ref[at, :] = ref[pl.ds(0, corner), :]
        last_ref[at, :] = ref[pl.ds(ref.shape[0] - corner, corner), :]


def land_kernel(cap, got_ref, cell_ref, rates_ref, out_ref, cell_smem, sem, *accs):
    block = cap + 1
    sources = got_ref.shape[0] // block
    per = LANES // cap
    copy = pltpu.make_async_copy(cell_ref, cell_smem, sem)
    copy.start()
    for acc in accs:
        acc[...] = jnp.zeros_like(acc)
    copy.wait()

    @pl.loop(0, sources // per)
    def _(m):
        base = m * (block * per)
        for j in range(per):
            for p in range(cap):
                acc = accs[p % len(accs)]
                at = pl.ds(cell_smem[m, j * cap + p], 1)
                acc[at, :] += got_ref[pl.ds(base + j * block + p, 1), :]

    step = 64

    @pl.loop(0, out_ref.shape[0] // step)
    def _(i):
        at = pl.ds(pl.multiple_of(i * step, step), step)
        total = accs[0][at, :]
        for acc in accs[1:]:
            total += acc[at, :]
        out_ref[at, :] = jnp.where(rates_ref[at, :] > 0.0, total, 0.0)


def faces_kernel(
    lat_cells, lon_cells, total_rows, first_ref,
    rates_ref, low_ref, high_ref, west_ref, east_ref, east_face, north_face, wide,
):
    rim = ITERS
    rows = lat_cells + 2 * rim
    width = lon_cells + 2 * SUB
    for r in range(rows):
        if rim <= r < rim + lat_cells:
            at = r - rim
            line, corner = rates_ref, (west_ref, east_ref)
            corner_at = (at * rim, at * rim)
        else:
            line, at = (low_ref, r) if r < rim else (high_ref, r - rim - lat_cells)
            corner = (line, line)
            corner_at = (rim * (lon_cells + at), rim * (lon_cells + rim + at))
        wide[r, pl.ds(SUB, lon_cells), :] = line[pl.ds(at * lon_cells, lon_cells), :]
        wide[r, pl.ds(SUB - rim, rim), :] = corner[0][pl.ds(corner_at[0], rim), :]
        wide[r, pl.ds(SUB + lon_cells, rim), :] = corner[1][pl.ds(corner_at[1], rim), :]
    half = LANES // 2
    zonal_lane = lax.broadcasted_iota(jnp.int32, (width, LANES), 1) < half

    @pl.loop(0, rows - 1)
    def _(r):
        here = wide[r]
        ocean_east = pltpu.roll(here, width - 1, 0) > 0.0
        ocean_north = wide[r + 1] > 0.0
        swapped = pltpu.roll(here, half, 1)
        row = lax.rem(first_ref[0] + r - rim + total_rows, total_rows)
        east_face[r] = jnp.where(ocean_east, jnp.where(zonal_lane, here, swapped), 0.0)
        north_face[r] = jnp.where(
            ocean_north & (row != total_rows - 1), jnp.where(zonal_lane, swapped, here), 0.0
        )


def next_line(r, south, old, east, north, width):
    s = old[r]
    flux_east = east(r) * (pltpu.roll(s, width - 1, 0) - s)
    flux_north = north(r) * (old[r + 1] - s)
    return s + flux_east - pltpu.roll(flux_east, 1, 0) + flux_north - south, flux_north


def bulk_kernel(
    lat_cells, lon_cells, state_ref, low_ref, high_ref, east_face, north_face, out_ref, even, odd
):
    rim = ITERS
    rows = lat_cells + 2 * rim
    own = pl.ds(SUB, lon_cells)

    def east(r):
        return east_face[r, own, :]

    def north(r):
        return north_face[r, own, :]

    for r in range(rim):
        even[r] = low_ref[pl.ds(r * lon_cells, lon_cells), :]
        even[rim + lat_cells + r] = high_ref[pl.ds(r * lon_cells, lon_cells), :]

    @pl.loop(0, lat_cells)
    def _(r):
        even[rim + r] = state_ref[pl.ds(pl.multiple_of(r * lon_cells, lon_cells), lon_cells), :]

    for step in range(ITERS):
        old, new = (even, odd) if step % 2 == 0 else (odd, even)

        def line(r, south):
            s, south = next_line(r, south, old, east, north, lon_cells)
            if step < ITERS - 1:
                new[r] = s
            else:
                at = pl.multiple_of((r - rim) * lon_cells, lon_cells)
                out_ref[pl.ds(at, lon_cells), :] = s
            return south

        south = north(step) * (old[step + 1] - old[step])
        lax.fori_loop(step + 1, rows - 1 - step, line, south)


def finish_kernel(
    lat_cells, lon_cells, bulk_ref, state_ref, low_ref, high_ref, west_ref, east_ref,
    east_face, north_face, out_hbm, even, odd, out_ref, sems,
):
    rim = ITERS
    rows = lat_cells + 2 * rim
    span = 2 * SUB
    width = 2 * span
    windows = (pl.ds(0, span), pl.ds(lon_cells, span))

    def east(r):
        return jnp.concatenate([east_face[r, w, :] for w in windows], axis=0)

    def north(r):
        return jnp.concatenate([north_face[r, w, :] for w in windows], axis=0)

    for r in range(rows):
        if r < rim:
            line, at = low_ref, r
        elif r < rim + lat_cells:
            line, at = state_ref, r - rim
        else:
            line, at = high_ref, r - rim - lat_cells
        even[r, pl.ds(SUB - rim, rim), :] = west_ref[pl.ds(r * rim, rim), :]
        even[r, pl.ds(SUB, SUB), :] = line[pl.ds(at * lon_cells, SUB), :]
        even[r, pl.ds(span, SUB), :] = line[pl.ds((at + 1) * lon_cells - SUB, SUB), :]
        even[r, pl.ds(span + SUB, rim), :] = east_ref[pl.ds(r * rim, rim), :]

    copies = []
    for step in range(ITERS):
        old, new = (even, odd) if step % 2 == 0 else (odd, even)
        south = north(step) * (old[step + 1] - old[step])
        for r in range(step + 1, rows - 1 - step):
            s, south = next_line(r, south, old, east, north, width)
            if step < ITERS - 1:
                new[r] = s
                continue
            at = (r - rim) * lon_cells
            column = jnp.concatenate(
                [
                    s[SUB : SUB + rim],
                    bulk_ref[pl.ds(at + rim, lon_cells - 2 * rim), :],
                    s[span + SUB - rim : span + SUB],
                ],
                axis=0,
            )
            out_ref[:, r - rim, :] = column.T
            done = r - rim + 1
            if done % SUB == 0:
                ready = pl.ds(done - SUB, SUB)
                copies += fetch(
                    [(out_ref.at[:, ready, :], out_hbm.at[:, ready, :])],
                    sems.at[pl.ds(done // SUB - 1, 1)],
                )
    for copy in copies:
        copy.wait()


def cost(microseconds):
    return pl.CostEstimate(
        flops=0, bytes_accessed=microseconds * 3_000_000, transcendentals=0
    )


def params(limit):
    return pltpu.CompilerParams(vmem_limit_bytes=limit)


def on_device(obs_rows, obs_tile, obs_cell, land_sea, zonal_rate, meridional_rate):
    count_x = lax.axis_size("gx")
    count_y = lax.axis_size("gy")
    devices = count_x * count_y
    owned, row_width = obs_rows.shape
    cap = 2 * owned // devices
    levels, lat_cells, lon_cells = land_sea.shape
    cells = lat_cells * lon_cells
    variables = row_width // levels
    rim = ITERS
    f32, i32 = jnp.float32, jnp.int32
    groups = owned // LANES
    sent = devices * (cap + 1)

    packed = pl.pallas_call(
        functools.partial(pack_kernel, cap, cells),
        out_shape=jax.ShapeDtypeStruct((sent, LANES), f32),
        in_specs=[HBM] * 3,
        out_specs=HBM,
        scratch_shapes=[
            pltpu.VMEM((groups, LANES), i32),
            pltpu.VMEM((groups, LANES), i32),
            pltpu.VMEM((owned, LANES), f32),
            pltpu.VMEM((sent, LANES), f32),
            pltpu.VMEM((groups, LANES), i32),
            pltpu.SMEM((groups, LANES), i32),
            pltpu.SemaphoreType.DMA,
            pltpu.SemaphoreType.DMA((3,)),
            pltpu.SemaphoreType.DMA((OUT_PARTS,)),
        ],
        compiler_params=params(63 << 20),
    )(obs_tile.reshape(groups, LANES), obs_cell.reshape(groups, LANES), obs_rows)
    got = lax.all_to_all(
        packed.reshape(sent, 1, LANES), ("gx", "gy"), split_axis=0, concat_axis=0, tiled=True
    ).reshape(sent, LANES)

    rates = pl.pallas_call(
        rates_kernel,
        out_shape=jax.ShapeDtypeStruct((cells, LANES), f32),
        in_specs=[HBM] * 3,
        out_specs=VMEM,
        scratch_shapes=[
            pltpu.VMEM(land_sea.shape, i32),
            pltpu.VMEM(land_sea.shape, f32),
            pltpu.VMEM(land_sea.shape, f32),
            pltpu.SemaphoreType.DMA((3,)),
        ],
        compiler_params=params(4 << 20),
        cost_estimate=cost(2),
    )(land_sea, zonal_rate, meridional_rate)

    def column_ends(*blocks):
        tall = [t.reshape(-1, lon_cells, LANES) for t in blocks]
        first = jnp.concatenate([t[:, :rim] for t in tall]).reshape(-1, LANES)
        last = jnp.concatenate([t[:, lon_cells - rim :] for t in tall]).reshape(-1, LANES)
        return first, last

    edge = rim * lon_cells
    corner = rim * rim
    west, east = from_both(*column_ends(rates), "gx")
    cell, first, last = pl.pallas_call(
        functools.partial(arrived_kernel, cap, edge, corner),
        out_shape=[jax.ShapeDtypeStruct((devices * cap // LANES, LANES), i32)]
        + [jax.ShapeDtypeStruct((edge + 2 * corner, LANES), f32)] * 2,
        in_specs=[VMEM] * 4,
        out_specs=[VMEM] * 3,
        compiler_params=params(1 << 20),
    )(got, rates, west, east)
    low, high = from_both(first, last, "gy")

    state = pl.pallas_call(
        functools.partial(land_kernel, cap),
        out_shape=jax.ShapeDtypeStruct((cells, LANES), f32),
        in_specs=[VMEM] * 3,
        out_specs=VMEM,
        scratch_shapes=[
            pltpu.SMEM((devices * cap // LANES, LANES), i32),
            pltpu.SemaphoreType.DMA,
        ]
        + [pltpu.VMEM((cells + SUB, LANES), f32)] * ACCS,
        compiler_params=params(8 << 20),
        cost_estimate=cost(7),
    )(got, cell, rates)
    state, low, high = lax.optimization_barrier((state, low, high))

    rows = lat_cells + 2 * rim
    wide = (rows, lon_cells + 2 * SUB, LANES)
    first_row = (lax.axis_index("gy") * lat_cells).astype(i32).reshape(1)
    faces = pl.pallas_call(
        functools.partial(faces_kernel, lat_cells, lon_cells, lat_cells * count_y),
        out_shape=[jax.ShapeDtypeStruct(wide, f32)] * 2,
        in_specs=[pl.BlockSpec(memory_space=pltpu.SMEM)] + [VMEM] * 5,
        out_specs=[VMEM] * 2,
        scratch_shapes=[pltpu.VMEM(wide, f32)],
        compiler_params=params(4 << 20),
        cost_estimate=cost(2),
    )(first_row, rates, low, high, west, east)

    s_low, s_high = from_both(state[:edge], state[-edge:], "gy")
    s_west, s_east = from_both(*column_ends(s_low, state, s_high), "gx")
    narrow = (rows, lon_cells, LANES)
    bulk = pl.pallas_call(
        functools.partial(bulk_kernel, lat_cells, lon_cells),
        out_shape=jax.ShapeDtypeStruct((cells, LANES), f32),
        in_specs=[VMEM] * 5,
        out_specs=VMEM,
        scratch_shapes=[pltpu.VMEM(narrow, f32)] * 2,
        compiler_params=params(8 << 20),
        cost_estimate=cost(4),
    )(state, s_low, s_high, *faces)
    strips = (rows, 4 * SUB, LANES)
    out_shape = (row_width, lat_cells, lon_cells)
    out = pl.pallas_call(
        functools.partial(finish_kernel, lat_cells, lon_cells),
        out_shape=jax.ShapeDtypeStruct(out_shape, f32),
        in_specs=[VMEM] * 8,
        out_specs=HBM,
        scratch_shapes=[pltpu.VMEM(strips, f32)] * 2
        + [pltpu.VMEM(out_shape, f32), pltpu.SemaphoreType.DMA((lat_cells // SUB,))],
        compiler_params=params(4 << 20),
        cost_estimate=cost(3),
    )(bulk, state, s_low, s_high, s_west, s_east, *faces)
    return out.reshape(variables, levels, lat_cells, lon_cells)


def solution(mesh):
    placed = (
        P(("gx", "gy"), None),
        P(("gx", "gy"), None),
        P(("gx", "gy")),
        P(None, "gy", "gx"),
        P(None, "gy", "gx"),
        P(None, "gy", "gx"),
    )
    return jax.shard_map(
        on_device, mesh=mesh, in_specs=placed, out_specs=P(None, None, "gy", "gx"), check_vma=False
    )
```

```python
import functools

import jax
import jax.numpy as jnp
from jax import lax
from jax.experimental import pallas as pl
from jax.experimental.pallas import tpu as pltpu
from jax.sharding import PartitionSpec as P

ITERS = 4
LANES = 128
SUB = 8
ACCS = 4
OUT_PARTS = 8
VMEM = pl.BlockSpec(memory_space=pltpu.VMEM)
HBM = pl.BlockSpec(memory_space=pltpu.HBM)


def ring(axis, step):
    count = lax.axis_size(axis)
    return [(i, (i + step) % count) for i in range(count)]


def mates():
    return [(i, i + 1 - 2 * (i % 2)) for i in range(lax.axis_size("gy"))]


def nexts():
    count = lax.axis_size("gy")
    return [(i, (i - 1 + 2 * (i % 2)) % count) for i in range(count)]


def from_both(low_edge, high_edge, axis):
    return (
        lax.ppermute(high_edge, axis, ring(axis, 1)),
        lax.ppermute(low_edge, axis, ring(axis, -1)),
    )


def fetch(pairs, sems):
    copies = [pltpu.make_async_copy(a, b, sems.at[i]) for i, (a, b) in enumerate(pairs)]
    for copy in copies:
        copy.start()
    return copies


def rates_kernel(land_hbm, zonal_hbm, merid_hbm, out_ref, land_ref, zonal_ref, merid_ref, sems):
    lat_cells, lon_cells = land_ref.shape[1:]
    for copy in fetch(
        [(land_hbm, land_ref), (zonal_hbm, zonal_ref), (merid_hbm, merid_ref)], sems
    ):
        copy.wait()
    for lat in range(lat_cells):
        ocean = land_ref[:, lat, :].astype(jnp.float32)
        both = jnp.concatenate(
            [zonal_ref[:, lat, :] * ocean, merid_ref[:, lat, :] * ocean], axis=0
        )
        out_ref[pl.ds(lat * lon_cells, lon_cells), :] = both.T


def pack_kernel(
    cap, cells, tile_hbm, cell_hbm, rows_hbm, out_hbm,
    tile_ref, cell_ref, rows_ref, out_ref, slot_vmem, slot_smem, sem, sems, out_sems,
):
    copies = fetch([(tile_hbm, tile_ref), (cell_hbm, cell_ref), (rows_hbm, rows_ref)], sems)
    copies[0].wait()
    copies[1].wait()
    groups = tile_ref.shape[0]
    tiles = out_ref.shape[0] // (cap + 1)
    f32, bf16 = jnp.float32, jnp.bfloat16
    down = lax.broadcasted_iota(jnp.int32, (tiles, LANES), 0)
    row_of = lax.broadcasted_iota(jnp.int32, (LANES, LANES), 0)
    col_of = lax.broadcasted_iota(jnp.int32, (LANES, LANES), 1)
    earlier = (row_of < col_of).astype(bf16)
    place = row_of % cap
    taken = jnp.zeros((tiles, 1), f32)
    high = jnp.zeros((tiles, LANES), f32)
    low = jnp.zeros((tiles, LANES), f32)
    across = (((1,), (1,)), ((), ()))
    for g in range(groups):
        tile = tile_ref[pl.ds(g, 1), :]
        code = cell_ref[pl.ds(g, 1), :] + 1
        hit = (down == tile).astype(f32)
        hit16 = hit.astype(bf16)
        before = jnp.dot(hit16, earlier, preferred_element_type=f32) + taken
        pos = jnp.sum(hit * before, axis=0, keepdims=True).astype(jnp.int32)
        taken = taken + jnp.sum(hit, axis=1, keepdims=True)
        slot_vmem[pl.ds(g, 1), :] = tile * (cap + 1) + pos
        here = place == pos
        top = jnp.where(here, (code >> 6).astype(f32), 0.0).astype(bf16)
        rest = jnp.where(here, (code & 63).astype(f32), 0.0).astype(bf16)
        high += lax.dot_general(hit16, top, across, preferred_element_type=f32)
        low += lax.dot_general(hit16, rest, across, preferred_element_type=f32)
    copy = pltpu.make_async_copy(slot_vmem, slot_smem, sem)
    copy.start()
    code = high * 64.0 + low
    out_ref[pl.ds(cap, tiles, stride=cap + 1), :] = jnp.where(
        code == 0.0, jnp.float32(cells), code - 1.0
    )
    copies[2].wait()
    copy.wait()

    @pl.loop(0, groups)
    def _(g):
        base = pl.multiple_of(g * LANES, LANES)
        for u in range(LANES):
            out_ref[pl.ds(slot_smem[g, u], 1), :] = rows_ref[pl.ds(base + u, 1), :]

    part = out_ref.shape[0] // OUT_PARTS
    spans = [pl.ds(i * part, part) for i in range(OUT_PARTS)]
    for copy in fetch([(out_ref.at[at], out_hbm.at[at]) for at in spans], out_sems):
        copy.wait()


def fill_edge(edge, corner, north, rates_ref, west_ref, east_ref, out_ref):
    at = jnp.where(north, rates_ref.shape[0] - edge, 0)
    out_ref[pl.ds(0, edge), :] = rates_ref[pl.ds(pl.multiple_of(at, edge), edge), :]
    at = jnp.where(north, west_ref.shape[0] - corner, 0)
    for i, ref in enumerate((west_ref, east_ref)):
        out_ref[pl.ds(edge + i * corner, corner), :] = ref[
            pl.ds(pl.multiple_of(at, corner), corner), :
        ]


def edge_kernel(edge, corner, rates_ref, west_ref, east_ref, out_ref):
    fill_edge(edge, corner, jnp.logical_not(is_odd()), rates_ref, west_ref, east_ref, out_ref)


def arrived_kernel(
    cap, edge, corner, got_ref, rates_ref, west_ref, east_ref, cell_ref, out_ref
):
    block = cap + 1
    sources = got_ref.shape[0] // block
    per = LANES // cap
    lane = lax.broadcasted_iota(jnp.int32, (sources // per, LANES), 1)
    found = jnp.zeros((sources // per, LANES), jnp.float32)
    for j in range(per):
        part = got_ref[pl.ds(block * j + cap, sources // per, stride=block * per), :]
        found = jnp.where(lane // cap == j, part, found)
    cell_ref[...] = found.astype(jnp.int32)
    fill_edge(edge, corner, is_odd(), rates_ref, west_ref, east_ref, out_ref)


def land_kernel(
    cap, got_ref, cell_ref, rates_ref, out_ref, mate_ref, next_ref, cell_smem, sem, *accs
):
    block = cap + 1
    sources = got_ref.shape[0] // block
    per = LANES // cap
    copy = pltpu.make_async_copy(cell_ref, cell_smem, sem)
    copy.start()
    for acc in accs:
        acc[...] = jnp.zeros_like(acc)
    copy.wait()

    @pl.loop(0, sources // per)
    def _(m):
        base = m * (block * per)
        for j in range(per):
            for p in range(cap):
                acc = accs[p % len(accs)]
                at = pl.ds(cell_smem[m, j * cap + p], 1)
                acc[at, :] += got_ref[pl.ds(base + j * block + p, 1), :]

    step = 64

    @pl.loop(0, out_ref.shape[0] // step)
    def _(i):
        at = pl.ds(pl.multiple_of(i * step, step), step)
        total = accs[0][at, :]
        for acc in accs[1:]:
            total += acc[at, :]
        out_ref[at, :] = jnp.where(rates_ref[at, :] > 0.0, total, 0.0)

    edge = mate_ref.shape[0]
    last = out_ref.shape[0] - edge
    odd = is_odd()
    mate_ref[...] = out_ref[pl.ds(pl.multiple_of(jnp.where(odd, 0, last), edge), edge), :]
    next_ref[...] = out_ref[pl.ds(pl.multiple_of(jnp.where(odd, last, 0), edge), edge), :]


def is_odd():
    return lax.rem(lax.axis_index("gy"), 2) == 1


def either(odd, from_mate, from_next, use):
    @pl.when(odd)
    def _():
        use(from_mate, from_next)

    @pl.when(jnp.logical_not(odd))
    def _():
        use(from_next, from_mate)


def faces_kernel(
    lat_cells, lon_cells, total_rows,
    rates_ref, mate_ref, next_ref, west_ref, east_ref, east_face, north_face, wide,
):
    rim = ITERS
    rows = lat_cells + 2 * rim
    width = lon_cells + 2 * SUB

    def fill(r, line, at, west, west_at, east, east_at):
        wide[r, pl.ds(SUB, lon_cells), :] = line[pl.ds(at * lon_cells, lon_cells), :]
        wide[r, pl.ds(SUB - rim, rim), :] = west[pl.ds(west_at, rim), :]
        wide[r, pl.ds(SUB + lon_cells, rim), :] = east[pl.ds(east_at, rim), :]

    for at in range(lat_cells):
        fill(rim + at, rates_ref, at, west_ref, at * rim, east_ref, at * rim)

    def ends(low, high):
        for at in range(rim):
            west_at, east_at = rim * (lon_cells + at), rim * (lon_cells + rim + at)
            fill(at, low, at, low, west_at, low, east_at)
            fill(rim + lat_cells + at, high, at, high, west_at, high, east_at)

    either(is_odd(), mate_ref, next_ref, ends)
    half = LANES // 2
    zonal_lane = lax.broadcasted_iota(jnp.int32, (width, LANES), 1) < half

    @pl.loop(0, rows - 1)
    def _(r):
        here = wide[r]
        ocean_east = pltpu.roll(here, width - 1, 0) > 0.0
        ocean_north = wide[r + 1] > 0.0
        swapped = pltpu.roll(here, half, 1)
        row = lax.rem(lax.axis_index("gy") * lat_cells + r - rim + total_rows, total_rows)
        east_face[r] = jnp.where(ocean_east, jnp.where(zonal_lane, here, swapped), 0.0)
        north_face[r] = jnp.where(
            ocean_north & (row != total_rows - 1), jnp.where(zonal_lane, swapped, here), 0.0
        )


def ends_kernel(
    lat_cells, lon_cells, state_ref, mate_ref, next_ref, _, low_ref, high_ref, first_ref
):
    def pick(low, high):
        low_ref[...] = low[...]
        high_ref[...] = high[...]

    either(is_odd(), mate_ref, next_ref, pick)
    columns(lat_cells, lon_cells, 0, state_ref, low_ref, high_ref, first_ref)


def columns(lat_cells, lon_cells, start, state_ref, low_ref, high_ref, out_ref):
    rim = ITERS
    for r in range(lat_cells + 2 * rim):
        if r < rim:
            line, at = low_ref, r
        elif r < rim + lat_cells:
            line, at = state_ref, r - rim
        else:
            line, at = high_ref, r - rim - lat_cells
        out_ref[pl.ds(r * rim, rim), :] = line[pl.ds(at * lon_cells + start, rim), :]


def next_line(r, south, old, east, north, width):
    s = old[r]
    flux_east = east(r) * (pltpu.roll(s, width - 1, 0) - s)
    flux_north = north(r) * (old[r + 1] - s)
    return s + flux_east - pltpu.roll(flux_east, 1, 0) + flux_north - south, flux_north


def bulk_kernel(
    lat_cells, lon_cells, state_ref, low_ref, high_ref, east_face, north_face,
    out_ref, last_ref, even, odd,
):
    rim = ITERS
    rows = lat_cells + 2 * rim
    own = pl.ds(SUB, lon_cells)
    columns(lat_cells, lon_cells, lon_cells - rim, state_ref, low_ref, high_ref, last_ref)

    def east(r):
        return east_face[r, own, :]

    def north(r):
        return north_face[r, own, :]

    for r in range(rim):
        even[r] = low_ref[pl.ds(r * lon_cells, lon_cells), :]
        even[rim + lat_cells + r] = high_ref[pl.ds(r * lon_cells, lon_cells), :]

    @pl.loop(0, lat_cells)
    def _(r):
        even[rim + r] = state_ref[pl.ds(pl.multiple_of(r * lon_cells, lon_cells), lon_cells), :]

    for step in range(ITERS):
        old, new = (even, odd) if step % 2 == 0 else (odd, even)

        def line(r, south):
            s, south = next_line(r, south, old, east, north, lon_cells)
            if step < ITERS - 1:
                new[r] = s
            else:
                at = pl.multiple_of((r - rim) * lon_cells, lon_cells)
                out_ref[pl.ds(at, lon_cells), :] = s
            return south

        south = north(step) * (old[step + 1] - old[step])
        lax.fori_loop(step + 1, rows - 1 - step, line, south)


def finish_kernel(
    lat_cells, lon_cells, bulk_ref, state_ref, low_ref, high_ref, west_ref, east_ref,
    east_face, north_face, out_hbm, even, odd, out_ref, sems,
):
    rim = ITERS
    rows = lat_cells + 2 * rim
    span = 2 * SUB
    width = 2 * span
    windows = (pl.ds(0, span), pl.ds(lon_cells, span))

    def east(r):
        return jnp.concatenate([east_face[r, w, :] for w in windows], axis=0)

    def north(r):
        return jnp.concatenate([north_face[r, w, :] for w in windows], axis=0)

    for r in range(rows):
        if r < rim:
            line, at = low_ref, r
        elif r < rim + lat_cells:
            line, at = state_ref, r - rim
        else:
            line, at = high_ref, r - rim - lat_cells
        even[r, pl.ds(SUB - rim, rim), :] = west_ref[pl.ds(r * rim, rim), :]
        even[r, pl.ds(SUB, SUB), :] = line[pl.ds(at * lon_cells, SUB), :]
        even[r, pl.ds(span, SUB), :] = line[pl.ds((at + 1) * lon_cells - SUB, SUB), :]
        even[r, pl.ds(span + SUB, rim), :] = east_ref[pl.ds(r * rim, rim), :]

    copies = []
    for step in range(ITERS):
        old, new = (even, odd) if step % 2 == 0 else (odd, even)
        south = north(step) * (old[step + 1] - old[step])
        for r in range(step + 1, rows - 1 - step):
            s, south = next_line(r, south, old, east, north, width)
            if step < ITERS - 1:
                new[r] = s
                continue
            at = (r - rim) * lon_cells
            column = jnp.concatenate(
                [
                    s[SUB : SUB + rim],
                    bulk_ref[pl.ds(at + rim, lon_cells - 2 * rim), :],
                    s[span + SUB - rim : span + SUB],
                ],
                axis=0,
            )
            out_ref[:, r - rim, :] = column.T
            done = r - rim + 1
            if done % SUB == 0:
                ready = pl.ds(done - SUB, SUB)
                copies += fetch(
                    [(out_ref.at[:, ready, :], out_hbm.at[:, ready, :])],
                    sems.at[pl.ds(done // SUB - 1, 1)],
                )
    for copy in copies:
        copy.wait()


def cost(microseconds):
    return pl.CostEstimate(
        flops=0, bytes_accessed=microseconds * 3_000_000, transcendentals=0
    )


def params(limit):
    return pltpu.CompilerParams(vmem_limit_bytes=limit)


def on_device(obs_rows, obs_tile, obs_cell, land_sea, zonal_rate, meridional_rate):
    count_x = lax.axis_size("gx")
    count_y = lax.axis_size("gy")
    devices = count_x * count_y
    owned, row_width = obs_rows.shape
    cap = 2 * owned // devices
    levels, lat_cells, lon_cells = land_sea.shape
    cells = lat_cells * lon_cells
    variables = row_width // levels
    rim = ITERS
    f32, i32 = jnp.float32, jnp.int32
    groups = owned // LANES
    sent = devices * (cap + 1)

    packed = pl.pallas_call(
        functools.partial(pack_kernel, cap, cells),
        out_shape=jax.ShapeDtypeStruct((sent, LANES), f32),
        in_specs=[HBM] * 3,
        out_specs=HBM,
        scratch_shapes=[
            pltpu.VMEM((groups, LANES), i32),
            pltpu.VMEM((groups, LANES), i32),
            pltpu.VMEM((owned, LANES), f32),
            pltpu.VMEM((sent, LANES), f32),
            pltpu.VMEM((groups, LANES), i32),
            pltpu.SMEM((groups, LANES), i32),
            pltpu.SemaphoreType.DMA,
            pltpu.SemaphoreType.DMA((3,)),
            pltpu.SemaphoreType.DMA((OUT_PARTS,)),
        ],
        compiler_params=params(63 << 20),
    )(obs_tile.reshape(groups, LANES), obs_cell.reshape(groups, LANES), obs_rows)
    got = lax.all_to_all(
        packed.reshape(sent, 1, LANES), ("gx", "gy"), split_axis=0, concat_axis=0, tiled=True
    ).reshape(sent, LANES)

    rates = pl.pallas_call(
        rates_kernel,
        out_shape=jax.ShapeDtypeStruct((cells, LANES), f32),
        in_specs=[HBM] * 3,
        out_specs=VMEM,
        scratch_shapes=[
            pltpu.VMEM(land_sea.shape, i32),
            pltpu.VMEM(land_sea.shape, f32),
            pltpu.VMEM(land_sea.shape, f32),
            pltpu.SemaphoreType.DMA((3,)),
        ],
        compiler_params=params(4 << 20),
        cost_estimate=cost(2),
    )(land_sea, zonal_rate, meridional_rate)

    def column_ends(*blocks):
        tall = [t.reshape(-1, lon_cells, LANES) for t in blocks]
        first = jnp.concatenate([t[:, :rim] for t in tall]).reshape(-1, LANES)
        last = jnp.concatenate([t[:, lon_cells - rim :] for t in tall]).reshape(-1, LANES)
        return first, last

    edge = rim * lon_cells
    corner = rim * rim
    west, east = from_both(*column_ends(rates), "gx")
    tall = jax.ShapeDtypeStruct((edge + 2 * corner, LANES), f32)
    to_mate = pl.pallas_call(
        functools.partial(edge_kernel, edge, corner),
        out_shape=tall,
        in_specs=[VMEM] * 3,
        out_specs=VMEM,
        compiler_params=params(1 << 20),
    )(rates, west, east)
    r_mate = lax.ppermute(to_mate, "gy", mates())
    cell, to_next = pl.pallas_call(
        functools.partial(arrived_kernel, cap, edge, corner),
        out_shape=[jax.ShapeDtypeStruct((devices * cap // LANES, LANES), i32), tall],
        in_specs=[VMEM] * 4,
        out_specs=[VMEM] * 2,
        compiler_params=params(1 << 20),
    )(got, rates, west, east)
    r_next = lax.ppermute(to_next, "gy", nexts())

    flat = jax.ShapeDtypeStruct((edge, LANES), f32)
    state, to_mate, to_next = pl.pallas_call(
        functools.partial(land_kernel, cap),
        out_shape=[jax.ShapeDtypeStruct((cells, LANES), f32), flat, flat],
        in_specs=[VMEM] * 3,
        out_specs=[VMEM] * 3,
        scratch_shapes=[
            pltpu.SMEM((devices * cap // LANES, LANES), i32),
            pltpu.SemaphoreType.DMA,
        ]
        + [pltpu.VMEM((cells + SUB, LANES), f32)] * ACCS,
        compiler_params=params(8 << 20),
        cost_estimate=cost(7),
    )(got, cell, rates)

    rows = lat_cells + 2 * rim
    wide = (rows, lon_cells + 2 * SUB, LANES)
    faces = pl.pallas_call(
        functools.partial(faces_kernel, lat_cells, lon_cells, lat_cells * count_y),
        out_shape=[jax.ShapeDtypeStruct(wide, f32)] * 2,
        in_specs=[VMEM] * 5,
        out_specs=[VMEM] * 2,
        scratch_shapes=[pltpu.VMEM(wide, f32)],
        compiler_params=params(4 << 20),
        cost_estimate=cost(2),
    )(rates, r_mate, r_next, west, east)

    s_next = lax.ppermute(to_next, "gy", nexts())
    s_mate = lax.ppermute(to_mate, "gy", mates())
    strip = jax.ShapeDtypeStruct((rows * rim, LANES), f32)
    s_low, s_high, to_west = pl.pallas_call(
        functools.partial(ends_kernel, lat_cells, lon_cells),
        out_shape=[flat, flat, strip],
        in_specs=[VMEM] * 3 + [pl.BlockSpec(memory_space=pl.ANY)],
        out_specs=[VMEM] * 3,
        compiler_params=params(1 << 20),
    )(state, s_mate, s_next, faces[0])
    s_east = lax.ppermute(to_west, "gx", ring("gx", -1))
    narrow = (rows, lon_cells, LANES)
    bulk, to_east = pl.pallas_call(
        functools.partial(bulk_kernel, lat_cells, lon_cells),
        out_shape=[jax.ShapeDtypeStruct((cells, LANES), f32), strip],
        in_specs=[VMEM] * 5,
        out_specs=[VMEM] * 2,
        scratch_shapes=[pltpu.VMEM(narrow, f32)] * 2,
        compiler_params=params(8 << 20),
        cost_estimate=cost(3),
    )(state, s_low, s_high, *faces)
    s_west = lax.ppermute(to_east, "gx", ring("gx", 1))
    strips = (rows, 4 * SUB, LANES)
    out_shape = (row_width, lat_cells, lon_cells)
    out = pl.pallas_call(
        functools.partial(finish_kernel, lat_cells, lon_cells),
        out_shape=jax.ShapeDtypeStruct(out_shape, f32),
        in_specs=[VMEM] * 8,
        out_specs=HBM,
        scratch_shapes=[pltpu.VMEM(strips, f32)] * 2
        + [pltpu.VMEM(out_shape, f32), pltpu.SemaphoreType.DMA((lat_cells // SUB,))],
        compiler_params=params(4 << 20),
        cost_estimate=cost(3),
    )(bulk, state, s_low, s_high, s_west, s_east, *faces)
    return out.reshape(variables, levels, lat_cells, lon_cells)


def solution(mesh):
    placed = (
        P(("gx", "gy"), None),
        P(("gx", "gy"), None),
        P(("gx", "gy")),
        P(None, "gy", "gx"),
        P(None, "gy", "gx"),
        P(None, "gy", "gx"),
    )
    return jax.shard_map(
        on_device, mesh=mesh, in_specs=placed, out_specs=P(None, None, "gy", "gx"), check_vma=False
    )
```

```python
import functools

import jax
import jax.numpy as jnp
from jax import lax
from jax.experimental import pallas as pl
from jax.experimental.pallas import tpu as pltpu
from jax.sharding import PartitionSpec as P

ITERS = 4
LANES = 128
SUB = 8
ACCS = 4
OUT_PARTS = 8
VMEM = pl.BlockSpec(memory_space=pltpu.VMEM)
HBM = pl.BlockSpec(memory_space=pltpu.HBM)


def pairs(axis, start, closed=True):
    count = lax.axis_size(axis)
    firsts = range(start, count if closed else count - 1, 2)
    both = [(i, (i + 1) % count) for i in firsts]
    return both + [(b, a) for a, b in both]


def to_both(ends):
    low = lax.ppermute(ends, "gx", pairs("gx", 0))
    high = lax.ppermute(ends, "gx", pairs("gx", 1))
    even = lax.axis_index("gx") % 2 == 0
    return jnp.where(even, high, low), jnp.where(even, low, high)


def column_ends(ref, lat_cells, lon_cells):
    first = lax.broadcasted_iota(jnp.int32, (SUB, LANES), 0) < SUB // 2
    return jnp.concatenate(
        [
            jnp.where(
                first,
                ref[pl.ds(r * lon_cells, SUB), :],
                ref[pl.ds((r + 1) * lon_cells - SUB, SUB), :],
            )
            for r in range(lat_cells)
        ],
        axis=0,
    )


def fetch(pairs, sems):
    copies = [pltpu.make_async_copy(a, b, sems.at[i]) for i, (a, b) in enumerate(pairs)]
    for copy in copies:
        copy.start()
    return copies


def rates_kernel(land_hbm, zonal_hbm, merid_hbm, out_ref, ends_ref, land_ref, zonal_ref, merid_ref, sems):
    lat_cells, lon_cells = land_ref.shape[1:]
    for copy in fetch(
        [(land_hbm, land_ref), (zonal_hbm, zonal_ref), (merid_hbm, merid_ref)], sems
    ):
        copy.wait()
    for lat in range(lat_cells):
        ocean = land_ref[:, lat, :].astype(jnp.float32)
        both = jnp.concatenate(
            [zonal_ref[:, lat, :] * ocean, merid_ref[:, lat, :] * ocean], axis=0
        )
        out_ref[pl.ds(lat * lon_cells, lon_cells), :] = both.T
    ends_ref[...] = column_ends(out_ref, lat_cells, lon_cells)


def pack_kernel(
    cap, cells, tile_hbm, cell_hbm, rows_hbm, out_hbm,
    tile_ref, cell_ref, rows_ref, out_ref, slot_vmem, slot_smem, sem, sems, out_sems,
):
    copies = fetch([(tile_hbm, tile_ref), (cell_hbm, cell_ref), (rows_hbm, rows_ref)], sems)
    out_ref[...] = jnp.zeros_like(out_ref)
    copies[0].wait()
    copies[1].wait()
    groups = tile_ref.shape[0]
    tiles = out_ref.shape[0] // (cap + 1)
    f32, bf16 = jnp.float32, jnp.bfloat16
    down = lax.broadcasted_iota(jnp.int32, (tiles, LANES), 0)
    row_of = lax.broadcasted_iota(jnp.int32, (LANES, LANES), 0)
    col_of = lax.broadcasted_iota(jnp.int32, (LANES, LANES), 1)
    earlier = (row_of < col_of).astype(bf16)
    place = row_of % cap
    taken = jnp.zeros((tiles, 1), f32)
    high = jnp.zeros((tiles, LANES), f32)
    low = jnp.zeros((tiles, LANES), f32)
    across = (((1,), (1,)), ((), ()))
    for g in range(groups):
        tile = tile_ref[pl.ds(g, 1), :]
        code = cell_ref[pl.ds(g, 1), :] + 1
        hit = (down == tile).astype(f32)
        hit16 = hit.astype(bf16)
        before = jnp.dot(hit16, earlier, preferred_element_type=f32) + taken
        pos = jnp.sum(hit * before, axis=0, keepdims=True).astype(jnp.int32)
        taken = taken + jnp.sum(hit, axis=1, keepdims=True)
        slot_vmem[pl.ds(g, 1), :] = tile * (cap + 1) + pos
        here = place == pos
        top = jnp.where(here, (code >> 6).astype(f32), 0.0).astype(bf16)
        rest = jnp.where(here, (code & 63).astype(f32), 0.0).astype(bf16)
        high += lax.dot_general(hit16, top, across, preferred_element_type=f32)
        low += lax.dot_general(hit16, rest, across, preferred_element_type=f32)
    copy = pltpu.make_async_copy(slot_vmem, slot_smem, sem)
    copy.start()
    code = high * 64.0 + low
    out_ref[pl.ds(cap, tiles, stride=cap + 1), :] = jnp.where(
        code == 0.0, jnp.float32(cells), code - 1.0
    )
    copies[2].wait()
    copy.wait()

    @pl.loop(0, groups)
    def _(g):
        base = pl.multiple_of(g * LANES, LANES)
        for u in range(LANES):
            out_ref[pl.ds(slot_smem[g, u], 1), :] = rows_ref[pl.ds(base + u, 1), :]

    part = out_ref.shape[0] // OUT_PARTS
    spans = [pl.ds(i * part, part) for i in range(OUT_PARTS)]
    for copy in fetch([(out_ref.at[at], out_hbm.at[at]) for at in spans], out_sems):
        copy.wait()


def widen(dest, row, lat, lon_cells, main_ref, west_ref, east_ref):
    at = pl.multiple_of(lat * SUB, SUB)
    dest[row, pl.ds(0, SUB), :] = west_ref[pl.ds(at, SUB), :]
    at = pl.multiple_of(lat * lon_cells, lon_cells)
    dest[row, pl.ds(SUB, lon_cells), :] = main_ref[pl.ds(at, lon_cells), :]
    at = pl.multiple_of(lat * SUB, SUB)
    dest[row, pl.ds(SUB + lon_cells, SUB), :] = east_ref[pl.ds(at, SUB), :]


def slab(dest, north, lat_cells, lon_cells, main_ref, west_ref, east_ref):
    start = jnp.where(north, lat_cells - ITERS, 0)
    for r in range(ITERS):
        widen(dest, r, start + r, lon_cells, main_ref, west_ref, east_ref)


def slabs_kernel(lat_cells, lon_cells, main_ref, west_ref, east_ref, *refs):
    mate_ref, next_ref = refs[-2:]
    odd = is_odd()
    slab(next_ref, odd, lat_cells, lon_cells, main_ref, west_ref, east_ref)
    slab(mate_ref, jnp.logical_not(odd), lat_cells, lon_cells, main_ref, west_ref, east_ref)


def arrived_kernel(cap, got_ref, cell_ref):
    block = cap + 1
    sources = got_ref.shape[0] // block
    per = LANES // cap
    lane = lax.broadcasted_iota(jnp.int32, (sources // per, LANES), 1)
    found = jnp.zeros((sources // per, LANES), jnp.float32)
    for j in range(per):
        part = got_ref[pl.ds(block * j + cap, sources // per, stride=block * per), :]
        found = jnp.where(lane // cap == j, part, found)
    cell_ref[...] = found.astype(jnp.int32)


def ends_kernel(cap, lat_cells, lon_cells, got_ref, cell_ref, rates_ref, out_ref):
    f32, bf16 = jnp.float32, jnp.bfloat16
    block = cap + 1
    per = LANES // cap
    ends = lat_cells * SUB
    place = lax.broadcasted_iota(jnp.int32, (ends, LANES), 0)
    column = place % SUB
    column = jnp.where(column < SUB // 2, column, column + lon_cells - SUB)
    place = place // SUB * lon_cells + column
    total = jnp.zeros((ends, LANES), f32)
    for m in range(cell_ref.shape[0]):
        hit = (place == cell_ref[pl.ds(m, 1), :]).astype(f32).astype(bf16)
        left = jnp.concatenate(
            [got_ref[pl.ds((m * per + j) * block, cap), :] for j in range(per)], axis=0
        )
        for piece in range(3):
            part = left.astype(bf16)
            total += jnp.dot(hit, part, preferred_element_type=f32)
            if piece < 2:
                left = left - part.astype(f32)
    ocean = column_ends(rates_ref, lat_cells, lon_cells) > 0.0
    out_ref[...] = jnp.where(ocean, total, 0.0)


def land_kernel(cap, got_ref, cell_ref, rates_ref, out_ref, cell_smem, sem, *accs):
    block = cap + 1
    per = LANES // cap
    copy = pltpu.make_async_copy(cell_ref, cell_smem, sem)
    copy.start()
    for acc in accs:
        acc[...] = jnp.zeros_like(acc)
    copy.wait()

    @pl.loop(0, cell_ref.shape[0])
    def _(m):
        base = m * (block * per)
        for j in range(per):
            for p in range(cap):
                acc = accs[p % len(accs)]
                at = pl.ds(cell_smem[m, j * cap + p], 1)
                acc[at, :] += got_ref[pl.ds(base + j * block + p, 1), :]

    step = 64

    @pl.loop(0, out_ref.shape[0] // step)
    def _(i):
        at = pl.ds(pl.multiple_of(i * step, step), step)
        total = accs[0][at, :]
        for acc in accs[1:]:
            total += acc[at, :]
        out_ref[at, :] = jnp.where(rates_ref[at, :] > 0.0, total, 0.0)


def is_odd():
    return lax.rem(lax.axis_index("gy"), 2) == 1


def either(from_mate, from_next, use):
    odd = is_odd()

    @pl.when(odd)
    def _():
        use(from_mate, from_next)

    @pl.when(jnp.logical_not(odd))
    def _():
        use(from_next, from_mate)


def faces_kernel(
    lat_cells, lon_cells, total_rows,
    rates_ref, mate_ref, next_ref, west_ref, east_ref, east_face, north_face, wide,
):
    rim = ITERS
    rows = lat_cells + 2 * rim
    width = lon_cells + 2 * SUB

    @pl.loop(0, lat_cells)
    def _(r):
        widen(wide, rim + r, r, lon_cells, rates_ref, west_ref, east_ref)

    def ends(low, high):
        for r in range(rim):
            wide[r] = low[r]
            wide[rim + lat_cells + r] = high[r]

    either(mate_ref, next_ref, ends)
    half = LANES // 2
    zonal_lane = lax.broadcasted_iota(jnp.int32, (width, LANES), 1) < half

    @pl.loop(0, rows - 1)
    def _(r):
        here = wide[r]
        ocean_east = pltpu.roll(here, width - 1, 0) > 0.0
        ocean_north = wide[r + 1] > 0.0
        swapped = pltpu.roll(here, half, 1)
        row = lax.rem(lax.axis_index("gy") * lat_cells + r - rim + total_rows, total_rows)
        east_face[r] = jnp.where(ocean_east, jnp.where(zonal_lane, here, swapped), 0.0)
        north_face[r] = jnp.where(
            ocean_north & (row != total_rows - 1), jnp.where(zonal_lane, swapped, here), 0.0
        )


def next_row(s, north, south_flux, east_face, north_face):
    flux_east = east_face * (pltpu.roll(s, s.shape[0] - 1, 0) - s)
    flux_north = north_face * (north - s)
    s = s + flux_east - pltpu.roll(flux_east, 1, 0) + flux_north - south_flux
    return s, flux_north


def inner_kernel(
    lat_cells, lon_cells, state_ref, west_ref, east_ref, east_face, north_face, *steps
):
    rim = ITERS

    @pl.loop(0, lat_cells)
    def _(r):
        widen(steps[0], r, r, lon_cells, state_ref, west_ref, east_ref)

    for step in range(ITERS):
        old, new = steps[step], steps[step + 1]

        def line(r, south):
            face = rim + r
            new[r], south = next_row(old[r], old[r + 1], south, east_face[face], north_face[face])
            return south

        south = north_face[rim + step] * (old[step + 1] - old[step])
        lax.fori_loop(step + 1, lat_cells - 1 - step, line, south)


def outer_kernel(lat_cells, lon_cells, mate_ref, next_ref, east_face, north_face, *refs):
    rim = ITERS
    steps = refs[: ITERS + 1]
    out_hbm, low_rows, high_rows, out_ref, sems = refs[ITERS + 1 :]

    def take(low, high):
        for r in range(rim):
            low_rows[0, r] = low[r]
            high_rows[0, r] = high[r]

    either(mate_ref, next_ref, take)

    def at(step, row):
        if row < step:
            return low_rows[step, row + rim - step]
        if row >= lat_cells - step:
            return high_rows[step, row - lat_cells + step]
        return steps[step][row]

    def write(row, s):
        out_ref[:, row, :] = s[SUB : SUB + lon_cells].T

    copies = []
    for rows, first in ((low_rows, -rim), (high_rows, lat_cells)):
        for step in range(1, ITERS + 1):
            start = first + step if first < 0 else first - step
            below = rim + start - 1
            south = north_face[below] * (at(step - 1, start) - at(step - 1, start - 1))
            for i in range(rim):
                r = start + i
                s, south = next_row(
                    at(step - 1, r), at(step - 1, r + 1), south,
                    east_face[rim + r], north_face[rim + r],
                )
                if step < ITERS:
                    rows[step, i] = s
                else:
                    write(r, s)
        inside = range(rim, SUB) if first < 0 else range(SUB, lat_cells - rim)
        for r in inside:
            write(r, steps[ITERS][r])
        side = 0 if first < 0 else 1
        ready = pl.ds(side * SUB, SUB)
        copies += fetch(
            [(out_ref.at[:, ready, :], out_hbm.at[:, ready, :])], sems.at[pl.ds(side, 1)]
        )
    for copy in copies:
        copy.wait()


def cost(microseconds):
    return pl.CostEstimate(
        flops=0, bytes_accessed=microseconds * 3_000_000, transcendentals=0
    )


def params(limit):
    return pltpu.CompilerParams(vmem_limit_bytes=limit)


def on_device(obs_rows, obs_tile, obs_cell, land_sea, zonal_rate, meridional_rate):
    count_x = lax.axis_size("gx")
    count_y = lax.axis_size("gy")
    devices = count_x * count_y
    owned, row_width = obs_rows.shape
    cap = 2 * owned // devices
    levels, lat_cells, lon_cells = land_sea.shape
    cells = lat_cells * lon_cells
    variables = row_width // levels
    rim = ITERS
    f32, i32 = jnp.float32, jnp.int32
    groups = owned // LANES
    sent = devices * (cap + 1)

    packed = pl.pallas_call(
        functools.partial(pack_kernel, cap, cells),
        out_shape=jax.ShapeDtypeStruct((sent, LANES), f32),
        in_specs=[HBM] * 3,
        out_specs=HBM,
        scratch_shapes=[
            pltpu.VMEM((groups, LANES), i32),
            pltpu.VMEM((groups, LANES), i32),
            pltpu.VMEM((owned, LANES), f32),
            pltpu.VMEM((sent, LANES), f32),
            pltpu.VMEM((groups, LANES), i32),
            pltpu.SMEM((groups, LANES), i32),
            pltpu.SemaphoreType.DMA,
            pltpu.SemaphoreType.DMA((3,)),
            pltpu.SemaphoreType.DMA((OUT_PARTS,)),
        ],
        compiler_params=params(63 << 20),
    )(obs_tile.reshape(groups, LANES), obs_cell.reshape(groups, LANES), obs_rows)
    got = lax.all_to_all(
        packed.reshape(sent, 1, LANES), ("gx", "gy"), split_axis=0, concat_axis=0, tiled=True
    ).reshape(sent, LANES)

    tile_ends = jax.ShapeDtypeStruct((lat_cells * SUB, LANES), f32)
    rates, r_ends = pl.pallas_call(
        rates_kernel,
        out_shape=[jax.ShapeDtypeStruct((cells, LANES), f32), tile_ends],
        in_specs=[HBM] * 3,
        out_specs=[VMEM] * 2,
        scratch_shapes=[
            pltpu.VMEM(land_sea.shape, i32),
            pltpu.VMEM(land_sea.shape, f32),
            pltpu.VMEM(land_sea.shape, f32),
            pltpu.SemaphoreType.DMA((3,)),
        ],
        compiler_params=params(4 << 20),
        cost_estimate=cost(2),
    )(land_sea, zonal_rate, meridional_rate)
    r_west, r_east = to_both(r_ends)
    width = lon_cells + 2 * SUB
    edge = jax.ShapeDtypeStruct((rim, width, LANES), f32)
    to_mate, to_next = pl.pallas_call(
        functools.partial(slabs_kernel, lat_cells, lon_cells),
        out_shape=[edge] * 2,
        in_specs=[VMEM] * 3,
        out_specs=[VMEM] * 2,
        compiler_params=params(1 << 20),
    )(rates, r_west, r_east)
    r_mate = lax.ppermute(to_mate, "gy", pairs("gy", 0))
    r_next = lax.ppermute(to_next, "gy", pairs("gy", 1, False))

    listed = (devices * cap // LANES, LANES)
    cell = pl.pallas_call(
        functools.partial(arrived_kernel, cap),
        out_shape=jax.ShapeDtypeStruct(listed, i32),
        in_specs=[VMEM],
        out_specs=VMEM,
        compiler_params=params(1 << 20),
    )(got)
    s_ends = pl.pallas_call(
        functools.partial(ends_kernel, cap, lat_cells, lon_cells),
        out_shape=tile_ends,
        in_specs=[VMEM] * 3,
        out_specs=VMEM,
        compiler_params=params(2 << 20),
        cost_estimate=cost(1),
    )(got, cell, rates)
    s_west, s_east = to_both(s_ends)
    state = pl.pallas_call(
        functools.partial(land_kernel, cap),
        out_shape=jax.ShapeDtypeStruct((cells, LANES), f32),
        in_specs=[VMEM] * 3,
        out_specs=VMEM,
        scratch_shapes=[pltpu.SMEM(listed, i32), pltpu.SemaphoreType.DMA]
        + [pltpu.VMEM((cells + SUB, LANES), f32)] * ACCS,
        compiler_params=params(8 << 20),
        cost_estimate=cost(7),
    )(got, cell, rates)

    to_mate, to_next = pl.pallas_call(
        functools.partial(slabs_kernel, lat_cells, lon_cells),
        out_shape=[edge] * 2,
        in_specs=[VMEM] * 3 + [pl.BlockSpec(memory_space=pl.ANY)] * 2,
        out_specs=[VMEM] * 2,
        compiler_params=params(1 << 20),
    )(state, s_west, s_east, r_mate, r_next)
    s_next = lax.ppermute(to_next, "gy", pairs("gy", 1, False))
    s_mate = lax.ppermute(to_mate, "gy", pairs("gy", 0))
    wide = (lat_cells + 2 * rim, width, LANES)
    faces = pl.pallas_call(
        functools.partial(faces_kernel, lat_cells, lon_cells, lat_cells * count_y),
        out_shape=[jax.ShapeDtypeStruct(wide, f32)] * 2,
        in_specs=[VMEM] * 5,
        out_specs=[VMEM] * 2,
        scratch_shapes=[pltpu.VMEM(wide, f32)],
        compiler_params=params(4 << 20),
        cost_estimate=cost(2),
    )(rates, r_mate, r_next, r_west, r_east)
    steps = pl.pallas_call(
        functools.partial(inner_kernel, lat_cells, lon_cells),
        out_shape=[jax.ShapeDtypeStruct((lat_cells, width, LANES), f32)] * (ITERS + 1),
        in_specs=[VMEM] * 5,
        out_specs=[VMEM] * (ITERS + 1),
        compiler_params=params(2 << 20),
        cost_estimate=cost(2),
    )(state, s_west, s_east, *faces)
    out_shape = (row_width, lat_cells, lon_cells)
    out = pl.pallas_call(
        functools.partial(outer_kernel, lat_cells, lon_cells),
        out_shape=jax.ShapeDtypeStruct(out_shape, f32),
        in_specs=[VMEM] * (4 + ITERS + 1),
        out_specs=HBM,
        scratch_shapes=[pltpu.VMEM((ITERS, rim, width, LANES), f32)] * 2
        + [pltpu.VMEM(out_shape, f32), pltpu.SemaphoreType.DMA((2,))],
        compiler_params=params(6 << 20),
        cost_estimate=cost(3),
    )(s_mate, s_next, *faces, *steps)
    return out.reshape(variables, levels, lat_cells, lon_cells)


def solution(mesh):
    placed = (
        P(("gx", "gy"), None),
        P(("gx", "gy"), None),
        P(("gx", "gy")),
        P(None, "gy", "gx"),
        P(None, "gy", "gx"),
        P(None, "gy", "gx"),
    )
    return jax.shard_map(
        on_device, mesh=mesh, in_specs=placed, out_specs=P(None, None, "gy", "gx"), check_vma=False
    )
```

```python
import functools

import jax
import jax.numpy as jnp
from jax import lax
from jax.experimental import pallas as pl
from jax.experimental.pallas import tpu as pltpu
from jax.sharding import PartitionSpec as P

ITERS = 4
LANES = 128
SUB = 8
ACCS = 4
OUT_PARTS = 8
VMEM = pl.BlockSpec(memory_space=pltpu.VMEM)
HBM = pl.BlockSpec(memory_space=pltpu.HBM)


def pairs(axis, start, closed=True):
    count = lax.axis_size(axis)
    firsts = range(start, count if closed else count - 1, 2)
    both = [(i, (i + 1) % count) for i in firsts]
    return both + [(b, a) for a, b in both]


def to_both(ends):
    low = lax.ppermute(ends, "gx", pairs("gx", 0))
    high = lax.ppermute(ends, "gx", pairs("gx", 1))
    even = lax.axis_index("gx") % 2 == 0
    return jnp.where(even, high, low), jnp.where(even, low, high)


def column_ends(ref, lat_cells, lon_cells):
    first = lax.broadcasted_iota(jnp.int32, (SUB, LANES), 0) < SUB // 2
    return jnp.concatenate(
        [
            jnp.where(
                first,
                ref[pl.ds(r * lon_cells, SUB), :],
                ref[pl.ds((r + 1) * lon_cells - SUB, SUB), :],
            )
            for r in range(lat_cells)
        ],
        axis=0,
    )


def fetch(pairs, sems):
    copies = [pltpu.make_async_copy(a, b, sems.at[i]) for i, (a, b) in enumerate(pairs)]
    for copy in copies:
        copy.start()
    return copies


def rates_kernel(land_hbm, zonal_hbm, merid_hbm, out_ref, ends_ref, land_ref, zonal_ref, merid_ref, sems):
    lat_cells, lon_cells = land_ref.shape[1:]
    for copy in fetch(
        [(land_hbm, land_ref), (zonal_hbm, zonal_ref), (merid_hbm, merid_ref)], sems
    ):
        copy.wait()
    for lat in range(lat_cells):
        ocean = land_ref[:, lat, :].astype(jnp.float32)
        both = jnp.concatenate(
            [zonal_ref[:, lat, :] * ocean, merid_ref[:, lat, :] * ocean], axis=0
        )
        out_ref[pl.ds(lat * lon_cells, lon_cells), :] = both.T
    ends_ref[...] = column_ends(out_ref, lat_cells, lon_cells)


def pack_kernel(
    cap, cells, tile_hbm, cell_hbm, rows_hbm, out_hbm,
    tile_ref, cell_ref, rows_ref, out_ref, slot_vmem, slot_smem, sem, sems, out_sems,
):
    copies = fetch([(tile_hbm, tile_ref), (cell_hbm, cell_ref), (rows_hbm, rows_ref)], sems)
    out_ref[...] = jnp.zeros_like(out_ref)
    copies[0].wait()
    copies[1].wait()
    groups = tile_ref.shape[0]
    tiles = out_ref.shape[0] // (cap + 1)
    f32, bf16 = jnp.float32, jnp.bfloat16
    down = lax.broadcasted_iota(jnp.int32, (tiles, LANES), 0)
    earlier = (
        lax.broadcasted_iota(jnp.int32, (LANES, 2 * LANES), 0)
        < lax.broadcasted_iota(jnp.int32, (LANES, 2 * LANES), 1)
    ).astype(bf16)
    place = lax.broadcasted_iota(jnp.int32, (LANES, LANES), 0) % cap
    hits, counts, spots = [], [], []
    for g in range(groups):
        hits.append((down == tile_ref[pl.ds(g, 1), :]).astype(f32).astype(bf16))
        counts.append(jnp.dot(hits[g], earlier, preferred_element_type=f32))
    taken = jnp.zeros((tiles, LANES), f32)
    for g in range(groups):
        tile = tile_ref[pl.ds(g, 1), :]
        before = jnp.where(down == tile, counts[g][:, :LANES] + taken, 0.0)
        spots.append(jnp.sum(before, axis=0, keepdims=True).astype(jnp.int32))
        taken += counts[g][:, LANES:]
        slot_vmem[pl.ds(g, 1), :] = tile * (cap + 1) + spots[g]
    copy = pltpu.make_async_copy(slot_vmem, slot_smem, sem)
    copy.start()
    codes = jnp.zeros((tiles, 2 * LANES), f32)
    for g in range(groups):
        here = place == spots[g]
        code = cell_ref[pl.ds(g, 1), :] + 1
        parts = [jnp.where(here, part.astype(f32), 0.0) for part in (code >> 6, code & 63)]
        codes += lax.dot_general(
            hits[g], jnp.concatenate(parts, axis=0).astype(bf16), (((1,), (1,)), ((), ())),
            preferred_element_type=f32,
        )
    code = codes[:, :LANES] * 64.0 + codes[:, LANES:]
    out_ref[pl.ds(cap, tiles, stride=cap + 1), :] = jnp.where(
        code == 0.0, jnp.float32(cells), code - 1.0
    )
    copies[2].wait()
    copy.wait()

    @pl.loop(0, groups)
    def _(g):
        base = pl.multiple_of(g * LANES, LANES)
        for u in range(LANES):
            out_ref[pl.ds(slot_smem[g, u], 1), :] = rows_ref[pl.ds(base + u, 1), :]

    part = out_ref.shape[0] // OUT_PARTS
    spans = [pl.ds(i * part, part) for i in range(OUT_PARTS)]
    for copy in fetch([(out_ref.at[at], out_hbm.at[at]) for at in spans], out_sems):
        copy.wait()


def widen(dest, row, lat, lon_cells, main_ref, west_ref, east_ref):
    at = pl.multiple_of(lat * SUB, SUB)
    dest[row, pl.ds(0, SUB), :] = west_ref[pl.ds(at, SUB), :]
    at = pl.multiple_of(lat * lon_cells, lon_cells)
    dest[row, pl.ds(SUB, lon_cells), :] = main_ref[pl.ds(at, lon_cells), :]
    at = pl.multiple_of(lat * SUB, SUB)
    dest[row, pl.ds(SUB + lon_cells, SUB), :] = east_ref[pl.ds(at, SUB), :]


def slab(dest, north, lat_cells, lon_cells, main_ref, west_ref, east_ref):
    start = jnp.where(north, lat_cells - ITERS, 0)
    for r in range(ITERS):
        widen(dest, r, start + r, lon_cells, main_ref, west_ref, east_ref)


def slabs_kernel(lat_cells, lon_cells, main_ref, west_ref, east_ref, *refs):
    mate_ref, next_ref = refs[-2:]
    odd = is_odd()
    slab(next_ref, odd, lat_cells, lon_cells, main_ref, west_ref, east_ref)
    slab(mate_ref, jnp.logical_not(odd), lat_cells, lon_cells, main_ref, west_ref, east_ref)


def arrived_kernel(cap, got_ref, cell_ref):
    block = cap + 1
    sources = got_ref.shape[0] // block
    per = LANES // cap
    lane = lax.broadcasted_iota(jnp.int32, (sources // per, LANES), 1)
    found = jnp.zeros((sources // per, LANES), jnp.float32)
    for j in range(per):
        part = got_ref[pl.ds(block * j + cap, sources // per, stride=block * per), :]
        found = jnp.where(lane // cap == j, part, found)
    cell_ref[...] = found.astype(jnp.int32)


def ends_kernel(cap, lat_cells, lon_cells, got_ref, cell_ref, rates_ref, out_ref):
    f32, bf16 = jnp.float32, jnp.bfloat16
    block = cap + 1
    per = LANES // cap
    ends = lat_cells * SUB
    place = lax.broadcasted_iota(jnp.int32, (ends, LANES), 0)
    column = place % SUB
    column = jnp.where(column < SUB // 2, column, column + lon_cells - SUB)
    place = place // SUB * lon_cells + column
    total = jnp.zeros((ends, LANES), f32)
    for m in range(cell_ref.shape[0]):
        hit = (place == cell_ref[pl.ds(m, 1), :]).astype(f32).astype(bf16)
        left = jnp.concatenate(
            [got_ref[pl.ds((m * per + j) * block, cap), :] for j in range(per)], axis=0
        )
        for piece in range(3):
            part = left.astype(bf16)
            total += jnp.dot(hit, part, preferred_element_type=f32)
            if piece < 2:
                left = left - part.astype(f32)
    ocean = column_ends(rates_ref, lat_cells, lon_cells) > 0.0
    out_ref[...] = jnp.where(ocean, total, 0.0)


def land_kernel(cap, got_ref, cell_ref, rates_ref, out_ref, cell_smem, sem, *accs):
    block = cap + 1
    per = LANES // cap
    copy = pltpu.make_async_copy(cell_ref, cell_smem, sem)
    copy.start()
    for acc in accs:
        acc[...] = jnp.zeros_like(acc)
    copy.wait()

    @pl.loop(0, cell_ref.shape[0])
    def _(m):
        base = m * (block * per)
        for j in range(per):
            for p in range(cap):
                acc = accs[p % len(accs)]
                at = pl.ds(cell_smem[m, j * cap + p], 1)
                acc[at, :] += got_ref[pl.ds(base + j * block + p, 1), :]

    step = 64

    @pl.loop(0, out_ref.shape[0] // step)
    def _(i):
        at = pl.ds(pl.multiple_of(i * step, step), step)
        total = accs[0][at, :]
        for acc in accs[1:]:
            total += acc[at, :]
        out_ref[at, :] = jnp.where(rates_ref[at, :] > 0.0, total, 0.0)


def is_odd():
    return lax.rem(lax.axis_index("gy"), 2) == 1


def either(from_mate, from_next, use):
    odd = is_odd()

    @pl.when(odd)
    def _():
        use(from_mate, from_next)

    @pl.when(jnp.logical_not(odd))
    def _():
        use(from_next, from_mate)


def faces_kernel(
    lat_cells, lon_cells, total_rows,
    rates_ref, mate_ref, next_ref, west_ref, east_ref, east_face, north_face, wide,
):
    rim = ITERS
    rows = lat_cells + 2 * rim
    width = lon_cells + 2 * SUB

    @pl.loop(0, lat_cells)
    def _(r):
        widen(wide, rim + r, r, lon_cells, rates_ref, west_ref, east_ref)

    def ends(low, high):
        for r in range(rim):
            wide[r] = low[r]
            wide[rim + lat_cells + r] = high[r]

    either(mate_ref, next_ref, ends)
    half = LANES // 2
    zonal_lane = lax.broadcasted_iota(jnp.int32, (width, LANES), 1) < half

    @pl.loop(0, rows - 1)
    def _(r):
        here = wide[r]
        ocean_east = pltpu.roll(here, width - 1, 0) > 0.0
        ocean_north = wide[r + 1] > 0.0
        swapped = pltpu.roll(here, half, 1)
        row = lax.rem(lax.axis_index("gy") * lat_cells + r - rim + total_rows, total_rows)
        east_face[r] = jnp.where(ocean_east, jnp.where(zonal_lane, here, swapped), 0.0)
        north_face[r] = jnp.where(
            ocean_north & (row != total_rows - 1), jnp.where(zonal_lane, swapped, here), 0.0
        )


def next_row(s, north, south_flux, east_face, north_face):
    flux_east = east_face * (pltpu.roll(s, s.shape[0] - 1, 0) - s)
    flux_north = north_face * (north - s)
    s = s + flux_east - pltpu.roll(flux_east, 1, 0) + flux_north - south_flux
    return s, flux_north


def inner_kernel(
    lat_cells, lon_cells, state_ref, west_ref, east_ref, east_face, north_face, *steps
):
    rim = ITERS

    @pl.loop(0, lat_cells)
    def _(r):
        widen(steps[0], r, r, lon_cells, state_ref, west_ref, east_ref)

    for step in range(ITERS):
        old, new = steps[step], steps[step + 1]

        def line(r, south):
            face = rim + r
            new[r], south = next_row(old[r], old[r + 1], south, east_face[face], north_face[face])
            return south

        south = north_face[rim + step] * (old[step + 1] - old[step])
        lax.fori_loop(step + 1, lat_cells - 1 - step, line, south)


def outer_kernel(lat_cells, lon_cells, mate_ref, next_ref, east_face, north_face, *refs):
    rim = ITERS
    steps = refs[: ITERS + 1]
    out_hbm, low_rows, high_rows, out_ref, sems = refs[ITERS + 1 :]

    def take(low, high):
        for r in range(rim):
            low_rows[0, r] = low[r]
            high_rows[0, r] = high[r]

    either(mate_ref, next_ref, take)

    def at(step, row):
        if row < step:
            return low_rows[step, row + rim - step]
        if row >= lat_cells - step:
            return high_rows[step, row - lat_cells + step]
        return steps[step][row]

    def write(row, s):
        out_ref[:, row, :] = s[SUB : SUB + lon_cells].T

    copies = []
    for rows, first in ((low_rows, -rim), (high_rows, lat_cells)):
        for step in range(1, ITERS + 1):
            start = first + step if first < 0 else first - step
            below = rim + start - 1
            south = north_face[below] * (at(step - 1, start) - at(step - 1, start - 1))
            for i in range(rim):
                r = start + i
                s, south = next_row(
                    at(step - 1, r), at(step - 1, r + 1), south,
                    east_face[rim + r], north_face[rim + r],
                )
                if step < ITERS:
                    rows[step, i] = s
                else:
                    write(r, s)
        inside = range(rim, SUB) if first < 0 else range(SUB, lat_cells - rim)
        for r in inside:
            write(r, steps[ITERS][r])
        side = 0 if first < 0 else 1
        ready = pl.ds(side * SUB, SUB)
        copies += fetch(
            [(out_ref.at[:, ready, :], out_hbm.at[:, ready, :])], sems.at[pl.ds(side, 1)]
        )
    for copy in copies:
        copy.wait()


def cost(microseconds):
    return pl.CostEstimate(
        flops=0, bytes_accessed=microseconds * 3_000_000, transcendentals=0
    )


def params(limit):
    return pltpu.CompilerParams(vmem_limit_bytes=limit)


def on_device(obs_rows, obs_tile, obs_cell, land_sea, zonal_rate, meridional_rate):
    count_x = lax.axis_size("gx")
    count_y = lax.axis_size("gy")
    devices = count_x * count_y
    owned, row_width = obs_rows.shape
    cap = 2 * owned // devices
    levels, lat_cells, lon_cells = land_sea.shape
    cells = lat_cells * lon_cells
    variables = row_width // levels
    rim = ITERS
    f32, i32 = jnp.float32, jnp.int32
    groups = owned // LANES
    sent = devices * (cap + 1)

    packed = pl.pallas_call(
        functools.partial(pack_kernel, cap, cells),
        out_shape=jax.ShapeDtypeStruct((sent, LANES), f32),
        in_specs=[HBM] * 3,
        out_specs=HBM,
        scratch_shapes=[
            pltpu.VMEM((groups, LANES), i32),
            pltpu.VMEM((groups, LANES), i32),
            pltpu.VMEM((owned, LANES), f32),
            pltpu.VMEM((sent, LANES), f32),
            pltpu.VMEM((groups, LANES), i32),
            pltpu.SMEM((groups, LANES), i32),
            pltpu.SemaphoreType.DMA,
            pltpu.SemaphoreType.DMA((3,)),
            pltpu.SemaphoreType.DMA((OUT_PARTS,)),
        ],
        compiler_params=params(63 << 20),
    )(obs_tile.reshape(groups, LANES), obs_cell.reshape(groups, LANES), obs_rows)
    got = lax.all_to_all(
        packed.reshape(sent, 1, LANES), ("gx", "gy"), split_axis=0, concat_axis=0, tiled=True
    ).reshape(sent, LANES)

    tile_ends = jax.ShapeDtypeStruct((lat_cells * SUB, LANES), f32)
    rates, r_ends = pl.pallas_call(
        rates_kernel,
        out_shape=[jax.ShapeDtypeStruct((cells, LANES), f32), tile_ends],
        in_specs=[HBM] * 3,
        out_specs=[VMEM] * 2,
        scratch_shapes=[
            pltpu.VMEM(land_sea.shape, i32),
            pltpu.VMEM(land_sea.shape, f32),
            pltpu.VMEM(land_sea.shape, f32),
            pltpu.SemaphoreType.DMA((3,)),
        ],
        compiler_params=params(4 << 20),
        cost_estimate=cost(2),
    )(land_sea, zonal_rate, meridional_rate)
    r_west, r_east = to_both(r_ends)
    width = lon_cells + 2 * SUB
    edge = jax.ShapeDtypeStruct((rim, width, LANES), f32)
    to_mate, to_next = pl.pallas_call(
        functools.partial(slabs_kernel, lat_cells, lon_cells),
        out_shape=[edge] * 2,
        in_specs=[VMEM] * 3,
        out_specs=[VMEM] * 2,
        compiler_params=params(1 << 20),
    )(rates, r_west, r_east)
    r_mate = lax.ppermute(to_mate, "gy", pairs("gy", 0))
    r_next = lax.ppermute(to_next, "gy", pairs("gy", 1, False))

    listed = (devices * cap // LANES, LANES)
    cell = pl.pallas_call(
        functools.partial(arrived_kernel, cap),
        out_shape=jax.ShapeDtypeStruct(listed, i32),
        in_specs=[VMEM],
        out_specs=VMEM,
        compiler_params=params(1 << 20),
    )(got)
    s_ends = pl.pallas_call(
        functools.partial(ends_kernel, cap, lat_cells, lon_cells),
        out_shape=tile_ends,
        in_specs=[VMEM] * 3,
        out_specs=VMEM,
        compiler_params=params(2 << 20),
        cost_estimate=cost(1),
    )(got, cell, rates)
    s_west, s_east = to_both(s_ends)
    state = pl.pallas_call(
        functools.partial(land_kernel, cap),
        out_shape=jax.ShapeDtypeStruct((cells, LANES), f32),
        in_specs=[VMEM] * 3,
        out_specs=VMEM,
        scratch_shapes=[pltpu.SMEM(listed, i32), pltpu.SemaphoreType.DMA]
        + [pltpu.VMEM((cells + SUB, LANES), f32)] * ACCS,
        compiler_params=params(8 << 20),
        cost_estimate=cost(7),
    )(got, cell, rates)

    to_mate, to_next = pl.pallas_call(
        functools.partial(slabs_kernel, lat_cells, lon_cells),
        out_shape=[edge] * 2,
        in_specs=[VMEM] * 3 + [pl.BlockSpec(memory_space=pl.ANY)] * 2,
        out_specs=[VMEM] * 2,
        compiler_params=params(1 << 20),
    )(state, s_west, s_east, r_mate, r_next)
    s_next = lax.ppermute(to_next, "gy", pairs("gy", 1, False))
    s_mate = lax.ppermute(to_mate, "gy", pairs("gy", 0))
    wide = (lat_cells + 2 * rim, width, LANES)
    faces = pl.pallas_call(
        functools.partial(faces_kernel, lat_cells, lon_cells, lat_cells * count_y),
        out_shape=[jax.ShapeDtypeStruct(wide, f32)] * 2,
        in_specs=[VMEM] * 5,
        out_specs=[VMEM] * 2,
        scratch_shapes=[pltpu.VMEM(wide, f32)],
        compiler_params=params(4 << 20),
        cost_estimate=cost(2),
    )(rates, r_mate, r_next, r_west, r_east)
    steps = pl.pallas_call(
        functools.partial(inner_kernel, lat_cells, lon_cells),
        out_shape=[jax.ShapeDtypeStruct((lat_cells, width, LANES), f32)] * (ITERS + 1),
        in_specs=[VMEM] * 5,
        out_specs=[VMEM] * (ITERS + 1),
        compiler_params=params(2 << 20),
        cost_estimate=cost(2),
    )(state, s_west, s_east, *faces)
    out_shape = (row_width, lat_cells, lon_cells)
    out = pl.pallas_call(
        functools.partial(outer_kernel, lat_cells, lon_cells),
        out_shape=jax.ShapeDtypeStruct(out_shape, f32),
        in_specs=[VMEM] * (4 + ITERS + 1),
        out_specs=HBM,
        scratch_shapes=[pltpu.VMEM((ITERS, rim, width, LANES), f32)] * 2
        + [pltpu.VMEM(out_shape, f32), pltpu.SemaphoreType.DMA((2,))],
        compiler_params=params(6 << 20),
        cost_estimate=cost(3),
    )(s_mate, s_next, *faces, *steps)
    return out.reshape(variables, levels, lat_cells, lon_cells)


def solution(mesh):
    placed = (
        P(("gx", "gy"), None),
        P(("gx", "gy"), None),
        P(("gx", "gy")),
        P(None, "gy", "gx"),
        P(None, "gy", "gx"),
        P(None, "gy", "gx"),
    )
    return jax.shard_map(
        on_device, mesh=mesh, in_specs=placed, out_specs=P(None, None, "gy", "gx"), check_vma=False
    )
```

```python
import functools

import jax
import jax.numpy as jnp
from jax import lax
from jax.experimental import pallas as pl
from jax.experimental.pallas import tpu as pltpu
from jax.sharding import PartitionSpec as P

ITERS = 4
LANES = 128
SUB = 8
ACCS = 4
OUT_PARTS = 8
VMEM = pl.BlockSpec(memory_space=pltpu.VMEM)
ANY = pl.BlockSpec(memory_space=pl.ANY)
HBM = pl.BlockSpec(memory_space=pltpu.HBM)


def pairs(axis, start, closed=True):
    count = lax.axis_size(axis)
    firsts = range(start, count if closed else count - 1, 2)
    both = [(i, (i + 1) % count) for i in firsts]
    return both + [(b, a) for a, b in both]


def to_both(ends):
    return lax.ppermute(ends, "gx", pairs("gx", 0)), lax.ppermute(ends, "gx", pairs("gx", 1))


def west_east(first, second, west_ref, east_ref):
    even = lax.rem(lax.axis_index("gx"), 2) == 0
    west_ref[...] = jnp.where(even, second[...], first[...])
    east_ref[...] = jnp.where(even, first[...], second[...])


def column_ends(ref, lat_cells, lon_cells):
    first = lax.broadcasted_iota(jnp.int32, (SUB, LANES), 0) < SUB // 2
    return jnp.concatenate(
        [
            jnp.where(
                first,
                ref[pl.ds(r * lon_cells, SUB), :],
                ref[pl.ds((r + 1) * lon_cells - SUB, SUB), :],
            )
            for r in range(lat_cells)
        ],
        axis=0,
    )


def fetch(pairs, sems):
    copies = [pltpu.make_async_copy(a, b, sems.at[i]) for i, (a, b) in enumerate(pairs)]
    for copy in copies:
        copy.start()
    return copies


def rates_kernel(
    land_hbm, zonal_hbm, merid_hbm, out_ref, ends_ref, mate_ref, next_ref,
    land_ref, zonal_ref, merid_ref, sems,
):
    lat_cells, lon_cells = land_ref.shape[1:]
    for copy in fetch(
        [(land_hbm, land_ref), (zonal_hbm, zonal_ref), (merid_hbm, merid_ref)], sems
    ):
        copy.wait()
    for lat in range(lat_cells):
        ocean = land_ref[:, lat, :].astype(jnp.float32)
        both = jnp.concatenate(
            [zonal_ref[:, lat, :] * ocean, merid_ref[:, lat, :] * ocean], axis=0
        )
        out_ref[pl.ds(lat * lon_cells, lon_cells), :] = both.T
    ends_ref[...] = column_ends(out_ref, lat_cells, lon_cells)
    odd = is_odd()
    last = lat_cells - ITERS
    for ref, start in ((mate_ref, jnp.where(odd, 0, last)), (next_ref, jnp.where(odd, last, 0))):
        for r in range(ITERS):
            at = pl.multiple_of((start + r) * lon_cells, lon_cells)
            ref[r] = out_ref[pl.ds(at, lon_cells), :]


def pack_kernel(
    cap, cells, tile_hbm, cell_hbm, rows_hbm, out_hbm,
    tile_ref, cell_ref, rows_ref, out_ref, slot_vmem, slot_smem, sem, sems, out_sems,
):
    copies = fetch([(tile_hbm, tile_ref), (cell_hbm, cell_ref), (rows_hbm, rows_ref)], sems)
    out_ref[...] = jnp.zeros_like(out_ref)
    copies[0].wait()
    copies[1].wait()
    groups = tile_ref.shape[0]
    tiles = out_ref.shape[0] // (cap + 1)
    f32, bf16 = jnp.float32, jnp.bfloat16
    down = lax.broadcasted_iota(jnp.int32, (tiles, LANES), 0)
    earlier = (
        lax.broadcasted_iota(jnp.int32, (LANES, 2 * LANES), 0)
        < lax.broadcasted_iota(jnp.int32, (LANES, 2 * LANES), 1)
    ).astype(bf16)
    place = lax.broadcasted_iota(jnp.int32, (LANES, LANES), 0) % cap
    hits, counts, spots = [], [], []
    for g in range(groups):
        hits.append((down == tile_ref[pl.ds(g, 1), :]).astype(f32).astype(bf16))
        counts.append(jnp.dot(hits[g], earlier, preferred_element_type=f32))
    taken = jnp.zeros((tiles, LANES), f32)
    for g in range(groups):
        tile = tile_ref[pl.ds(g, 1), :]
        before = jnp.where(down == tile, counts[g][:, :LANES] + taken, 0.0)
        spots.append(jnp.sum(before, axis=0, keepdims=True).astype(jnp.int32))
        taken += counts[g][:, LANES:]
        slot_vmem[pl.ds(g, 1), :] = tile * (cap + 1) + spots[g]
    copy = pltpu.make_async_copy(slot_vmem, slot_smem, sem)
    copy.start()
    codes = jnp.zeros((tiles, 2 * LANES), f32)
    for g in range(groups):
        here = place == spots[g]
        code = cell_ref[pl.ds(g, 1), :] + 1
        parts = [jnp.where(here, part.astype(f32), 0.0) for part in (code >> 6, code & 63)]
        codes += lax.dot_general(
            hits[g], jnp.concatenate(parts, axis=0).astype(bf16), (((1,), (1,)), ((), ())),
            preferred_element_type=f32,
        )
    code = codes[:, :LANES] * 64.0 + codes[:, LANES:]
    out_ref[pl.ds(cap, tiles, stride=cap + 1), :] = jnp.where(
        code == 0.0, jnp.float32(cells), code - 1.0
    )
    copies[2].wait()
    copy.wait()

    @pl.loop(0, groups)
    def _(g):
        base = pl.multiple_of(g * LANES, LANES)
        for u in range(LANES):
            out_ref[pl.ds(slot_smem[g, u], 1), :] = rows_ref[pl.ds(base + u, 1), :]

    part = out_ref.shape[0] // OUT_PARTS
    spans = [pl.ds(i * part, part) for i in range(OUT_PARTS)]
    for copy in fetch([(out_ref.at[at], out_hbm.at[at]) for at in spans], out_sems):
        copy.wait()


def widen(dest, row, lat, lon_cells, main_ref, west_ref, east_ref):
    at = pl.multiple_of(lat * SUB, SUB)
    dest[row, pl.ds(0, SUB), :] = west_ref[pl.ds(at, SUB), :]
    dest[row, pl.ds(SUB + lon_cells, SUB), :] = east_ref[pl.ds(at, SUB), :]
    at = pl.multiple_of(lat * lon_cells, lon_cells)
    dest[row, pl.ds(SUB, lon_cells), :] = main_ref[pl.ds(at, lon_cells), :]


def slab(dest, north, lat_cells, lon_cells, main_ref, west_ref, east_ref):
    start = jnp.where(north, lat_cells - ITERS, 0)
    for r in range(ITERS):
        widen(dest, r, start + r, lon_cells, main_ref, west_ref, east_ref)


def slabs_kernel(
    lat_cells, lon_cells, main_ref, first_ref, second_ref, mate_ref, next_ref, west_ref, east_ref
):
    west_east(first_ref, second_ref, west_ref, east_ref)
    odd = is_odd()
    slab(next_ref, odd, lat_cells, lon_cells, main_ref, west_ref, east_ref)
    slab(mate_ref, jnp.logical_not(odd), lat_cells, lon_cells, main_ref, west_ref, east_ref)


def arrived_kernel(cap, got_ref, cell_ref):
    block = cap + 1
    sources = got_ref.shape[0] // block
    per = LANES // cap
    lane = lax.broadcasted_iota(jnp.int32, (sources // per, LANES), 1)
    found = jnp.zeros((sources // per, LANES), jnp.float32)
    for j in range(per):
        part = got_ref[pl.ds(block * j + cap, sources // per, stride=block * per), :]
        found = jnp.where(lane // cap == j, part, found)
    cell_ref[...] = found.astype(jnp.int32)


def ends_kernel(
    cap, lat_cells, lon_cells, got_ref, cell_ref, rates_ref, next_any, mate_any, *refs
):
    out_ref, rim_ref, sems = refs[-3:]
    sides = [pl.ds(0, SUB), pl.ds(lon_cells - SUB, SUB)]

    def tiles(i, ref):
        return [
            (ref.at[:, side, :], rim_ref.at[i, :, pl.ds(k * SUB, SUB), :])
            for k, side in enumerate(sides)
        ]

    def start(low, high):
        for i, ref in enumerate((low, high)):
            fetch(tiles(i, ref), sems.at[pl.ds(2 * i, 2)])

    either(mate_any, next_any, start)
    f32, bf16 = jnp.float32, jnp.bfloat16
    block = cap + 1
    per = LANES // cap
    ends = lat_cells * SUB
    place = lax.broadcasted_iota(jnp.int32, (ends, LANES), 0)
    column = place % SUB
    column = jnp.where(column < SUB // 2, column, column + lon_cells - SUB)
    place = place // SUB * lon_cells + column
    total = jnp.zeros((ends, LANES), f32)
    for m in range(cell_ref.shape[0]):
        hit = (place == cell_ref[pl.ds(m, 1), :]).astype(f32).astype(bf16)
        left = jnp.concatenate(
            [got_ref[pl.ds((m * per + j) * block, cap), :] for j in range(per)], axis=0
        )
        for piece in range(3):
            part = left.astype(bf16)
            total += jnp.dot(hit, part, preferred_element_type=f32)
            if piece < 2:
                left = left - part.astype(f32)
    ocean = column_ends(rates_ref, lat_cells, lon_cells) > 0.0
    out_ref[pl.ds(0, ends), :] = jnp.where(ocean, total, 0.0)

    first = lax.broadcasted_iota(jnp.int32, (SUB, LANES), 0) < SUB // 2
    for i in range(2):
        for k, (source, target) in enumerate(tiles(i, mate_any)):
            pltpu.make_async_copy(source, target, sems.at[2 * i + k]).wait()
        for r in range(ITERS):
            out_ref[pl.ds(ends + (i * ITERS + r) * SUB, SUB), :] = jnp.where(
                first, rim_ref[i, r, pl.ds(0, SUB), :], rim_ref[i, r, pl.ds(SUB, SUB), :]
            )


def land_kernel(cap, got_ref, cell_ref, rates_ref, out_ref, cell_smem, sem, *accs):
    block = cap + 1
    per = LANES // cap
    copy = pltpu.make_async_copy(cell_ref, cell_smem, sem)
    copy.start()
    for acc in accs:
        acc[...] = jnp.zeros_like(acc)
    copy.wait()

    @pl.loop(0, cell_ref.shape[0])
    def _(m):
        base = m * (block * per)
        for j in range(per):
            for p in range(cap):
                acc = accs[p % len(accs)]
                at = pl.ds(cell_smem[m, j * cap + p], 1)
                acc[at, :] += got_ref[pl.ds(base + j * block + p, 1), :]

    step = 64

    @pl.loop(0, out_ref.shape[0] // step)
    def _(i):
        at = pl.ds(pl.multiple_of(i * step, step), step)
        total = accs[0][at, :]
        for acc in accs[1:]:
            total += acc[at, :]
        out_ref[at, :] = jnp.where(rates_ref[at, :] > 0.0, total, 0.0)


def is_odd():
    return lax.rem(lax.axis_index("gy"), 2) == 1


def either(from_mate, from_next, use):
    odd = is_odd()

    @pl.when(odd)
    def _():
        use(from_mate, from_next)

    @pl.when(jnp.logical_not(odd))
    def _():
        use(from_next, from_mate)


def faces_kernel(
    lat_cells, lon_cells, total_rows, rates_ref, next_any, mate_any, first_any, second_any,
    west_ends, east_ends, east_face, north_face, wide, west_ref, east_ref, pair_ref, sems,
):
    rim = ITERS
    rows = lat_cells + 2 * rim
    width = lon_cells + 2 * SUB
    main = pl.ds(SUB, lon_cells)
    outer = [wide.at[pl.ds(0, rim), main, :], wide.at[pl.ds(rim + lat_cells, rim), main, :]]
    ends = fetch([(first_any, pair_ref.at[0]), (second_any, pair_ref.at[1])], sems.at[pl.ds(0, 2)])

    def start(low, high):
        fetch([(low, outer[0]), (high, outer[1])], sems.at[pl.ds(2, 2)])

    either(mate_any, next_any, start)
    for r in range(rim):
        for i, row in enumerate((r, rim + lat_cells + r)):
            at = pl.ds((lat_cells + i * rim + r) * SUB, SUB)
            wide[row, pl.ds(0, SUB), :] = west_ends[at, :]
            wide[row, pl.ds(SUB + lon_cells, SUB), :] = east_ends[at, :]
    for copy in ends:
        copy.wait()
    west_east(pair_ref.at[0], pair_ref.at[1], west_ref, east_ref)

    @pl.loop(0, lat_cells)
    def _(r):
        widen(wide, rim + r, r, lon_cells, rates_ref, west_ref, east_ref)

    for i in range(2):
        pltpu.make_async_copy(mate_any, outer[i], sems.at[2 + i]).wait()
    half = LANES // 2
    zonal_lane = lax.broadcasted_iota(jnp.int32, (width, LANES), 1) < half

    @pl.loop(0, rows - 1)
    def _(r):
        here = wide[r]
        ocean_east = pltpu.roll(here, width - 1, 0) > 0.0
        ocean_north = wide[r + 1] > 0.0
        swapped = pltpu.roll(here, half, 1)
        row = lax.rem(lax.axis_index("gy") * lat_cells + r - rim + total_rows, total_rows)
        east_face[r] = jnp.where(ocean_east, jnp.where(zonal_lane, here, swapped), 0.0)
        north_face[r] = jnp.where(
            ocean_north & (row != total_rows - 1), jnp.where(zonal_lane, swapped, here), 0.0
        )


def next_row(s, north, south_flux, east_face, north_face):
    flux_east = east_face * (pltpu.roll(s, s.shape[0] - 1, 0) - s)
    flux_north = north_face * (north - s)
    s = s + flux_east - pltpu.roll(flux_east, 1, 0) + flux_north - south_flux
    return s, flux_north


def inner_kernel(
    lat_cells, lon_cells, state_ref, west_ref, east_ref, east_face, north_face, *steps
):
    rim = ITERS

    @pl.loop(0, lat_cells)
    def _(r):
        widen(steps[0], r, r, lon_cells, state_ref, west_ref, east_ref)

    for step in range(ITERS):
        old, new = steps[step], steps[step + 1]

        def line(r, south):
            face = rim + r
            new[r], south = next_row(old[r], old[r + 1], south, east_face[face], north_face[face])
            return south

        south = north_face[rim + step] * (old[step + 1] - old[step])
        lax.fori_loop(step + 1, lat_cells - 1 - step, line, south)


def outer_kernel(lat_cells, lon_cells, next_ref, mate_ref, east_face, north_face, *refs):
    rim = ITERS
    steps = refs[: ITERS + 1]
    out_hbm, low_rows, high_rows, out_ref, sems = refs[ITERS + 1 :]

    def take(low, high):
        for r in range(rim):
            low_rows[0, r] = low[r]
            high_rows[0, r] = high[r]

    either(mate_ref, next_ref, take)

    def at(step, row):
        if row < step:
            return low_rows[step, row + rim - step]
        if row >= lat_cells - step:
            return high_rows[step, row - lat_cells + step]
        return steps[step][row]

    def write(row, s):
        out_ref[:, row, :] = s[SUB : SUB + lon_cells].T

    copies = []
    for rows, first in ((low_rows, -rim), (high_rows, lat_cells)):
        for step in range(1, ITERS + 1):
            start = first + step if first < 0 else first - step
            below = rim + start - 1
            south = north_face[below] * (at(step - 1, start) - at(step - 1, start - 1))
            for i in range(rim):
                r = start + i
                s, south = next_row(
                    at(step - 1, r), at(step - 1, r + 1), south,
                    east_face[rim + r], north_face[rim + r],
                )
                if step < ITERS:
                    rows[step, i] = s
                else:
                    write(r, s)
        inside = range(rim, SUB) if first < 0 else range(SUB, lat_cells - rim)
        for r in inside:
            write(r, steps[ITERS][r])
        side = 0 if first < 0 else 1
        ready = pl.ds(side * SUB, SUB)
        copies += fetch(
            [(out_ref.at[:, ready, :], out_hbm.at[:, ready, :])], sems.at[pl.ds(side, 1)]
        )
    for copy in copies:
        copy.wait()


def cost(microseconds):
    return pl.CostEstimate(
        flops=0, bytes_accessed=microseconds * 3_000_000, transcendentals=0
    )


def params(limit):
    return pltpu.CompilerParams(vmem_limit_bytes=limit)


def on_device(obs_rows, obs_tile, obs_cell, land_sea, zonal_rate, meridional_rate):
    count_x = lax.axis_size("gx")
    count_y = lax.axis_size("gy")
    devices = count_x * count_y
    owned, row_width = obs_rows.shape
    cap = 2 * owned // devices
    levels, lat_cells, lon_cells = land_sea.shape
    cells = lat_cells * lon_cells
    variables = row_width // levels
    rim = ITERS
    f32, i32 = jnp.float32, jnp.int32
    groups = owned // LANES
    sent = devices * (cap + 1)

    packed = pl.pallas_call(
        functools.partial(pack_kernel, cap, cells),
        out_shape=jax.ShapeDtypeStruct((sent, LANES), f32),
        in_specs=[HBM] * 3,
        out_specs=HBM,
        scratch_shapes=[
            pltpu.VMEM((groups, LANES), i32),
            pltpu.VMEM((groups, LANES), i32),
            pltpu.VMEM((owned, LANES), f32),
            pltpu.VMEM((sent, LANES), f32),
            pltpu.VMEM((groups, LANES), i32),
            pltpu.SMEM((groups, LANES), i32),
            pltpu.SemaphoreType.DMA,
            pltpu.SemaphoreType.DMA((3,)),
            pltpu.SemaphoreType.DMA((OUT_PARTS,)),
        ],
        compiler_params=params(63 << 20),
    )(obs_tile.reshape(groups, LANES), obs_cell.reshape(groups, LANES), obs_rows)
    got = lax.all_to_all(
        packed.reshape(sent, 1, LANES), ("gx", "gy"), split_axis=0, concat_axis=0, tiled=True
    ).reshape(sent, LANES)

    tile_ends = jax.ShapeDtypeStruct((lat_cells * SUB, LANES), f32)
    flat = jax.ShapeDtypeStruct((rim, lon_cells, LANES), f32)
    rates, r_ends, to_mate, to_next = pl.pallas_call(
        rates_kernel,
        out_shape=[jax.ShapeDtypeStruct((cells, LANES), f32), tile_ends, flat, flat],
        in_specs=[HBM] * 3,
        out_specs=[VMEM] * 4,
        scratch_shapes=[
            pltpu.VMEM(land_sea.shape, i32),
            pltpu.VMEM(land_sea.shape, f32),
            pltpu.VMEM(land_sea.shape, f32),
            pltpu.SemaphoreType.DMA((3,)),
        ],
        compiler_params=params(4 << 20),
        cost_estimate=cost(2),
    )(land_sea, zonal_rate, meridional_rate)
    r_first, r_second = to_both(r_ends)
    width = lon_cells + 2 * SUB
    edge = jax.ShapeDtypeStruct((rim, width, LANES), f32)
    r_mate = lax.ppermute(to_mate, "gy", pairs("gy", 0))
    r_next = lax.ppermute(to_next, "gy", pairs("gy", 1, False))

    listed = (devices * cap // LANES, LANES)
    cell = pl.pallas_call(
        functools.partial(arrived_kernel, cap),
        out_shape=jax.ShapeDtypeStruct(listed, i32),
        in_specs=[VMEM],
        out_specs=VMEM,
        compiler_params=params(1 << 20),
    )(got)
    s_ends = pl.pallas_call(
        functools.partial(ends_kernel, cap, lat_cells, lon_cells),
        out_shape=jax.ShapeDtypeStruct(((lat_cells + 2 * rim) * SUB, LANES), f32),
        in_specs=[VMEM] * 3 + [ANY] * 4,
        out_specs=VMEM,
        scratch_shapes=[
            pltpu.VMEM((2, rim, 2 * SUB, LANES), f32),
            pltpu.SemaphoreType.DMA((4,)),
        ],
        compiler_params=params(2 << 20),
        cost_estimate=cost(1),
    )(got, cell, rates, r_next, r_mate, r_first, r_second)
    s_first, s_second = to_both(s_ends)
    state = pl.pallas_call(
        functools.partial(land_kernel, cap),
        out_shape=jax.ShapeDtypeStruct((cells, LANES), f32),
        in_specs=[VMEM] * 3,
        out_specs=VMEM,
        scratch_shapes=[pltpu.SMEM(listed, i32), pltpu.SemaphoreType.DMA]
        + [pltpu.VMEM((cells + SUB, LANES), f32)] * ACCS,
        compiler_params=params(8 << 20),
        cost_estimate=cost(7),
    )(got, cell, rates)

    to_mate, to_next, s_west, s_east = pl.pallas_call(
        functools.partial(slabs_kernel, lat_cells, lon_cells),
        out_shape=[edge] * 2 + [jax.ShapeDtypeStruct(s_ends.shape, f32)] * 2,
        in_specs=[VMEM] * 3,
        out_specs=[VMEM] * 4,
        compiler_params=params(1 << 20),
    )(state, s_first, s_second)
    s_next = lax.ppermute(to_next, "gy", pairs("gy", 1, False))
    s_mate = lax.ppermute(to_mate, "gy", pairs("gy", 0))
    wide = (lat_cells + 2 * rim, width, LANES)
    faces = pl.pallas_call(
        functools.partial(faces_kernel, lat_cells, lon_cells, lat_cells * count_y),
        out_shape=[jax.ShapeDtypeStruct(wide, f32)] * 2,
        in_specs=[VMEM] + [ANY] * 4 + [VMEM] * 2,
        out_specs=[VMEM] * 2,
        scratch_shapes=[
            pltpu.VMEM(wide, f32),
            pltpu.VMEM(tile_ends.shape, f32),
            pltpu.VMEM(tile_ends.shape, f32),
            pltpu.VMEM((2, *tile_ends.shape), f32),
            pltpu.SemaphoreType.DMA((4,)),
        ],
        compiler_params=params(4 << 20),
        cost_estimate=cost(2),
    )(rates, r_next, r_mate, r_first, r_second, s_west, s_east)
    steps = pl.pallas_call(
        functools.partial(inner_kernel, lat_cells, lon_cells),
        out_shape=[jax.ShapeDtypeStruct((lat_cells, width, LANES), f32)] * (ITERS + 1),
        in_specs=[VMEM] * 5,
        out_specs=[VMEM] * (ITERS + 1),
        compiler_params=params(2 << 20),
        cost_estimate=cost(2),
    )(state, s_west, s_east, *faces)
    out_shape = (row_width, lat_cells, lon_cells)
    out = pl.pallas_call(
        functools.partial(outer_kernel, lat_cells, lon_cells),
        out_shape=jax.ShapeDtypeStruct(out_shape, f32),
        in_specs=[VMEM] * (4 + ITERS + 1),
        out_specs=HBM,
        scratch_shapes=[pltpu.VMEM((ITERS, rim, width, LANES), f32)] * 2
        + [pltpu.VMEM(out_shape, f32), pltpu.SemaphoreType.DMA((2,))],
        compiler_params=params(6 << 20),
        cost_estimate=cost(3),
    )(s_next, s_mate, *faces, *steps)
    return out.reshape(variables, levels, lat_cells, lon_cells)


def solution(mesh):
    placed = (
        P(("gx", "gy"), None),
        P(("gx", "gy"), None),
        P(("gx", "gy")),
        P(None, "gy", "gx"),
        P(None, "gy", "gx"),
        P(None, "gy", "gx"),
    )
    return jax.shard_map(
        on_device, mesh=mesh, in_specs=placed, out_specs=P(None, None, "gy", "gx"), check_vma=False
    )
```

```python
import functools

import jax
import jax.numpy as jnp
from jax import lax
from jax.experimental import pallas as pl
from jax.experimental.pallas import tpu as pltpu
from jax.sharding import PartitionSpec as P

ITERS = 4
LANES = 128
SUB = 8
ACCS = 8
OUT_PARTS = 8
VMEM = pl.BlockSpec(memory_space=pltpu.VMEM)
ANY = pl.BlockSpec(memory_space=pl.ANY)
HBM = pl.BlockSpec(memory_space=pltpu.HBM)


def pairs(axis, start, closed=True):
    count = lax.axis_size(axis)
    firsts = range(start, count if closed else count - 1, 2)
    both = [(i, (i + 1) % count) for i in firsts]
    return both + [(b, a) for a, b in both]


def to_both(ends):
    return lax.ppermute(ends, "gx", pairs("gx", 0)), lax.ppermute(ends, "gx", pairs("gx", 1))


def west_east(first, second, west_ref, east_ref):
    even = lax.rem(lax.axis_index("gx"), 2) == 0
    west_ref[...] = jnp.where(even, second[...], first[...])
    east_ref[...] = jnp.where(even, first[...], second[...])


def column_ends(ref, lat_cells, lon_cells):
    first = lax.broadcasted_iota(jnp.int32, (SUB, LANES), 0) < SUB // 2
    return jnp.concatenate(
        [
            jnp.where(
                first,
                ref[pl.ds(r * lon_cells, SUB), :],
                ref[pl.ds((r + 1) * lon_cells - SUB, SUB), :],
            )
            for r in range(lat_cells)
        ],
        axis=0,
    )


def fetch(pairs, sems):
    copies = [pltpu.make_async_copy(a, b, sems.at[i]) for i, (a, b) in enumerate(pairs)]
    for copy in copies:
        copy.start()
    return copies


def rates_kernel(
    land_hbm, zonal_hbm, merid_hbm, out_ref, ends_ref, mate_ref, next_ref,
    land_ref, zonal_ref, merid_ref, sems,
):
    lat_cells, lon_cells = land_ref.shape[1:]
    for copy in fetch(
        [(land_hbm, land_ref), (zonal_hbm, zonal_ref), (merid_hbm, merid_ref)], sems
    ):
        copy.wait()
    for lat in range(lat_cells):
        ocean = land_ref[:, lat, :].astype(jnp.float32)
        both = jnp.concatenate(
            [zonal_ref[:, lat, :] * ocean, merid_ref[:, lat, :] * ocean], axis=0
        )
        out_ref[pl.ds(lat * lon_cells, lon_cells), :] = both.T
    ends_ref[...] = column_ends(out_ref, lat_cells, lon_cells)
    odd = is_odd()
    last = lat_cells - ITERS
    for ref, start in ((mate_ref, jnp.where(odd, 0, last)), (next_ref, jnp.where(odd, last, 0))):
        for r in range(ITERS):
            at = pl.multiple_of((start + r) * lon_cells, lon_cells)
            ref[r] = out_ref[pl.ds(at, lon_cells), :]


def pack_kernel(
    cap, cells, tile_hbm, cell_hbm, rows_hbm, out_hbm,
    tile_ref, cell_ref, rows_ref, out_ref, slot_vmem, slot_smem, sem, sems, out_sems,
):
    copies = fetch([(tile_hbm, tile_ref), (cell_hbm, cell_ref), (rows_hbm, rows_ref)], sems)
    out_ref[...] = jnp.zeros_like(out_ref)
    copies[0].wait()
    copies[1].wait()
    groups = tile_ref.shape[0]
    tiles = out_ref.shape[0] // (cap + 1)
    f32, bf16 = jnp.float32, jnp.bfloat16
    down = lax.broadcasted_iota(jnp.int32, (tiles, LANES), 0)
    earlier = (
        lax.broadcasted_iota(jnp.int32, (LANES, 2 * LANES), 0)
        < lax.broadcasted_iota(jnp.int32, (LANES, 2 * LANES), 1)
    ).astype(bf16)
    place = lax.broadcasted_iota(jnp.int32, (LANES, LANES), 0) % cap
    hits, counts, spots = [], [], []
    for g in range(groups):
        hits.append((down == tile_ref[pl.ds(g, 1), :]).astype(f32).astype(bf16))
        counts.append(jnp.dot(hits[g], earlier, preferred_element_type=f32))
    taken = jnp.zeros((tiles, LANES), f32)
    for g in range(groups):
        tile = tile_ref[pl.ds(g, 1), :]
        before = jnp.where(down == tile, counts[g][:, :LANES] + taken, 0.0)
        spots.append(jnp.sum(before, axis=0, keepdims=True).astype(jnp.int32))
        taken += counts[g][:, LANES:]
        slot_vmem[pl.ds(g, 1), :] = tile * (cap + 1) + spots[g]
    copy = pltpu.make_async_copy(slot_vmem, slot_smem, sem)
    copy.start()
    codes = jnp.zeros((tiles, 2 * LANES), f32)
    for g in range(groups):
        here = place == spots[g]
        code = cell_ref[pl.ds(g, 1), :] + 1
        parts = [jnp.where(here, part.astype(f32), 0.0) for part in (code >> 6, code & 63)]
        codes += lax.dot_general(
            hits[g], jnp.concatenate(parts, axis=0).astype(bf16), (((1,), (1,)), ((), ())),
            preferred_element_type=f32,
        )
    code = codes[:, :LANES] * 64.0 + codes[:, LANES:]
    out_ref[pl.ds(cap, tiles, stride=cap + 1), :] = jnp.where(
        code == 0.0, jnp.float32(cells), code - 1.0
    )
    copies[2].wait()
    copy.wait()

    @pl.loop(0, groups)
    def _(g):
        base = pl.multiple_of(g * LANES, LANES)
        for u in range(LANES):
            out_ref[pl.ds(slot_smem[g, u], 1), :] = rows_ref[pl.ds(base + u, 1), :]

    part = out_ref.shape[0] // OUT_PARTS
    spans = [pl.ds(i * part, part) for i in range(OUT_PARTS)]
    for copy in fetch([(out_ref.at[at], out_hbm.at[at]) for at in spans], out_sems):
        copy.wait()


def widen(dest, row, lat, lon_cells, main_ref, west_ref, east_ref):
    at = pl.multiple_of(lat * SUB, SUB)
    dest[row, pl.ds(0, SUB), :] = west_ref[pl.ds(at, SUB), :]
    dest[row, pl.ds(SUB + lon_cells, SUB), :] = east_ref[pl.ds(at, SUB), :]
    at = pl.multiple_of(lat * lon_cells, lon_cells)
    dest[row, pl.ds(SUB, lon_cells), :] = main_ref[pl.ds(at, lon_cells), :]


def slab(dest, north, lat_cells, lon_cells, main_ref, west_ref, east_ref):
    start = jnp.where(north, lat_cells - ITERS, 0)
    for r in range(ITERS):
        widen(dest, r, start + r, lon_cells, main_ref, west_ref, east_ref)


def slabs_kernel(
    lat_cells, lon_cells, main_ref, first_ref, second_ref, mate_ref, next_ref, west_ref, east_ref
):
    west_east(first_ref, second_ref, west_ref, east_ref)
    odd = is_odd()
    slab(next_ref, odd, lat_cells, lon_cells, main_ref, west_ref, east_ref)
    slab(mate_ref, jnp.logical_not(odd), lat_cells, lon_cells, main_ref, west_ref, east_ref)


def arrived_kernel(cap, got_ref, cell_ref):
    block = cap + 1
    sources = got_ref.shape[0] // block
    per = LANES // cap
    lane = lax.broadcasted_iota(jnp.int32, (sources // per, LANES), 1)
    found = jnp.zeros((sources // per, LANES), jnp.float32)
    for j in range(per):
        part = got_ref[pl.ds(block * j + cap, sources // per, stride=block * per), :]
        found = jnp.where(lane // cap == j, part, found)
    cell_ref[...] = found.astype(jnp.int32)


def ends_kernel(
    cap, lat_cells, lon_cells, got_ref, cell_ref, rates_ref, next_any, mate_any, *refs
):
    out_ref, rim_ref, sems = refs[-3:]
    sides = [pl.ds(0, SUB), pl.ds(lon_cells - SUB, SUB)]

    def tiles(i, ref):
        return [
            (ref.at[:, side, :], rim_ref.at[i, :, pl.ds(k * SUB, SUB), :])
            for k, side in enumerate(sides)
        ]

    def start(low, high):
        for i, ref in enumerate((low, high)):
            fetch(tiles(i, ref), sems.at[pl.ds(2 * i, 2)])

    either(mate_any, next_any, start)
    f32, bf16 = jnp.float32, jnp.bfloat16
    block = cap + 1
    per = LANES // cap
    ends = lat_cells * SUB
    place = lax.broadcasted_iota(jnp.int32, (ends, LANES), 0)
    column = place % SUB
    column = jnp.where(column < SUB // 2, column, column + lon_cells - SUB)
    place = place // SUB * lon_cells + column
    total = jnp.zeros((ends, LANES), f32)
    for m in range(cell_ref.shape[0]):
        hit = (place == cell_ref[pl.ds(m, 1), :]).astype(f32).astype(bf16)
        left = jnp.concatenate(
            [got_ref[pl.ds((m * per + j) * block, cap), :] for j in range(per)], axis=0
        )
        for piece in range(3):
            part = left.astype(bf16)
            total += jnp.dot(hit, part, preferred_element_type=f32)
            if piece < 2:
                left = left - part.astype(f32)
    ocean = column_ends(rates_ref, lat_cells, lon_cells) > 0.0
    out_ref[pl.ds(0, ends), :] = jnp.where(ocean, total, 0.0)

    first = lax.broadcasted_iota(jnp.int32, (SUB, LANES), 0) < SUB // 2
    for i in range(2):
        for k, (source, target) in enumerate(tiles(i, mate_any)):
            pltpu.make_async_copy(source, target, sems.at[2 * i + k]).wait()
        for r in range(ITERS):
            out_ref[pl.ds(ends + (i * ITERS + r) * SUB, SUB), :] = jnp.where(
                first, rim_ref[i, r, pl.ds(0, SUB), :], rim_ref[i, r, pl.ds(SUB, SUB), :]
            )


def land_kernel(cap, got_ref, cell_ref, rates_ref, out_ref, cell_smem, sem, *accs):
    block = cap + 1
    per = LANES // cap
    copy = pltpu.make_async_copy(cell_ref, cell_smem, sem)
    copy.start()
    for acc in accs:
        acc[...] = jnp.zeros_like(acc)
    copy.wait()

    @pl.loop(0, cell_ref.shape[0])
    def _(m):
        base = m * (block * per)
        for j in range(per):
            for p in range(cap):
                acc = accs[(j * cap + p) % len(accs)]
                at = pl.ds(cell_smem[m, j * cap + p], 1)
                acc[at, :] += got_ref[pl.ds(base + j * block + p, 1), :]

    step = 64

    @pl.loop(0, out_ref.shape[0] // step)
    def _(i):
        at = pl.ds(pl.multiple_of(i * step, step), step)
        total = accs[0][at, :]
        for acc in accs[1:]:
            total += acc[at, :]
        out_ref[at, :] = jnp.where(rates_ref[at, :] > 0.0, total, 0.0)


def is_odd():
    return lax.rem(lax.axis_index("gy"), 2) == 1


def either(from_mate, from_next, use):
    odd = is_odd()

    @pl.when(odd)
    def _():
        use(from_mate, from_next)

    @pl.when(jnp.logical_not(odd))
    def _():
        use(from_next, from_mate)


def faces_kernel(
    lat_cells, lon_cells, total_rows, rates_ref, next_any, mate_any, first_any, second_any,
    west_ends, east_ends, east_face, north_face, wide, west_ref, east_ref, pair_ref, sems,
):
    rim = ITERS
    rows = lat_cells + 2 * rim
    width = lon_cells + 2 * SUB
    main = pl.ds(SUB, lon_cells)
    outer = [wide.at[pl.ds(0, rim), main, :], wide.at[pl.ds(rim + lat_cells, rim), main, :]]
    ends = fetch([(first_any, pair_ref.at[0]), (second_any, pair_ref.at[1])], sems.at[pl.ds(0, 2)])

    def start(low, high):
        fetch([(low, outer[0]), (high, outer[1])], sems.at[pl.ds(2, 2)])

    either(mate_any, next_any, start)
    for r in range(rim):
        for i, row in enumerate((r, rim + lat_cells + r)):
            at = pl.ds((lat_cells + i * rim + r) * SUB, SUB)
            wide[row, pl.ds(0, SUB), :] = west_ends[at, :]
            wide[row, pl.ds(SUB + lon_cells, SUB), :] = east_ends[at, :]
    for copy in ends:
        copy.wait()
    west_east(pair_ref.at[0], pair_ref.at[1], west_ref, east_ref)

    @pl.loop(0, lat_cells)
    def _(r):
        widen(wide, rim + r, r, lon_cells, rates_ref, west_ref, east_ref)

    for i in range(2):
        pltpu.make_async_copy(mate_any, outer[i], sems.at[2 + i]).wait()
    half = LANES // 2
    zonal_lane = lax.broadcasted_iota(jnp.int32, (width, LANES), 1) < half

    @pl.loop(0, rows - 1)
    def _(r):
        here = wide[r]
        ocean_east = pltpu.roll(here, width - 1, 0) > 0.0
        ocean_north = wide[r + 1] > 0.0
        swapped = pltpu.roll(here, half, 1)
        row = lax.rem(lax.axis_index("gy") * lat_cells + r - rim + total_rows, total_rows)
        east_face[r] = jnp.where(ocean_east, jnp.where(zonal_lane, here, swapped), 0.0)
        north_face[r] = jnp.where(
            ocean_north & (row != total_rows - 1), jnp.where(zonal_lane, swapped, here), 0.0
        )


def next_row(s, north, south_flux, east_face, north_face):
    flux_east = east_face * (pltpu.roll(s, s.shape[0] - 1, 0) - s)
    flux_north = north_face * (north - s)
    s = s + flux_east - pltpu.roll(flux_east, 1, 0) + flux_north - south_flux
    return s, flux_north


def inner_kernel(
    lat_cells, lon_cells, state_ref, west_ref, east_ref, east_face, north_face, *steps
):
    rim = ITERS

    @pl.loop(0, lat_cells)
    def _(r):
        widen(steps[0], r, r, lon_cells, state_ref, west_ref, east_ref)

    for step in range(ITERS):
        old, new = steps[step], steps[step + 1]

        def line(r, south):
            face = rim + r
            new[r], south = next_row(old[r], old[r + 1], south, east_face[face], north_face[face])
            return south

        south = north_face[rim + step] * (old[step + 1] - old[step])
        lax.fori_loop(step + 1, lat_cells - 1 - step, line, south)


def outer_kernel(lat_cells, lon_cells, next_ref, mate_ref, east_face, north_face, *refs):
    rim = ITERS
    steps = refs[: ITERS + 1]
    out_hbm, low_rows, high_rows, out_ref, sems = refs[ITERS + 1 :]

    def take(low, high):
        for r in range(rim):
            low_rows[0, r] = low[r]
            high_rows[0, r] = high[r]

    either(mate_ref, next_ref, take)

    def at(step, row):
        if row < step:
            return low_rows[step, row + rim - step]
        if row >= lat_cells - step:
            return high_rows[step, row - lat_cells + step]
        return steps[step][row]

    def write(row, s):
        out_ref[:, row, :] = s[SUB : SUB + lon_cells].T

    copies = []
    for rows, first in ((low_rows, -rim), (high_rows, lat_cells)):
        for step in range(1, ITERS + 1):
            start = first + step if first < 0 else first - step
            below = rim + start - 1
            south = north_face[below] * (at(step - 1, start) - at(step - 1, start - 1))
            for i in range(rim):
                r = start + i
                s, south = next_row(
                    at(step - 1, r), at(step - 1, r + 1), south,
                    east_face[rim + r], north_face[rim + r],
                )
                if step < ITERS:
                    rows[step, i] = s
                else:
                    write(r, s)
        inside = range(rim, SUB) if first < 0 else range(SUB, lat_cells - rim)
        for r in inside:
            write(r, steps[ITERS][r])
        side = 0 if first < 0 else 1
        ready = pl.ds(side * SUB, SUB)
        copies += fetch(
            [(out_ref.at[:, ready, :], out_hbm.at[:, ready, :])], sems.at[pl.ds(side, 1)]
        )
    for copy in copies:
        copy.wait()


def cost(microseconds):
    return pl.CostEstimate(
        flops=0, bytes_accessed=microseconds * 3_000_000, transcendentals=0
    )


def params(limit):
    return pltpu.CompilerParams(vmem_limit_bytes=limit)


def on_device(obs_rows, obs_tile, obs_cell, land_sea, zonal_rate, meridional_rate):
    count_x = lax.axis_size("gx")
    count_y = lax.axis_size("gy")
    devices = count_x * count_y
    owned, row_width = obs_rows.shape
    cap = 2 * owned // devices
    levels, lat_cells, lon_cells = land_sea.shape
    cells = lat_cells * lon_cells
    variables = row_width // levels
    rim = ITERS
    f32, i32 = jnp.float32, jnp.int32
    groups = owned // LANES
    sent = devices * (cap + 1)

    packed = pl.pallas_call(
        functools.partial(pack_kernel, cap, cells),
        out_shape=jax.ShapeDtypeStruct((sent, LANES), f32),
        in_specs=[HBM] * 3,
        out_specs=HBM,
        scratch_shapes=[
            pltpu.VMEM((groups, LANES), i32),
            pltpu.VMEM((groups, LANES), i32),
            pltpu.VMEM((owned, LANES), f32),
            pltpu.VMEM((sent, LANES), f32),
            pltpu.VMEM((groups, LANES), i32),
            pltpu.SMEM((groups, LANES), i32),
            pltpu.SemaphoreType.DMA,
            pltpu.SemaphoreType.DMA((3,)),
            pltpu.SemaphoreType.DMA((OUT_PARTS,)),
        ],
        compiler_params=params(63 << 20),
    )(obs_tile.reshape(groups, LANES), obs_cell.reshape(groups, LANES), obs_rows)
    got = lax.all_to_all(
        packed.reshape(sent, 1, LANES), ("gx", "gy"), split_axis=0, concat_axis=0, tiled=True
    ).reshape(sent, LANES)

    tile_ends = jax.ShapeDtypeStruct((lat_cells * SUB, LANES), f32)
    flat = jax.ShapeDtypeStruct((rim, lon_cells, LANES), f32)
    rates, r_ends, to_mate, to_next = pl.pallas_call(
        rates_kernel,
        out_shape=[jax.ShapeDtypeStruct((cells, LANES), f32), tile_ends, flat, flat],
        in_specs=[HBM] * 3,
        out_specs=[VMEM] * 4,
        scratch_shapes=[
            pltpu.VMEM(land_sea.shape, i32),
            pltpu.VMEM(land_sea.shape, f32),
            pltpu.VMEM(land_sea.shape, f32),
            pltpu.SemaphoreType.DMA((3,)),
        ],
        compiler_params=params(4 << 20),
        cost_estimate=cost(2),
    )(land_sea, zonal_rate, meridional_rate)
    r_first, r_second = to_both(r_ends)
    width = lon_cells + 2 * SUB
    edge = jax.ShapeDtypeStruct((rim, width, LANES), f32)
    r_mate = lax.ppermute(to_mate, "gy", pairs("gy", 0))
    r_next = lax.ppermute(to_next, "gy", pairs("gy", 1, False))

    listed = (devices * cap // LANES, LANES)
    cell = pl.pallas_call(
        functools.partial(arrived_kernel, cap),
        out_shape=jax.ShapeDtypeStruct(listed, i32),
        in_specs=[VMEM],
        out_specs=VMEM,
        compiler_params=params(1 << 20),
    )(got)
    s_ends = pl.pallas_call(
        functools.partial(ends_kernel, cap, lat_cells, lon_cells),
        out_shape=jax.ShapeDtypeStruct(((lat_cells + 2 * rim) * SUB, LANES), f32),
        in_specs=[VMEM] * 3 + [ANY] * 4,
        out_specs=VMEM,
        scratch_shapes=[
            pltpu.VMEM((2, rim, 2 * SUB, LANES), f32),
            pltpu.SemaphoreType.DMA((4,)),
        ],
        compiler_params=params(2 << 20),
        cost_estimate=cost(1),
    )(got, cell, rates, r_next, r_mate, r_first, r_second)
    s_first, s_second = to_both(s_ends)
    state = pl.pallas_call(
        functools.partial(land_kernel, cap),
        out_shape=jax.ShapeDtypeStruct((cells, LANES), f32),
        in_specs=[VMEM] * 3,
        out_specs=VMEM,
        scratch_shapes=[pltpu.SMEM(listed, i32), pltpu.SemaphoreType.DMA]
        + [pltpu.VMEM((cells + SUB, LANES), f32)] * ACCS,
        compiler_params=params(12 << 20),
        cost_estimate=cost(7),
    )(got, cell, rates)

    to_mate, to_next, s_west, s_east = pl.pallas_call(
        functools.partial(slabs_kernel, lat_cells, lon_cells),
        out_shape=[edge] * 2 + [jax.ShapeDtypeStruct(s_ends.shape, f32)] * 2,
        in_specs=[VMEM] * 3,
        out_specs=[VMEM] * 4,
        compiler_params=params(1 << 20),
    )(state, s_first, s_second)
    s_next = lax.ppermute(to_next, "gy", pairs("gy", 1, False))
    s_mate = lax.ppermute(to_mate, "gy", pairs("gy", 0))
    wide = (lat_cells + 2 * rim, width, LANES)
    faces = pl.pallas_call(
        functools.partial(faces_kernel, lat_cells, lon_cells, lat_cells * count_y),
        out_shape=[jax.ShapeDtypeStruct(wide, f32)] * 2,
        in_specs=[VMEM] + [ANY] * 4 + [VMEM] * 2,
        out_specs=[VMEM] * 2,
        scratch_shapes=[
            pltpu.VMEM(wide, f32),
            pltpu.VMEM(tile_ends.shape, f32),
            pltpu.VMEM(tile_ends.shape, f32),
            pltpu.VMEM((2, *tile_ends.shape), f32),
            pltpu.SemaphoreType.DMA((4,)),
        ],
        compiler_params=params(4 << 20),
        cost_estimate=cost(2),
    )(rates, r_next, r_mate, r_first, r_second, s_west, s_east)
    steps = pl.pallas_call(
        functools.partial(inner_kernel, lat_cells, lon_cells),
        out_shape=[jax.ShapeDtypeStruct((lat_cells, width, LANES), f32)] * (ITERS + 1),
        in_specs=[VMEM] * 5,
        out_specs=[VMEM] * (ITERS + 1),
        compiler_params=params(2 << 20),
        cost_estimate=cost(2),
    )(state, s_west, s_east, *faces)
    out_shape = (row_width, lat_cells, lon_cells)
    out = pl.pallas_call(
        functools.partial(outer_kernel, lat_cells, lon_cells),
        out_shape=jax.ShapeDtypeStruct(out_shape, f32),
        in_specs=[VMEM] * (4 + ITERS + 1),
        out_specs=HBM,
        scratch_shapes=[pltpu.VMEM((ITERS, rim, width, LANES), f32)] * 2
        + [pltpu.VMEM(out_shape, f32), pltpu.SemaphoreType.DMA((2,))],
        compiler_params=params(6 << 20),
        cost_estimate=cost(3),
    )(s_next, s_mate, *faces, *steps)
    return out.reshape(variables, levels, lat_cells, lon_cells)


def solution(mesh):
    placed = (
        P(("gx", "gy"), None),
        P(("gx", "gy"), None),
        P(("gx", "gy")),
        P(None, "gy", "gx"),
        P(None, "gy", "gx"),
        P(None, "gy", "gx"),
    )
    return jax.shard_map(
        on_device, mesh=mesh, in_specs=placed, out_specs=P(None, None, "gy", "gx"), check_vma=False
    )
```

```python
import functools

import jax
import jax.numpy as jnp
from jax import lax
from jax.experimental import pallas as pl
from jax.experimental.pallas import tpu as pltpu
from jax.sharding import PartitionSpec as P

ITERS = 4
LANES = 128
SUB = 8
ACCS = 8
OUT_PARTS = 8
VMEM = pl.BlockSpec(memory_space=pltpu.VMEM)
ANY = pl.BlockSpec(memory_space=pl.ANY)
HBM = pl.BlockSpec(memory_space=pltpu.HBM)


def pairs(axis, start, closed=True):
    count = lax.axis_size(axis)
    firsts = range(start, count if closed else count - 1, 2)
    both = [(i, (i + 1) % count) for i in firsts]
    return both + [(b, a) for a, b in both]


def to_both(first, second):
    return lax.ppermute(first, "gx", pairs("gx", 0)), lax.ppermute(second, "gx", pairs("gx", 1))


def even_column():
    return lax.rem(lax.axis_index("gx"), 2) == 0


def west_east(first, second, west_ref, east_ref):
    even = even_column()
    west_ref[...] = jnp.where(even, second[...], first[...])
    east_ref[...] = jnp.where(even, first[...], second[...])


def column_ends(ref, lat_cells, lon_cells):
    first = lax.broadcasted_iota(jnp.int32, (SUB, LANES), 0) < SUB // 2
    return jnp.concatenate(
        [
            jnp.where(
                first,
                ref[pl.ds(r * lon_cells, SUB), :],
                ref[pl.ds((r + 1) * lon_cells - SUB, SUB), :],
            )
            for r in range(lat_cells)
        ],
        axis=0,
    )


def fetch(pairs, sems):
    copies = [pltpu.make_async_copy(a, b, sems.at[i]) for i, (a, b) in enumerate(pairs)]
    for copy in copies:
        copy.start()
    return copies


def rates_kernel(
    land_hbm, zonal_hbm, merid_hbm, out_ref, ends_ref, mate_ref, next_ref,
    land_ref, zonal_ref, merid_ref, sems,
):
    lat_cells, lon_cells = land_ref.shape[1:]
    for copy in fetch(
        [(land_hbm, land_ref), (zonal_hbm, zonal_ref), (merid_hbm, merid_ref)], sems
    ):
        copy.wait()
    for lat in range(lat_cells):
        ocean = land_ref[:, lat, :].astype(jnp.float32)
        both = jnp.concatenate(
            [zonal_ref[:, lat, :] * ocean, merid_ref[:, lat, :] * ocean], axis=0
        )
        out_ref[pl.ds(lat * lon_cells, lon_cells), :] = both.T
    ends_ref[...] = column_ends(out_ref, lat_cells, lon_cells)
    odd = is_odd()
    last = lat_cells - ITERS
    for ref, start in ((mate_ref, jnp.where(odd, 0, last)), (next_ref, jnp.where(odd, last, 0))):
        for r in range(ITERS):
            at = pl.multiple_of((start + r) * lon_cells, lon_cells)
            ref[r] = out_ref[pl.ds(at, lon_cells), :]


def pack_kernel(
    cap, cells, tile_hbm, cell_hbm, rows_hbm, out_hbm,
    tile_ref, cell_ref, rows_ref, out_ref, slot_vmem, slot_smem, sem, sems, out_sems,
):
    copies = fetch([(tile_hbm, tile_ref), (cell_hbm, cell_ref), (rows_hbm, rows_ref)], sems)
    out_ref[...] = jnp.zeros_like(out_ref)
    copies[0].wait()
    copies[1].wait()
    groups = tile_ref.shape[0]
    tiles = out_ref.shape[0] // (cap + 1)
    f32, bf16 = jnp.float32, jnp.bfloat16
    down = lax.broadcasted_iota(jnp.int32, (tiles, LANES), 0)
    earlier = (
        lax.broadcasted_iota(jnp.int32, (LANES, 2 * LANES), 0)
        < lax.broadcasted_iota(jnp.int32, (LANES, 2 * LANES), 1)
    ).astype(bf16)
    place = lax.broadcasted_iota(jnp.int32, (LANES, LANES), 0) % cap
    hits, counts, spots = [], [], []
    for g in range(groups):
        hits.append((down == tile_ref[pl.ds(g, 1), :]).astype(f32).astype(bf16))
        counts.append(jnp.dot(hits[g], earlier, preferred_element_type=f32))
    taken = jnp.zeros((tiles, LANES), f32)
    for g in range(groups):
        tile = tile_ref[pl.ds(g, 1), :]
        before = jnp.where(down == tile, counts[g][:, :LANES] + taken, 0.0)
        spots.append(jnp.sum(before, axis=0, keepdims=True).astype(jnp.int32))
        taken += counts[g][:, LANES:]
        slot_vmem[pl.ds(g, 1), :] = tile * (cap + 1) + spots[g]
    copy = pltpu.make_async_copy(slot_vmem, slot_smem, sem)
    copy.start()
    codes = jnp.zeros((tiles, 2 * LANES), f32)
    for g in range(groups):
        here = place == spots[g]
        code = cell_ref[pl.ds(g, 1), :] + 1
        parts = [jnp.where(here, part.astype(f32), 0.0) for part in (code >> 6, code & 63)]
        codes += lax.dot_general(
            hits[g], jnp.concatenate(parts, axis=0).astype(bf16), (((1,), (1,)), ((), ())),
            preferred_element_type=f32,
        )
    code = codes[:, :LANES] * 64.0 + codes[:, LANES:]
    out_ref[pl.ds(cap, tiles, stride=cap + 1), :] = jnp.where(
        code == 0.0, jnp.float32(cells), code - 1.0
    )
    copies[2].wait()
    copy.wait()

    @pl.loop(0, groups)
    def _(g):
        base = pl.multiple_of(g * LANES, LANES)
        for u in range(LANES):
            out_ref[pl.ds(slot_smem[g, u], 1), :] = rows_ref[pl.ds(base + u, 1), :]

    part = out_ref.shape[0] // OUT_PARTS
    spans = [pl.ds(i * part, part) for i in range(OUT_PARTS)]
    for copy in fetch([(out_ref.at[at], out_hbm.at[at]) for at in spans], out_sems):
        copy.wait()


def widen(dest, row, lat, lon_cells, main_ref, west_ref, east_ref):
    at = pl.multiple_of(lat * SUB, SUB)
    dest[row, pl.ds(0, SUB), :] = west_ref[pl.ds(at, SUB), :]
    dest[row, pl.ds(SUB + lon_cells, SUB), :] = east_ref[pl.ds(at, SUB), :]
    at = pl.multiple_of(lat * lon_cells, lon_cells)
    dest[row, pl.ds(SUB, lon_cells), :] = main_ref[pl.ds(at, lon_cells), :]


def slab(dest, north, lat_cells, lon_cells, main_ref, west_ref, east_ref):
    start = jnp.where(north, lat_cells - ITERS, 0)
    for r in range(ITERS):
        widen(dest, r, start + r, lon_cells, main_ref, west_ref, east_ref)


def slabs_kernel(
    lat_cells, lon_cells, main_ref, first_ref, second_ref, mate_ref, next_ref, west_ref, east_ref
):
    even = even_column()
    for q in range(first_ref.shape[0] // SUB):
        at = pl.ds(q * SUB, SUB)
        first, second = first_ref[at, :], second_ref[at, :]
        west = jnp.where(even, second, first)
        east = jnp.where(even, first, second)
        low, high = (pl.ds((2 * q + i) * SUB, SUB) for i in range(2))
        west_ref[low, :] = pltpu.roll(west, SUB // 2, 0)
        west_ref[high, :] = west
        east_ref[low, :] = east
        east_ref[high, :] = pltpu.roll(east, SUB // 2, 0)
    odd = is_odd()
    slab(next_ref, odd, lat_cells, lon_cells, main_ref, west_ref, east_ref)
    slab(mate_ref, jnp.logical_not(odd), lat_cells, lon_cells, main_ref, west_ref, east_ref)


def arrived_kernel(cap, got_ref, cell_ref):
    block = cap + 1
    sources = got_ref.shape[0] // block
    per = LANES // cap
    lane = lax.broadcasted_iota(jnp.int32, (sources // per, LANES), 1)
    found = jnp.zeros((sources // per, LANES), jnp.float32)
    for j in range(per):
        part = got_ref[pl.ds(block * j + cap, sources // per, stride=block * per), :]
        found = jnp.where(lane // cap == j, part, found)
    cell_ref[...] = found.astype(jnp.int32)


def ends_kernel(
    cap, lat_cells, lon_cells, got_ref, cell_ref, rates_ref, next_any, mate_any, *refs
):
    first_out, second_out, out_ref, rim_ref, sems = refs[-5:]
    sides = [pl.ds(0, SUB), pl.ds(lon_cells - SUB, SUB)]

    def tiles(i, ref):
        return [
            (ref.at[:, side, :], rim_ref.at[i, :, pl.ds(k * SUB, SUB), :])
            for k, side in enumerate(sides)
        ]

    def start(low, high):
        for i, ref in enumerate((low, high)):
            fetch(tiles(i, ref), sems.at[pl.ds(2 * i, 2)])

    either(mate_any, next_any, start)
    f32, bf16 = jnp.float32, jnp.bfloat16
    block = cap + 1
    per = LANES // cap
    ends = lat_cells * SUB
    place = lax.broadcasted_iota(jnp.int32, (ends, LANES), 0)
    column = place % SUB
    column = jnp.where(column < SUB // 2, column, column + lon_cells - SUB)
    place = place // SUB * lon_cells + column
    total = jnp.zeros((ends, LANES), f32)
    for m in range(cell_ref.shape[0]):
        hit = (place == cell_ref[pl.ds(m, 1), :]).astype(f32).astype(bf16)
        left = jnp.concatenate(
            [got_ref[pl.ds((m * per + j) * block, cap), :] for j in range(per)], axis=0
        )
        for piece in range(3):
            part = left.astype(bf16)
            total += jnp.dot(hit, part, preferred_element_type=f32)
            if piece < 2:
                left = left - part.astype(f32)
    ocean = column_ends(rates_ref, lat_cells, lon_cells) > 0.0
    out_ref[pl.ds(0, ends), :] = jnp.where(ocean, total, 0.0)

    first = lax.broadcasted_iota(jnp.int32, (SUB, LANES), 0) < SUB // 2
    for i in range(2):
        for k, (source, target) in enumerate(tiles(i, mate_any)):
            pltpu.make_async_copy(source, target, sems.at[2 * i + k]).wait()
        for r in range(ITERS):
            out_ref[pl.ds(ends + (i * ITERS + r) * SUB, SUB), :] = jnp.where(
                first, rim_ref[i, r, pl.ds(0, SUB), :], rim_ref[i, r, pl.ds(SUB, SUB), :]
            )
    even = even_column()
    for q in range(first_out.shape[0] // SUB):
        a, b = (out_ref[pl.ds((2 * q + i) * SUB, SUB), :] for i in range(2))
        west = jnp.where(first, a, pltpu.roll(b, SUB // 2, 0))
        east = jnp.where(first, pltpu.roll(a, SUB // 2, 0), b)
        at = pl.ds(q * SUB, SUB)
        first_out[at, :] = jnp.where(even, east, west)
        second_out[at, :] = jnp.where(even, west, east)


def land_kernel(cap, got_ref, cell_ref, rates_ref, out_ref, cell_smem, sem, *accs):
    block = cap + 1
    per = LANES // cap
    copy = pltpu.make_async_copy(cell_ref, cell_smem, sem)
    copy.start()
    for acc in accs:
        acc[...] = jnp.zeros_like(acc)
    copy.wait()

    @pl.loop(0, cell_ref.shape[0])
    def _(m):
        base = m * (block * per)
        for j in range(per):
            for p in range(cap):
                acc = accs[(j * cap + p) % len(accs)]
                at = pl.ds(cell_smem[m, j * cap + p], 1)
                acc[at, :] += got_ref[pl.ds(base + j * block + p, 1), :]

    step = 64

    @pl.loop(0, out_ref.shape[0] // step)
    def _(i):
        at = pl.ds(pl.multiple_of(i * step, step), step)
        total = accs[0][at, :]
        for acc in accs[1:]:
            total += acc[at, :]
        out_ref[at, :] = jnp.where(rates_ref[at, :] > 0.0, total, 0.0)


def is_odd():
    return lax.rem(lax.axis_index("gy"), 2) == 1


def either(from_mate, from_next, use):
    odd = is_odd()

    @pl.when(odd)
    def _():
        use(from_mate, from_next)

    @pl.when(jnp.logical_not(odd))
    def _():
        use(from_next, from_mate)


def faces_kernel(
    lat_cells, lon_cells, total_rows, rates_ref, next_any, mate_any, first_any, second_any,
    west_ends, east_ends, east_face, north_face, wide, west_ref, east_ref, pair_ref, sems,
):
    rim = ITERS
    rows = lat_cells + 2 * rim
    width = lon_cells + 2 * SUB
    main = pl.ds(SUB, lon_cells)
    outer = [wide.at[pl.ds(0, rim), main, :], wide.at[pl.ds(rim + lat_cells, rim), main, :]]
    ends = fetch([(first_any, pair_ref.at[0]), (second_any, pair_ref.at[1])], sems.at[pl.ds(0, 2)])

    def start(low, high):
        fetch([(low, outer[0]), (high, outer[1])], sems.at[pl.ds(2, 2)])

    either(mate_any, next_any, start)
    for r in range(rim):
        for i, row in enumerate((r, rim + lat_cells + r)):
            at = pl.ds((lat_cells + i * rim + r) * SUB, SUB)
            wide[row, pl.ds(0, SUB), :] = west_ends[at, :]
            wide[row, pl.ds(SUB + lon_cells, SUB), :] = east_ends[at, :]

    @pl.loop(0, lat_cells)
    def _(r):
        at = pl.multiple_of(r * lon_cells, lon_cells)
        wide[rim + r, main, :] = rates_ref[pl.ds(at, lon_cells), :]

    for copy in ends:
        copy.wait()
    west_east(pair_ref.at[0], pair_ref.at[1], west_ref, east_ref)
    for r in range(lat_cells):
        at = pl.ds(r * SUB, SUB)
        wide[rim + r, pl.ds(0, SUB), :] = west_ref[at, :]
        wide[rim + r, pl.ds(SUB + lon_cells, SUB), :] = east_ref[at, :]

    half = LANES // 2
    zonal_lane = lax.broadcasted_iota(jnp.int32, (width, LANES), 1) < half

    def faces(r):
        here = wide[r]
        ocean_east = pltpu.roll(here, width - 1, 0) > 0.0
        ocean_north = wide[r + 1] > 0.0
        swapped = pltpu.roll(here, half, 1)
        row = lax.rem(lax.axis_index("gy") * lat_cells + r - rim + total_rows, total_rows)
        east_face[r] = jnp.where(ocean_east, jnp.where(zonal_lane, here, swapped), 0.0)
        north_face[r] = jnp.where(
            ocean_north & (row != total_rows - 1), jnp.where(zonal_lane, swapped, here), 0.0
        )

    pl.loop(rim, rim + lat_cells - 1)(faces)
    for i in range(2):
        pltpu.make_async_copy(mate_any, outer[i], sems.at[2 + i]).wait()
    pl.loop(0, rim)(faces)
    pl.loop(rim + lat_cells - 1, rows - 1)(faces)


def next_row(s, north, south_flux, east_face, north_face):
    flux_east = east_face * (pltpu.roll(s, s.shape[0] - 1, 0) - s)
    flux_north = north_face * (north - s)
    s = s + flux_east - pltpu.roll(flux_east, 1, 0) + flux_north - south_flux
    return s, flux_north


def inner_kernel(
    lat_cells, lon_cells, state_ref, west_ref, east_ref, east_face, north_face, *steps
):
    rim = ITERS

    @pl.loop(0, lat_cells)
    def _(r):
        widen(steps[0], r, r, lon_cells, state_ref, west_ref, east_ref)

    for step in range(ITERS):
        old, new = steps[step], steps[step + 1]

        def line(r, south):
            face = rim + r
            new[r], south = next_row(old[r], old[r + 1], south, east_face[face], north_face[face])
            return south

        south = north_face[rim + step] * (old[step + 1] - old[step])
        lax.fori_loop(step + 1, lat_cells - 1 - step, line, south)


def outer_kernel(lat_cells, lon_cells, next_ref, mate_ref, east_face, north_face, *refs):
    rim = ITERS
    steps = refs[: ITERS + 1]
    out_hbm, low_rows, high_rows, out_ref, sems = refs[ITERS + 1 :]

    def take(low, high):
        for r in range(rim):
            low_rows[0, r] = low[r]
            high_rows[0, r] = high[r]

    either(mate_ref, next_ref, take)

    def at(step, row):
        if row < step:
            return low_rows[step, row + rim - step]
        if row >= lat_cells - step:
            return high_rows[step, row - lat_cells + step]
        return steps[step][row]

    def write(row, s):
        out_ref[:, row, :] = s[SUB : SUB + lon_cells].T

    copies = []
    for rows, first in ((low_rows, -rim), (high_rows, lat_cells)):
        for step in range(1, ITERS + 1):
            start = first + step if first < 0 else first - step
            below = rim + start - 1
            south = north_face[below] * (at(step - 1, start) - at(step - 1, start - 1))
            for i in range(rim):
                r = start + i
                s, south = next_row(
                    at(step - 1, r), at(step - 1, r + 1), south,
                    east_face[rim + r], north_face[rim + r],
                )
                if step < ITERS:
                    rows[step, i] = s
                else:
                    write(r, s)
        inside = range(rim, SUB) if first < 0 else range(SUB, lat_cells - rim)
        for r in inside:
            write(r, steps[ITERS][r])
        side = 0 if first < 0 else 1
        ready = pl.ds(side * SUB, SUB)
        copies += fetch(
            [(out_ref.at[:, ready, :], out_hbm.at[:, ready, :])], sems.at[pl.ds(side, 1)]
        )
    for copy in copies:
        copy.wait()


def cost(microseconds):
    return pl.CostEstimate(
        flops=0, bytes_accessed=microseconds * 3_000_000, transcendentals=0
    )


def params(limit):
    return pltpu.CompilerParams(vmem_limit_bytes=limit)


def on_device(obs_rows, obs_tile, obs_cell, land_sea, zonal_rate, meridional_rate):
    count_x = lax.axis_size("gx")
    count_y = lax.axis_size("gy")
    devices = count_x * count_y
    owned, row_width = obs_rows.shape
    cap = 2 * owned // devices
    levels, lat_cells, lon_cells = land_sea.shape
    cells = lat_cells * lon_cells
    variables = row_width // levels
    rim = ITERS
    f32, i32 = jnp.float32, jnp.int32
    groups = owned // LANES
    sent = devices * (cap + 1)

    packed = pl.pallas_call(
        functools.partial(pack_kernel, cap, cells),
        out_shape=jax.ShapeDtypeStruct((sent, LANES), f32),
        in_specs=[HBM] * 3,
        out_specs=HBM,
        scratch_shapes=[
            pltpu.VMEM((groups, LANES), i32),
            pltpu.VMEM((groups, LANES), i32),
            pltpu.VMEM((owned, LANES), f32),
            pltpu.VMEM((sent, LANES), f32),
            pltpu.VMEM((groups, LANES), i32),
            pltpu.SMEM((groups, LANES), i32),
            pltpu.SemaphoreType.DMA,
            pltpu.SemaphoreType.DMA((3,)),
            pltpu.SemaphoreType.DMA((OUT_PARTS,)),
        ],
        compiler_params=params(63 << 20),
    )(obs_tile.reshape(groups, LANES), obs_cell.reshape(groups, LANES), obs_rows)
    got = lax.all_to_all(
        packed.reshape(sent, 1, LANES), ("gx", "gy"), split_axis=0, concat_axis=0, tiled=True
    ).reshape(sent, LANES)

    tile_ends = jax.ShapeDtypeStruct((lat_cells * SUB, LANES), f32)
    flat = jax.ShapeDtypeStruct((rim, lon_cells, LANES), f32)
    rates, r_ends, to_mate, to_next = pl.pallas_call(
        rates_kernel,
        out_shape=[jax.ShapeDtypeStruct((cells, LANES), f32), tile_ends, flat, flat],
        in_specs=[HBM] * 3,
        out_specs=[VMEM] * 4,
        scratch_shapes=[
            pltpu.VMEM(land_sea.shape, i32),
            pltpu.VMEM(land_sea.shape, f32),
            pltpu.VMEM(land_sea.shape, f32),
            pltpu.SemaphoreType.DMA((3,)),
        ],
        compiler_params=params(4 << 20),
        cost_estimate=cost(2),
    )(land_sea, zonal_rate, meridional_rate)
    r_first, r_second = to_both(r_ends, r_ends)
    width = lon_cells + 2 * SUB
    edge = jax.ShapeDtypeStruct((rim, width, LANES), f32)
    r_mate = lax.ppermute(to_mate, "gy", pairs("gy", 0))
    r_next = lax.ppermute(to_next, "gy", pairs("gy", 1, False))

    listed = (devices * cap // LANES, LANES)
    cell = pl.pallas_call(
        functools.partial(arrived_kernel, cap),
        out_shape=jax.ShapeDtypeStruct(listed, i32),
        in_specs=[VMEM],
        out_specs=VMEM,
        compiler_params=params(1 << 20),
    )(got)
    all_ends = ((lat_cells + 2 * rim) * SUB, LANES)
    s_ends = pl.pallas_call(
        functools.partial(ends_kernel, cap, lat_cells, lon_cells),
        out_shape=[jax.ShapeDtypeStruct((all_ends[0] // 2, LANES), f32)] * 2,
        in_specs=[VMEM] * 3 + [ANY] * 4,
        out_specs=[VMEM] * 2,
        scratch_shapes=[
            pltpu.VMEM(all_ends, f32),
            pltpu.VMEM((2, rim, 2 * SUB, LANES), f32),
            pltpu.SemaphoreType.DMA((4,)),
        ],
        compiler_params=params(2 << 20),
        cost_estimate=cost(1),
    )(got, cell, rates, r_next, r_mate, r_first, r_second)
    s_first, s_second = to_both(*s_ends)
    state = pl.pallas_call(
        functools.partial(land_kernel, cap),
        out_shape=jax.ShapeDtypeStruct((cells, LANES), f32),
        in_specs=[VMEM] * 3,
        out_specs=VMEM,
        scratch_shapes=[pltpu.SMEM(listed, i32), pltpu.SemaphoreType.DMA]
        + [pltpu.VMEM((cells + SUB, LANES), f32)] * ACCS,
        compiler_params=params(12 << 20),
        cost_estimate=cost(7),
    )(got, cell, rates)

    to_mate, to_next, s_west, s_east = pl.pallas_call(
        functools.partial(slabs_kernel, lat_cells, lon_cells),
        out_shape=[edge] * 2 + [jax.ShapeDtypeStruct(all_ends, f32)] * 2,
        in_specs=[VMEM] * 3,
        out_specs=[VMEM] * 4,
        compiler_params=params(1 << 20),
    )(state, s_first, s_second)
    s_next = lax.ppermute(to_next, "gy", pairs("gy", 1, False))
    s_mate = lax.ppermute(to_mate, "gy", pairs("gy", 0))
    wide = (lat_cells + 2 * rim, width, LANES)
    faces = pl.pallas_call(
        functools.partial(faces_kernel, lat_cells, lon_cells, lat_cells * count_y),
        out_shape=[jax.ShapeDtypeStruct(wide, f32)] * 2,
        in_specs=[VMEM] + [ANY] * 4 + [VMEM] * 2,
        out_specs=[VMEM] * 2,
        scratch_shapes=[
            pltpu.VMEM(wide, f32),
            pltpu.VMEM(tile_ends.shape, f32),
            pltpu.VMEM(tile_ends.shape, f32),
            pltpu.VMEM((2, *tile_ends.shape), f32),
            pltpu.SemaphoreType.DMA((4,)),
        ],
        compiler_params=params(4 << 20),
        cost_estimate=cost(2),
    )(rates, r_next, r_mate, r_first, r_second, s_west, s_east)
    steps = pl.pallas_call(
        functools.partial(inner_kernel, lat_cells, lon_cells),
        out_shape=[jax.ShapeDtypeStruct((lat_cells, width, LANES), f32)] * (ITERS + 1),
        in_specs=[VMEM] * 5,
        out_specs=[VMEM] * (ITERS + 1),
        compiler_params=params(2 << 20),
        cost_estimate=cost(2),
    )(state, s_west, s_east, *faces)
    out_shape = (row_width, lat_cells, lon_cells)
    out = pl.pallas_call(
        functools.partial(outer_kernel, lat_cells, lon_cells),
        out_shape=jax.ShapeDtypeStruct(out_shape, f32),
        in_specs=[VMEM] * (4 + ITERS + 1),
        out_specs=HBM,
        scratch_shapes=[pltpu.VMEM((ITERS, rim, width, LANES), f32)] * 2
        + [pltpu.VMEM(out_shape, f32), pltpu.SemaphoreType.DMA((2,))],
        compiler_params=params(6 << 20),
        cost_estimate=cost(3),
    )(s_next, s_mate, *faces, *steps)
    return out.reshape(variables, levels, lat_cells, lon_cells)


def solution(mesh):
    placed = (
        P(("gx", "gy"), None),
        P(("gx", "gy"), None),
        P(("gx", "gy")),
        P(None, "gy", "gx"),
        P(None, "gy", "gx"),
        P(None, "gy", "gx"),
    )
    return jax.shard_map(
        on_device, mesh=mesh, in_specs=placed, out_specs=P(None, None, "gy", "gx"), check_vma=False
    )
```

```python
import functools

import jax
import jax.numpy as jnp
from jax import lax
from jax.experimental import pallas as pl
from jax.experimental.pallas import tpu as pltpu
from jax.sharding import PartitionSpec as P

ITERS = 4
LANES = 128
SUB = 8
ACCS = 8
OUT_PARTS = 8
VMEM = pl.BlockSpec(memory_space=pltpu.VMEM)
ANY = pl.BlockSpec(memory_space=pl.ANY)
HBM = pl.BlockSpec(memory_space=pltpu.HBM)


def pairs(axis, start, closed=True):
    count = lax.axis_size(axis)
    firsts = range(start, count if closed else count - 1, 2)
    both = [(i, (i + 1) % count) for i in firsts]
    return both + [(b, a) for a, b in both]


def to_both(first, second):
    return lax.ppermute(first, "gx", pairs("gx", 0)), lax.ppermute(second, "gx", pairs("gx", 1))


def even_column():
    return lax.rem(lax.axis_index("gx"), 2) == 0


def west_east(first, second, west_ref, east_ref):
    even = even_column()
    west_ref[...] = jnp.where(even, second[...], first[...])
    east_ref[...] = jnp.where(even, first[...], second[...])


def column_ends(ref, lat_cells, lon_cells):
    first = lax.broadcasted_iota(jnp.int32, (SUB, LANES), 0) < SUB // 2
    return jnp.concatenate(
        [
            jnp.where(
                first,
                ref[pl.ds(r * lon_cells, SUB), :],
                ref[pl.ds((r + 1) * lon_cells - SUB, SUB), :],
            )
            for r in range(lat_cells)
        ],
        axis=0,
    )


def fetch(pairs, sems):
    copies = [pltpu.make_async_copy(a, b, sems.at[i]) for i, (a, b) in enumerate(pairs)]
    for copy in copies:
        copy.start()
    return copies


def rates_kernel(
    land_hbm, zonal_hbm, merid_hbm, out_ref, ends_ref, mate_ref, next_ref,
    land_ref, zonal_ref, merid_ref, sems,
):
    lat_cells, lon_cells = land_ref.shape[1:]
    for copy in fetch(
        [(land_hbm, land_ref), (zonal_hbm, zonal_ref), (merid_hbm, merid_ref)], sems
    ):
        copy.wait()
    for lat in range(lat_cells):
        ocean = land_ref[:, lat, :].astype(jnp.float32)
        both = jnp.concatenate(
            [zonal_ref[:, lat, :] * ocean, merid_ref[:, lat, :] * ocean], axis=0
        )
        out_ref[pl.ds(lat * lon_cells, lon_cells), :] = both.T
    ends_ref[...] = column_ends(out_ref, lat_cells, lon_cells)
    odd = is_odd()
    last = lat_cells - ITERS
    for ref, start in ((mate_ref, jnp.where(odd, 0, last)), (next_ref, jnp.where(odd, last, 0))):
        for r in range(ITERS):
            at = pl.multiple_of((start + r) * lon_cells, lon_cells)
            ref[r] = out_ref[pl.ds(at, lon_cells), :]


def pack_kernel(
    cap, cells, tile_hbm, cell_hbm, rows_hbm, out_hbm,
    tile_ref, cell_ref, rows_ref, out_ref, slot_vmem, slot_smem, sem, sems, out_sems,
):
    copies = fetch([(tile_hbm, tile_ref), (cell_hbm, cell_ref), (rows_hbm, rows_ref)], sems)
    out_ref[...] = jnp.zeros_like(out_ref)
    copies[0].wait()
    copies[1].wait()
    groups = tile_ref.shape[0]
    tiles = out_ref.shape[0] // (cap + 1)
    f32, bf16 = jnp.float32, jnp.bfloat16
    down = lax.broadcasted_iota(jnp.int32, (tiles, LANES), 0)
    earlier = (
        lax.broadcasted_iota(jnp.int32, (LANES, 2 * LANES), 0)
        < lax.broadcasted_iota(jnp.int32, (LANES, 2 * LANES), 1)
    ).astype(bf16)
    place = lax.broadcasted_iota(jnp.int32, (LANES, LANES), 0) % cap
    hits, counts, spots = [], [], []
    for g in range(groups):
        hits.append((down == tile_ref[pl.ds(g, 1), :]).astype(f32).astype(bf16))
        counts.append(jnp.dot(hits[g], earlier, preferred_element_type=f32))
    taken = jnp.zeros((tiles, LANES), f32)
    for g in range(groups):
        tile = tile_ref[pl.ds(g, 1), :]
        before = jnp.where(down == tile, counts[g][:, :LANES] + taken, 0.0)
        spots.append(jnp.sum(before, axis=0, keepdims=True).astype(jnp.int32))
        taken += counts[g][:, LANES:]
        slot_vmem[pl.ds(g, 1), :] = tile * (cap + 1) + spots[g]
    copy = pltpu.make_async_copy(slot_vmem, slot_smem, sem)
    copy.start()
    codes = jnp.zeros((tiles, 2 * LANES), f32)
    for g in range(groups):
        here = place == spots[g]
        code = cell_ref[pl.ds(g, 1), :] + 1
        parts = [jnp.where(here, part.astype(f32), 0.0) for part in (code >> 6, code & 63)]
        codes += lax.dot_general(
            hits[g], jnp.concatenate(parts, axis=0).astype(bf16), (((1,), (1,)), ((), ())),
            preferred_element_type=f32,
        )
    code = codes[:, :LANES] * 64.0 + codes[:, LANES:]
    out_ref[pl.ds(cap, tiles, stride=cap + 1), :] = jnp.where(
        code == 0.0, jnp.float32(cells), code - 1.0
    )
    copies[2].wait()
    copy.wait()

    @pl.loop(0, groups)
    def _(g):
        base = pl.multiple_of(g * LANES, LANES)
        for u in range(LANES):
            out_ref[pl.ds(slot_smem[g, u], 1), :] = rows_ref[pl.ds(base + u, 1), :]

    part = out_ref.shape[0] // OUT_PARTS
    spans = [pl.ds(i * part, part) for i in range(OUT_PARTS)]
    for copy in fetch([(out_ref.at[at], out_hbm.at[at]) for at in spans], out_sems):
        copy.wait()


def widen(dest, row, lat, lon_cells, main_ref, west_ref, east_ref):
    at = pl.multiple_of(lat * SUB, SUB)
    dest[row, pl.ds(0, SUB), :] = west_ref[pl.ds(at, SUB), :]
    dest[row, pl.ds(SUB + lon_cells, SUB), :] = east_ref[pl.ds(at, SUB), :]
    at = pl.multiple_of(lat * lon_cells, lon_cells)
    dest[row, pl.ds(SUB, lon_cells), :] = main_ref[pl.ds(at, lon_cells), :]


def slab(dest, north, lat_cells, lon_cells, main_ref, west_ref, east_ref):
    start = jnp.where(north, lat_cells - ITERS, 0)
    for r in range(ITERS):
        widen(dest, r, start + r, lon_cells, main_ref, west_ref, east_ref)


def slabs_kernel(
    lat_cells, lon_cells, main_ref, first_ref, second_ref, mate_ref, next_ref, west_ref, east_ref
):
    even = even_column()
    for q in range(first_ref.shape[0] // SUB):
        at = pl.ds(q * SUB, SUB)
        first, second = first_ref[at, :], second_ref[at, :]
        west = jnp.where(even, second, first)
        east = jnp.where(even, first, second)
        low, high = (pl.ds((2 * q + i) * SUB, SUB) for i in range(2))
        west_ref[low, :] = pltpu.roll(west, SUB // 2, 0)
        west_ref[high, :] = west
        east_ref[low, :] = east
        east_ref[high, :] = pltpu.roll(east, SUB // 2, 0)
    odd = is_odd()
    slab(next_ref, odd, lat_cells, lon_cells, main_ref, west_ref, east_ref)
    slab(mate_ref, jnp.logical_not(odd), lat_cells, lon_cells, main_ref, west_ref, east_ref)


def arrived_kernel(cap, got_ref, cell_ref):
    block = cap + 1
    sources = got_ref.shape[0] // block
    per = LANES // cap
    lane = lax.broadcasted_iota(jnp.int32, (sources // per, LANES), 1)
    found = jnp.zeros((sources // per, LANES), jnp.float32)
    for j in range(per):
        part = got_ref[pl.ds(block * j + cap, sources // per, stride=block * per), :]
        found = jnp.where(lane // cap == j, part, found)
    cell_ref[...] = found.astype(jnp.int32)


def ends_kernel(
    cap, lat_cells, lon_cells, got_ref, cell_ref, rates_ref, next_any, mate_any, *refs
):
    first_out, second_out, out_ref, rim_ref, sems = refs[-5:]
    sides = [pl.ds(0, SUB), pl.ds(lon_cells - SUB, SUB)]

    def tiles(i, ref):
        return [
            (ref.at[:, side, :], rim_ref.at[i, :, pl.ds(k * SUB, SUB), :])
            for k, side in enumerate(sides)
        ]

    def start(low, high):
        for i, ref in enumerate((low, high)):
            fetch(tiles(i, ref), sems.at[pl.ds(2 * i, 2)])

    either(mate_any, next_any, start)
    f32, bf16 = jnp.float32, jnp.bfloat16
    block = cap + 1
    per = LANES // cap
    ends = lat_cells * SUB
    place = lax.broadcasted_iota(jnp.int32, (ends, LANES), 0)
    column = place % SUB
    column = jnp.where(column < SUB // 2, column, column + lon_cells - SUB)
    place = place // SUB * lon_cells + column
    total = jnp.zeros((ends, 3 * LANES), f32)
    for m in range(0, cell_ref.shape[0], 2):
        hits = [(place == cell_ref[pl.ds(m + i, 1), :]).astype(f32).astype(bf16) for i in range(2)]
        left = jnp.concatenate(
            [got_ref[pl.ds((m * per + j) * block, cap), :] for j in range(2 * per)], axis=0
        )
        parts = []
        for _ in range(3):
            parts.append(left.astype(bf16))
            left = left - parts[-1].astype(f32)
        total += jnp.dot(
            jnp.concatenate(hits, axis=1), jnp.concatenate(parts, axis=1),
            preferred_element_type=f32,
        )
    total = total[:, :LANES] + total[:, LANES : 2 * LANES] + total[:, 2 * LANES :]
    ocean = column_ends(rates_ref, lat_cells, lon_cells) > 0.0
    out_ref[pl.ds(0, ends), :] = jnp.where(ocean, total, 0.0)

    first = lax.broadcasted_iota(jnp.int32, (SUB, LANES), 0) < SUB // 2
    for i in range(2):
        for k, (source, target) in enumerate(tiles(i, mate_any)):
            pltpu.make_async_copy(source, target, sems.at[2 * i + k]).wait()
        for r in range(ITERS):
            out_ref[pl.ds(ends + (i * ITERS + r) * SUB, SUB), :] = jnp.where(
                first, rim_ref[i, r, pl.ds(0, SUB), :], rim_ref[i, r, pl.ds(SUB, SUB), :]
            )
    even = even_column()
    for q in range(first_out.shape[0] // SUB):
        a, b = (out_ref[pl.ds((2 * q + i) * SUB, SUB), :] for i in range(2))
        west = jnp.where(first, a, pltpu.roll(b, SUB // 2, 0))
        east = jnp.where(first, pltpu.roll(a, SUB // 2, 0), b)
        at = pl.ds(q * SUB, SUB)
        first_out[at, :] = jnp.where(even, east, west)
        second_out[at, :] = jnp.where(even, west, east)


def land_kernel(cap, got_ref, cell_ref, rates_ref, out_ref, cell_smem, sem, *accs):
    block = cap + 1
    per = LANES // cap
    copy = pltpu.make_async_copy(cell_ref, cell_smem, sem)
    copy.start()
    for acc in accs:
        acc[...] = jnp.zeros_like(acc)
    copy.wait()

    @pl.loop(0, cell_ref.shape[0])
    def _(m):
        base = m * (block * per)
        for j in range(per):
            for p in range(cap):
                acc = accs[(j * cap + p) % len(accs)]
                at = pl.ds(cell_smem[m, j * cap + p], 1)
                acc[at, :] += got_ref[pl.ds(base + j * block + p, 1), :]

    step = 64

    @pl.loop(0, out_ref.shape[0] // step)
    def _(i):
        at = pl.ds(pl.multiple_of(i * step, step), step)
        total = accs[0][at, :]
        for acc in accs[1:]:
            total += acc[at, :]
        out_ref[at, :] = jnp.where(rates_ref[at, :] > 0.0, total, 0.0)


def is_odd():
    return lax.rem(lax.axis_index("gy"), 2) == 1


def either(from_mate, from_next, use):
    odd = is_odd()

    @pl.when(odd)
    def _():
        use(from_mate, from_next)

    @pl.when(jnp.logical_not(odd))
    def _():
        use(from_next, from_mate)


def faces_kernel(
    lat_cells, lon_cells, total_rows, rates_ref, next_any, mate_any, first_any, second_any,
    west_ends, east_ends, east_face, north_face, wide, west_ref, east_ref, pair_ref, sems,
):
    rim = ITERS
    rows = lat_cells + 2 * rim
    width = lon_cells + 2 * SUB
    main = pl.ds(SUB, lon_cells)
    outer = [wide.at[pl.ds(0, rim), main, :], wide.at[pl.ds(rim + lat_cells, rim), main, :]]
    ends = fetch([(first_any, pair_ref.at[0]), (second_any, pair_ref.at[1])], sems.at[pl.ds(0, 2)])

    def start(low, high):
        fetch([(low, outer[0]), (high, outer[1])], sems.at[pl.ds(2, 2)])

    either(mate_any, next_any, start)
    for r in range(rim):
        for i, row in enumerate((r, rim + lat_cells + r)):
            at = pl.ds((lat_cells + i * rim + r) * SUB, SUB)
            wide[row, pl.ds(0, SUB), :] = west_ends[at, :]
            wide[row, pl.ds(SUB + lon_cells, SUB), :] = east_ends[at, :]

    @pl.loop(0, lat_cells)
    def _(r):
        at = pl.multiple_of(r * lon_cells, lon_cells)
        wide[rim + r, main, :] = rates_ref[pl.ds(at, lon_cells), :]

    for copy in ends:
        copy.wait()
    west_east(pair_ref.at[0], pair_ref.at[1], west_ref, east_ref)
    for r in range(lat_cells):
        at = pl.ds(r * SUB, SUB)
        wide[rim + r, pl.ds(0, SUB), :] = west_ref[at, :]
        wide[rim + r, pl.ds(SUB + lon_cells, SUB), :] = east_ref[at, :]

    half = LANES // 2
    zonal_lane = lax.broadcasted_iota(jnp.int32, (width, LANES), 1) < half

    def faces(r):
        here = wide[r]
        ocean_east = pltpu.roll(here, width - 1, 0) > 0.0
        ocean_north = wide[r + 1] > 0.0
        swapped = pltpu.roll(here, half, 1)
        row = lax.rem(lax.axis_index("gy") * lat_cells + r - rim + total_rows, total_rows)
        east_face[r] = jnp.where(ocean_east, jnp.where(zonal_lane, here, swapped), 0.0)
        north_face[r] = jnp.where(
            ocean_north & (row != total_rows - 1), jnp.where(zonal_lane, swapped, here), 0.0
        )

    pl.loop(rim, rim + lat_cells - 1)(faces)
    for i in range(2):
        pltpu.make_async_copy(mate_any, outer[i], sems.at[2 + i]).wait()
    pl.loop(0, rim)(faces)
    pl.loop(rim + lat_cells - 1, rows - 1)(faces)


def next_row(s, north, south_flux, east_face, north_face):
    flux_east = east_face * (pltpu.roll(s, s.shape[0] - 1, 0) - s)
    flux_north = north_face * (north - s)
    s = s + flux_east - pltpu.roll(flux_east, 1, 0) + flux_north - south_flux
    return s, flux_north


def inner_kernel(
    lat_cells, lon_cells, state_ref, west_ref, east_ref, east_face, north_face, *steps
):
    rim = ITERS

    @pl.loop(0, lat_cells)
    def _(r):
        widen(steps[0], r, r, lon_cells, state_ref, west_ref, east_ref)

    for step in range(ITERS):
        old, new = steps[step], steps[step + 1]

        def line(r, south):
            face = rim + r
            new[r], south = next_row(old[r], old[r + 1], south, east_face[face], north_face[face])
            return south

        south = north_face[rim + step] * (old[step + 1] - old[step])
        lax.fori_loop(step + 1, lat_cells - 1 - step, line, south)


def outer_kernel(lat_cells, lon_cells, next_ref, mate_ref, east_face, north_face, *refs):
    rim = ITERS
    steps = refs[: ITERS + 1]
    out_hbm, low_rows, high_rows, out_ref, sems = refs[ITERS + 1 :]

    def take(low, high):
        for r in range(rim):
            low_rows[0, r] = low[r]
            high_rows[0, r] = high[r]

    either(mate_ref, next_ref, take)

    def at(step, row):
        if row < step:
            return low_rows[step, row + rim - step]
        if row >= lat_cells - step:
            return high_rows[step, row - lat_cells + step]
        return steps[step][row]

    def write(row, s):
        out_ref[:, row, :] = s[SUB : SUB + lon_cells].T

    copies = []
    for rows, first in ((low_rows, -rim), (high_rows, lat_cells)):
        for step in range(1, ITERS + 1):
            start = first + step if first < 0 else first - step
            below = rim + start - 1
            south = north_face[below] * (at(step - 1, start) - at(step - 1, start - 1))
            for i in range(rim):
                r = start + i
                s, south = next_row(
                    at(step - 1, r), at(step - 1, r + 1), south,
                    east_face[rim + r], north_face[rim + r],
                )
                if step < ITERS:
                    rows[step, i] = s
                else:
                    write(r, s)
        inside = range(rim, SUB) if first < 0 else range(SUB, lat_cells - rim)
        for r in inside:
            write(r, steps[ITERS][r])
        side = 0 if first < 0 else 1
        ready = pl.ds(side * SUB, SUB)
        copies += fetch(
            [(out_ref.at[:, ready, :], out_hbm.at[:, ready, :])], sems.at[pl.ds(side, 1)]
        )
    for copy in copies:
        copy.wait()


def cost(microseconds):
    return pl.CostEstimate(
        flops=0, bytes_accessed=microseconds * 3_000_000, transcendentals=0
    )


def params(limit):
    return pltpu.CompilerParams(vmem_limit_bytes=limit)


def on_device(obs_rows, obs_tile, obs_cell, land_sea, zonal_rate, meridional_rate):
    count_x = lax.axis_size("gx")
    count_y = lax.axis_size("gy")
    devices = count_x * count_y
    owned, row_width = obs_rows.shape
    cap = 2 * owned // devices
    levels, lat_cells, lon_cells = land_sea.shape
    cells = lat_cells * lon_cells
    variables = row_width // levels
    rim = ITERS
    f32, i32 = jnp.float32, jnp.int32
    groups = owned // LANES
    sent = devices * (cap + 1)

    packed = pl.pallas_call(
        functools.partial(pack_kernel, cap, cells),
        out_shape=jax.ShapeDtypeStruct((sent, LANES), f32),
        in_specs=[HBM] * 3,
        out_specs=HBM,
        scratch_shapes=[
            pltpu.VMEM((groups, LANES), i32),
            pltpu.VMEM((groups, LANES), i32),
            pltpu.VMEM((owned, LANES), f32),
            pltpu.VMEM((sent, LANES), f32),
            pltpu.VMEM((groups, LANES), i32),
            pltpu.SMEM((groups, LANES), i32),
            pltpu.SemaphoreType.DMA,
            pltpu.SemaphoreType.DMA((3,)),
            pltpu.SemaphoreType.DMA((OUT_PARTS,)),
        ],
        compiler_params=params(63 << 20),
    )(obs_tile.reshape(groups, LANES), obs_cell.reshape(groups, LANES), obs_rows)
    got = lax.all_to_all(
        packed.reshape(sent, 1, LANES), ("gx", "gy"), split_axis=0, concat_axis=0, tiled=True
    ).reshape(sent, LANES)

    tile_ends = jax.ShapeDtypeStruct((lat_cells * SUB, LANES), f32)
    flat = jax.ShapeDtypeStruct((rim, lon_cells, LANES), f32)
    rates, r_ends, to_mate, to_next = pl.pallas_call(
        rates_kernel,
        out_shape=[jax.ShapeDtypeStruct((cells, LANES), f32), tile_ends, flat, flat],
        in_specs=[HBM] * 3,
        out_specs=[VMEM] * 4,
        scratch_shapes=[
            pltpu.VMEM(land_sea.shape, i32),
            pltpu.VMEM(land_sea.shape, f32),
            pltpu.VMEM(land_sea.shape, f32),
            pltpu.SemaphoreType.DMA((3,)),
        ],
        compiler_params=params(4 << 20),
        cost_estimate=cost(2),
    )(land_sea, zonal_rate, meridional_rate)
    r_first, r_second = to_both(r_ends, r_ends)
    width = lon_cells + 2 * SUB
    edge = jax.ShapeDtypeStruct((rim, width, LANES), f32)
    r_mate = lax.ppermute(to_mate, "gy", pairs("gy", 0))
    r_next = lax.ppermute(to_next, "gy", pairs("gy", 1, False))

    listed = (devices * cap // LANES, LANES)
    cell = pl.pallas_call(
        functools.partial(arrived_kernel, cap),
        out_shape=jax.ShapeDtypeStruct(listed, i32),
        in_specs=[VMEM],
        out_specs=VMEM,
        compiler_params=params(1 << 20),
    )(got)
    all_ends = ((lat_cells + 2 * rim) * SUB, LANES)
    s_ends = pl.pallas_call(
        functools.partial(ends_kernel, cap, lat_cells, lon_cells),
        out_shape=[jax.ShapeDtypeStruct((all_ends[0] // 2, LANES), f32)] * 2,
        in_specs=[VMEM] * 3 + [ANY] * 4,
        out_specs=[VMEM] * 2,
        scratch_shapes=[
            pltpu.VMEM(all_ends, f32),
            pltpu.VMEM((2, rim, 2 * SUB, LANES), f32),
            pltpu.SemaphoreType.DMA((4,)),
        ],
        compiler_params=params(2 << 20),
        cost_estimate=cost(1),
    )(got, cell, rates, r_next, r_mate, r_first, r_second)
    s_first, s_second = to_both(*s_ends)
    state = pl.pallas_call(
        functools.partial(land_kernel, cap),
        out_shape=jax.ShapeDtypeStruct((cells, LANES), f32),
        in_specs=[VMEM] * 3,
        out_specs=VMEM,
        scratch_shapes=[pltpu.SMEM(listed, i32), pltpu.SemaphoreType.DMA]
        + [pltpu.VMEM((cells + SUB, LANES), f32)] * ACCS,
        compiler_params=params(12 << 20),
        cost_estimate=cost(7),
    )(got, cell, rates)

    to_mate, to_next, s_west, s_east = pl.pallas_call(
        functools.partial(slabs_kernel, lat_cells, lon_cells),
        out_shape=[edge] * 2 + [jax.ShapeDtypeStruct(all_ends, f32)] * 2,
        in_specs=[VMEM] * 3,
        out_specs=[VMEM] * 4,
        compiler_params=params(1 << 20),
    )(state, s_first, s_second)
    s_next = lax.ppermute(to_next, "gy", pairs("gy", 1, False))
    s_mate = lax.ppermute(to_mate, "gy", pairs("gy", 0))
    wide = (lat_cells + 2 * rim, width, LANES)
    faces = pl.pallas_call(
        functools.partial(faces_kernel, lat_cells, lon_cells, lat_cells * count_y),
        out_shape=[jax.ShapeDtypeStruct(wide, f32)] * 2,
        in_specs=[VMEM] + [ANY] * 4 + [VMEM] * 2,
        out_specs=[VMEM] * 2,
        scratch_shapes=[
            pltpu.VMEM(wide, f32),
            pltpu.VMEM(tile_ends.shape, f32),
            pltpu.VMEM(tile_ends.shape, f32),
            pltpu.VMEM((2, *tile_ends.shape), f32),
            pltpu.SemaphoreType.DMA((4,)),
        ],
        compiler_params=params(4 << 20),
        cost_estimate=cost(2),
    )(rates, r_next, r_mate, r_first, r_second, s_west, s_east)
    steps = pl.pallas_call(
        functools.partial(inner_kernel, lat_cells, lon_cells),
        out_shape=[jax.ShapeDtypeStruct((lat_cells, width, LANES), f32)] * (ITERS + 1),
        in_specs=[VMEM] * 5,
        out_specs=[VMEM] * (ITERS + 1),
        compiler_params=params(2 << 20),
        cost_estimate=cost(2),
    )(state, s_west, s_east, *faces)
    out_shape = (row_width, lat_cells, lon_cells)
    out = pl.pallas_call(
        functools.partial(outer_kernel, lat_cells, lon_cells),
        out_shape=jax.ShapeDtypeStruct(out_shape, f32),
        in_specs=[VMEM] * (4 + ITERS + 1),
        out_specs=HBM,
        scratch_shapes=[pltpu.VMEM((ITERS, rim, width, LANES), f32)] * 2
        + [pltpu.VMEM(out_shape, f32), pltpu.SemaphoreType.DMA((2,))],
        compiler_params=params(6 << 20),
        cost_estimate=cost(3),
    )(s_next, s_mate, *faces, *steps)
    return out.reshape(variables, levels, lat_cells, lon_cells)


def solution(mesh):
    placed = (
        P(("gx", "gy"), None),
        P(("gx", "gy"), None),
        P(("gx", "gy")),
        P(None, "gy", "gx"),
        P(None, "gy", "gx"),
        P(None, "gy", "gx"),
    )
    return jax.shard_map(
        on_device, mesh=mesh, in_specs=placed, out_specs=P(None, None, "gy", "gx"), check_vma=False
    )
```

```python
import functools

import jax
import jax.numpy as jnp
from jax import lax
from jax.experimental import pallas as pl
from jax.experimental.pallas import tpu as pltpu
from jax.sharding import PartitionSpec as P

ITERS = 4
LANES = 128
SUB = 8
ACCS = 6
OUT_PARTS = 8
VMEM = pl.BlockSpec(memory_space=pltpu.VMEM)
ANY = pl.BlockSpec(memory_space=pl.ANY)
HBM = pl.BlockSpec(memory_space=pltpu.HBM)


def pairs(axis, start, closed=True):
    count = lax.axis_size(axis)
    firsts = range(start, count if closed else count - 1, 2)
    both = [(i, (i + 1) % count) for i in firsts]
    return both + [(b, a) for a, b in both]


def to_both(first, second):
    return lax.ppermute(first, "gx", pairs("gx", 0)), lax.ppermute(second, "gx", pairs("gx", 1))


def even_column():
    return lax.rem(lax.axis_index("gx"), 2) == 0


def west_east(first, second, west_ref, east_ref):
    even = even_column()
    west_ref[...] = jnp.where(even, second[...], first[...])
    east_ref[...] = jnp.where(even, first[...], second[...])


def column_ends(ref, lat_cells, lon_cells):
    first = lax.broadcasted_iota(jnp.int32, (SUB, LANES), 0) < SUB // 2
    return jnp.concatenate(
        [
            jnp.where(
                first,
                ref[pl.ds(r * lon_cells, SUB), :],
                ref[pl.ds((r + 1) * lon_cells - SUB, SUB), :],
            )
            for r in range(lat_cells)
        ],
        axis=0,
    )


def fetch(pairs, sems):
    copies = [pltpu.make_async_copy(a, b, sems.at[i]) for i, (a, b) in enumerate(pairs)]
    for copy in copies:
        copy.start()
    return copies


def rates_kernel(
    land_hbm, zonal_hbm, merid_hbm, out_ref, ends_ref, mate_ref, next_ref,
    land_ref, zonal_ref, merid_ref, sems,
):
    lat_cells, lon_cells = land_ref.shape[1:]
    for copy in fetch(
        [(land_hbm, land_ref), (zonal_hbm, zonal_ref), (merid_hbm, merid_ref)], sems
    ):
        copy.wait()
    for lat in range(lat_cells):
        ocean = land_ref[:, lat, :].astype(jnp.float32)
        both = jnp.concatenate(
            [zonal_ref[:, lat, :] * ocean, merid_ref[:, lat, :] * ocean], axis=0
        )
        out_ref[pl.ds(lat * lon_cells, lon_cells), :] = both.T
    ends_ref[...] = column_ends(out_ref, lat_cells, lon_cells)
    odd = is_odd()
    last = lat_cells - ITERS
    for ref, start in ((mate_ref, jnp.where(odd, 0, last)), (next_ref, jnp.where(odd, last, 0))):
        for r in range(ITERS):
            at = pl.multiple_of((start + r) * lon_cells, lon_cells)
            ref[r] = out_ref[pl.ds(at, lon_cells), :]


def pack_kernel(
    cap, cells, tile_hbm, cell_hbm, rows_hbm, out_hbm,
    tile_ref, cell_ref, rows_ref, out_ref, slot_vmem, slot_smem, sem, sems, out_sems,
):
    copies = fetch([(tile_hbm, tile_ref), (cell_hbm, cell_ref), (rows_hbm, rows_ref)], sems)
    out_ref[...] = jnp.zeros_like(out_ref)
    copies[0].wait()
    copies[1].wait()
    groups = tile_ref.shape[0]
    tiles = out_ref.shape[0] // (cap + 1)
    f32, bf16 = jnp.float32, jnp.bfloat16
    down = lax.broadcasted_iota(jnp.int32, (tiles, LANES), 0)
    earlier = (
        lax.broadcasted_iota(jnp.int32, (LANES, 2 * LANES), 0)
        < lax.broadcasted_iota(jnp.int32, (LANES, 2 * LANES), 1)
    ).astype(bf16)
    place = lax.broadcasted_iota(jnp.int32, (LANES, LANES), 0) % cap
    hits, counts, spots = [], [], []
    for g in range(groups):
        hits.append((down == tile_ref[pl.ds(g, 1), :]).astype(f32).astype(bf16))
        counts.append(jnp.dot(hits[g], earlier, preferred_element_type=f32))
    taken = jnp.zeros((tiles, LANES), f32)
    for g in range(groups):
        tile = tile_ref[pl.ds(g, 1), :]
        before = jnp.where(down == tile, counts[g][:, :LANES] + taken, 0.0)
        spots.append(jnp.sum(before, axis=0, keepdims=True).astype(jnp.int32))
        taken += counts[g][:, LANES:]
        slot_vmem[pl.ds(g, 1), :] = tile * (cap + 1) + spots[g]
    copy = pltpu.make_async_copy(slot_vmem, slot_smem, sem)
    copy.start()
    codes = jnp.zeros((tiles, 2 * LANES), f32)
    for g in range(groups):
        here = place == spots[g]
        code = cell_ref[pl.ds(g, 1), :] + 1
        parts = [jnp.where(here, part.astype(f32), 0.0) for part in (code >> 6, code & 63)]
        codes += lax.dot_general(
            hits[g], jnp.concatenate(parts, axis=0).astype(bf16), (((1,), (1,)), ((), ())),
            preferred_element_type=f32,
        )
    code = codes[:, :LANES] * 64.0 + codes[:, LANES:]
    out_ref[pl.ds(cap, tiles, stride=cap + 1), :] = jnp.where(
        code == 0.0, jnp.float32(cells), code - 1.0
    )
    copies[2].wait()
    copy.wait()

    @pl.loop(0, groups)
    def _(g):
        base = pl.multiple_of(g * LANES, LANES)
        for u in range(LANES):
            out_ref[pl.ds(slot_smem[g, u], 1), :] = rows_ref[pl.ds(base + u, 1), :]

    part = out_ref.shape[0] // OUT_PARTS
    spans = [pl.ds(i * part, part) for i in range(OUT_PARTS)]
    for copy in fetch([(out_ref.at[at], out_hbm.at[at]) for at in spans], out_sems):
        copy.wait()


def widen(dest, row, lat, lon_cells, main_ref, west_ref, east_ref):
    at = pl.multiple_of(lat * SUB, SUB)
    dest[row, pl.ds(0, SUB), :] = west_ref[pl.ds(at, SUB), :]
    dest[row, pl.ds(SUB + lon_cells, SUB), :] = east_ref[pl.ds(at, SUB), :]
    at = pl.multiple_of(lat * lon_cells, lon_cells)
    dest[row, pl.ds(SUB, lon_cells), :] = main_ref[pl.ds(at, lon_cells), :]


def slab(dest, north, lat_cells, lon_cells, main_ref, west_ref, east_ref):
    start = jnp.where(north, lat_cells - ITERS, 0)
    for r in range(ITERS):
        widen(dest, r, start + r, lon_cells, main_ref, west_ref, east_ref)


def slabs_kernel(
    lat_cells, lon_cells, main_ref, first_ref, second_ref, mate_ref, next_ref, west_ref, east_ref
):
    even = even_column()
    for q in range(first_ref.shape[0] // SUB):
        at = pl.ds(q * SUB, SUB)
        first, second = first_ref[at, :], second_ref[at, :]
        west = jnp.where(even, second, first)
        east = jnp.where(even, first, second)
        low, high = (pl.ds((2 * q + i) * SUB, SUB) for i in range(2))
        west_ref[low, :] = pltpu.roll(west, SUB // 2, 0)
        west_ref[high, :] = west
        east_ref[low, :] = east
        east_ref[high, :] = pltpu.roll(east, SUB // 2, 0)
    odd = is_odd()
    slab(next_ref, odd, lat_cells, lon_cells, main_ref, west_ref, east_ref)
    slab(mate_ref, jnp.logical_not(odd), lat_cells, lon_cells, main_ref, west_ref, east_ref)


def arrived_kernel(cap, got_ref, cell_ref):
    block = cap + 1
    sources = got_ref.shape[0] // block
    per = LANES // cap
    lane = lax.broadcasted_iota(jnp.int32, (sources // per, LANES), 1)
    found = jnp.zeros((sources // per, LANES), jnp.float32)
    for j in range(per):
        part = got_ref[pl.ds(block * j + cap, sources // per, stride=block * per), :]
        found = jnp.where(lane // cap == j, part, found)
    cell_ref[...] = found.astype(jnp.int32)


def ends_kernel(
    cap, lat_cells, lon_cells, got_ref, cell_ref, rates_ref, next_any, mate_any, *refs
):
    first_out, second_out, out_ref, rim_ref, sems = refs[-5:]
    sides = [pl.ds(0, SUB), pl.ds(lon_cells - SUB, SUB)]

    def tiles(i, ref):
        return [
            (ref.at[:, side, :], rim_ref.at[i, :, pl.ds(k * SUB, SUB), :])
            for k, side in enumerate(sides)
        ]

    def start(low, high):
        for i, ref in enumerate((low, high)):
            fetch(tiles(i, ref), sems.at[pl.ds(2 * i, 2)])

    either(mate_any, next_any, start)
    f32, bf16 = jnp.float32, jnp.bfloat16
    block = cap + 1
    per = LANES // cap
    ends = lat_cells * SUB
    place = lax.broadcasted_iota(jnp.int32, (ends, LANES), 0)
    column = place % SUB
    column = jnp.where(column < SUB // 2, column, column + lon_cells - SUB)
    place = place // SUB * lon_cells + column
    total = jnp.zeros((ends, 3 * LANES), f32)
    for m in range(0, cell_ref.shape[0], 2):
        hits = [(place == cell_ref[pl.ds(m + i, 1), :]).astype(f32).astype(bf16) for i in range(2)]
        left = jnp.concatenate(
            [got_ref[pl.ds((m * per + j) * block, cap), :] for j in range(2 * per)], axis=0
        )
        parts = []
        for _ in range(3):
            parts.append(left.astype(bf16))
            left = left - parts[-1].astype(f32)
        total += jnp.dot(
            jnp.concatenate(hits, axis=1), jnp.concatenate(parts, axis=1),
            preferred_element_type=f32,
        )
    total = total[:, :LANES] + total[:, LANES : 2 * LANES] + total[:, 2 * LANES :]
    ocean = column_ends(rates_ref, lat_cells, lon_cells) > 0.0
    out_ref[pl.ds(0, ends), :] = jnp.where(ocean, total, 0.0)

    first = lax.broadcasted_iota(jnp.int32, (SUB, LANES), 0) < SUB // 2
    for i in range(2):
        for k, (source, target) in enumerate(tiles(i, mate_any)):
            pltpu.make_async_copy(source, target, sems.at[2 * i + k]).wait()
        for r in range(ITERS):
            out_ref[pl.ds(ends + (i * ITERS + r) * SUB, SUB), :] = jnp.where(
                first, rim_ref[i, r, pl.ds(0, SUB), :], rim_ref[i, r, pl.ds(SUB, SUB), :]
            )
    even = even_column()
    for q in range(first_out.shape[0] // SUB):
        a, b = (out_ref[pl.ds((2 * q + i) * SUB, SUB), :] for i in range(2))
        west = jnp.where(first, a, pltpu.roll(b, SUB // 2, 0))
        east = jnp.where(first, pltpu.roll(a, SUB // 2, 0), b)
        at = pl.ds(q * SUB, SUB)
        first_out[at, :] = jnp.where(even, east, west)
        second_out[at, :] = jnp.where(even, west, east)


def land_kernel(cap, got_ref, cell_ref, rates_ref, out_ref, cell_smem, sem, *accs):
    block = cap + 1
    per = LANES // cap
    copy = pltpu.make_async_copy(cell_ref, cell_smem, sem)
    copy.start()
    for acc in accs:
        acc[...] = jnp.zeros_like(acc)
    copy.wait()

    @pl.loop(0, cell_ref.shape[0])
    def _(m):
        base = m * (block * per)
        for j in range(per):
            for p in range(cap):
                acc = accs[(j * cap + p) % len(accs)]
                at = pl.ds(cell_smem[m, j * cap + p], 1)
                acc[at, :] += got_ref[pl.ds(base + j * block + p, 1), :]

    step = 64

    @pl.loop(0, out_ref.shape[0] // step)
    def _(i):
        at = pl.ds(pl.multiple_of(i * step, step), step)
        total = accs[0][at, :]
        for acc in accs[1:]:
            total += acc[at, :]
        out_ref[at, :] = jnp.where(rates_ref[at, :] > 0.0, total, 0.0)


def is_odd():
    return lax.rem(lax.axis_index("gy"), 2) == 1


def either(from_mate, from_next, use):
    odd = is_odd()

    @pl.when(odd)
    def _():
        use(from_mate, from_next)

    @pl.when(jnp.logical_not(odd))
    def _():
        use(from_next, from_mate)


def faces_kernel(
    lat_cells, lon_cells, total_rows, rates_ref, next_any, mate_any, first_any, second_any,
    west_ends, east_ends, east_face, north_face, wide, west_ref, east_ref, pair_ref, sems,
):
    rim = ITERS
    rows = lat_cells + 2 * rim
    width = lon_cells + 2 * SUB
    main = pl.ds(SUB, lon_cells)
    outer = [wide.at[pl.ds(0, rim), main, :], wide.at[pl.ds(rim + lat_cells, rim), main, :]]
    ends = fetch([(first_any, pair_ref.at[0]), (second_any, pair_ref.at[1])], sems.at[pl.ds(0, 2)])

    def start(low, high):
        fetch([(low, outer[0]), (high, outer[1])], sems.at[pl.ds(2, 2)])

    either(mate_any, next_any, start)
    for r in range(rim):
        for i, row in enumerate((r, rim + lat_cells + r)):
            at = pl.ds((lat_cells + i * rim + r) * SUB, SUB)
            wide[row, pl.ds(0, SUB), :] = west_ends[at, :]
            wide[row, pl.ds(SUB + lon_cells, SUB), :] = east_ends[at, :]

    @pl.loop(0, lat_cells)
    def _(r):
        at = pl.multiple_of(r * lon_cells, lon_cells)
        wide[rim + r, main, :] = rates_ref[pl.ds(at, lon_cells), :]

    for copy in ends:
        copy.wait()
    west_east(pair_ref.at[0], pair_ref.at[1], west_ref, east_ref)
    for r in range(lat_cells):
        at = pl.ds(r * SUB, SUB)
        wide[rim + r, pl.ds(0, SUB), :] = west_ref[at, :]
        wide[rim + r, pl.ds(SUB + lon_cells, SUB), :] = east_ref[at, :]

    half = LANES // 2
    zonal_lane = lax.broadcasted_iota(jnp.int32, (width, LANES), 1) < half

    def faces(r):
        here = wide[r]
        ocean_east = pltpu.roll(here, width - 1, 0) > 0.0
        ocean_north = wide[r + 1] > 0.0
        swapped = pltpu.roll(here, half, 1)
        row = lax.rem(lax.axis_index("gy") * lat_cells + r - rim + total_rows, total_rows)
        east_face[r] = jnp.where(ocean_east, jnp.where(zonal_lane, here, swapped), 0.0)
        north_face[r] = jnp.where(
            ocean_north & (row != total_rows - 1), jnp.where(zonal_lane, swapped, here), 0.0
        )

    pl.loop(rim, rim + lat_cells - 1)(faces)
    for i in range(2):
        pltpu.make_async_copy(mate_any, outer[i], sems.at[2 + i]).wait()
    pl.loop(0, rim)(faces)
    pl.loop(rim + lat_cells - 1, rows - 1)(faces)


def next_row(s, north, south_flux, east_face, north_face):
    flux_east = east_face * (pltpu.roll(s, s.shape[0] - 1, 0) - s)
    flux_north = north_face * (north - s)
    s = s + flux_east - pltpu.roll(flux_east, 1, 0) + flux_north - south_flux
    return s, flux_north


def inner_kernel(
    lat_cells, lon_cells, state_ref, west_ref, east_ref, east_face, north_face, *steps
):
    rim = ITERS

    @pl.loop(0, lat_cells)
    def _(r):
        widen(steps[0], r, r, lon_cells, state_ref, west_ref, east_ref)

    for step in range(ITERS):
        old, new = steps[step], steps[step + 1]

        def line(r, south):
            face = rim + r
            new[r], south = next_row(old[r], old[r + 1], south, east_face[face], north_face[face])
            return south

        south = north_face[rim + step] * (old[step + 1] - old[step])
        lax.fori_loop(step + 1, lat_cells - 1 - step, line, south)


def outer_kernel(lat_cells, lon_cells, next_ref, mate_ref, east_face, north_face, *refs):
    rim = ITERS
    steps = refs[: ITERS + 1]
    out_hbm, low_rows, high_rows, out_ref, sems = refs[ITERS + 1 :]

    def take(low, high):
        for r in range(rim):
            low_rows[0, r] = low[r]
            high_rows[0, r] = high[r]

    either(mate_ref, next_ref, take)

    def at(step, row):
        if row < step:
            return low_rows[step, row + rim - step]
        if row >= lat_cells - step:
            return high_rows[step, row - lat_cells + step]
        return steps[step][row]

    def write(row, s):
        out_ref[:, row, :] = s[SUB : SUB + lon_cells].T

    copies = []
    for rows, first in ((low_rows, -rim), (high_rows, lat_cells)):
        for step in range(1, ITERS + 1):
            start = first + step if first < 0 else first - step
            below = rim + start - 1
            south = north_face[below] * (at(step - 1, start) - at(step - 1, start - 1))
            for i in range(rim):
                r = start + i
                s, south = next_row(
                    at(step - 1, r), at(step - 1, r + 1), south,
                    east_face[rim + r], north_face[rim + r],
                )
                if step < ITERS:
                    rows[step, i] = s
                else:
                    write(r, s)
        inside = range(rim, SUB) if first < 0 else range(SUB, lat_cells - rim)
        for r in inside:
            write(r, steps[ITERS][r])
        side = 0 if first < 0 else 1
        ready = pl.ds(side * SUB, SUB)
        copies += fetch(
            [(out_ref.at[:, ready, :], out_hbm.at[:, ready, :])], sems.at[pl.ds(side, 1)]
        )
    for copy in copies:
        copy.wait()


def cost(microseconds):
    return pl.CostEstimate(
        flops=0, bytes_accessed=microseconds * 3_000_000, transcendentals=0
    )


def params(limit):
    return pltpu.CompilerParams(vmem_limit_bytes=limit)


def on_device(obs_rows, obs_tile, obs_cell, land_sea, zonal_rate, meridional_rate):
    count_x = lax.axis_size("gx")
    count_y = lax.axis_size("gy")
    devices = count_x * count_y
    owned, row_width = obs_rows.shape
    cap = 2 * owned // devices
    levels, lat_cells, lon_cells = land_sea.shape
    cells = lat_cells * lon_cells
    variables = row_width // levels
    rim = ITERS
    f32, i32 = jnp.float32, jnp.int32
    groups = owned // LANES
    sent = devices * (cap + 1)

    packed = pl.pallas_call(
        functools.partial(pack_kernel, cap, cells),
        out_shape=jax.ShapeDtypeStruct((sent, LANES), f32),
        in_specs=[HBM] * 3,
        out_specs=HBM,
        scratch_shapes=[
            pltpu.VMEM((groups, LANES), i32),
            pltpu.VMEM((groups, LANES), i32),
            pltpu.VMEM((owned, LANES), f32),
            pltpu.VMEM((sent, LANES), f32),
            pltpu.VMEM((groups, LANES), i32),
            pltpu.SMEM((groups, LANES), i32),
            pltpu.SemaphoreType.DMA,
            pltpu.SemaphoreType.DMA((3,)),
            pltpu.SemaphoreType.DMA((OUT_PARTS,)),
        ],
        compiler_params=params(63 << 20),
    )(obs_tile.reshape(groups, LANES), obs_cell.reshape(groups, LANES), obs_rows)
    got = lax.all_to_all(
        packed.reshape(sent, 1, LANES), ("gx", "gy"), split_axis=0, concat_axis=0, tiled=True
    ).reshape(sent, LANES)

    tile_ends = jax.ShapeDtypeStruct((lat_cells * SUB, LANES), f32)
    flat = jax.ShapeDtypeStruct((rim, lon_cells, LANES), f32)
    rates, r_ends, to_mate, to_next = pl.pallas_call(
        rates_kernel,
        out_shape=[jax.ShapeDtypeStruct((cells, LANES), f32), tile_ends, flat, flat],
        in_specs=[HBM] * 3,
        out_specs=[VMEM] * 4,
        scratch_shapes=[
            pltpu.VMEM(land_sea.shape, i32),
            pltpu.VMEM(land_sea.shape, f32),
            pltpu.VMEM(land_sea.shape, f32),
            pltpu.SemaphoreType.DMA((3,)),
        ],
        compiler_params=params(4 << 20),
        cost_estimate=cost(2),
    )(land_sea, zonal_rate, meridional_rate)
    r_first, r_second = to_both(r_ends, r_ends)
    width = lon_cells + 2 * SUB
    edge = jax.ShapeDtypeStruct((rim, width, LANES), f32)
    r_mate = lax.ppermute(to_mate, "gy", pairs("gy", 0))
    r_next = lax.ppermute(to_next, "gy", pairs("gy", 1, False))

    listed = (devices * cap // LANES, LANES)
    cell = pl.pallas_call(
        functools.partial(arrived_kernel, cap),
        out_shape=jax.ShapeDtypeStruct(listed, i32),
        in_specs=[VMEM],
        out_specs=VMEM,
        compiler_params=params(1 << 20),
    )(got)
    all_ends = ((lat_cells + 2 * rim) * SUB, LANES)
    s_ends = pl.pallas_call(
        functools.partial(ends_kernel, cap, lat_cells, lon_cells),
        out_shape=[jax.ShapeDtypeStruct((all_ends[0] // 2, LANES), f32)] * 2,
        in_specs=[VMEM] * 3 + [ANY] * 4,
        out_specs=[VMEM] * 2,
        scratch_shapes=[
            pltpu.VMEM(all_ends, f32),
            pltpu.VMEM((2, rim, 2 * SUB, LANES), f32),
            pltpu.SemaphoreType.DMA((4,)),
        ],
        compiler_params=params(2 << 20),
        cost_estimate=cost(1),
    )(got, cell, rates, r_next, r_mate, r_first, r_second)
    s_first, s_second = to_both(*s_ends)
    state = pl.pallas_call(
        functools.partial(land_kernel, cap),
        out_shape=jax.ShapeDtypeStruct((cells, LANES), f32),
        in_specs=[VMEM] * 3,
        out_specs=VMEM,
        scratch_shapes=[pltpu.SMEM(listed, i32), pltpu.SemaphoreType.DMA]
        + [pltpu.VMEM((cells + SUB, LANES), f32)] * ACCS,
        compiler_params=params(12 << 20),
        cost_estimate=cost(7),
    )(got, cell, rates)

    to_mate, to_next, s_west, s_east = pl.pallas_call(
        functools.partial(slabs_kernel, lat_cells, lon_cells),
        out_shape=[edge] * 2 + [jax.ShapeDtypeStruct(all_ends, f32)] * 2,
        in_specs=[VMEM] * 3,
        out_specs=[VMEM] * 4,
        compiler_params=params(1 << 20),
    )(state, s_first, s_second)
    s_next = lax.ppermute(to_next, "gy", pairs("gy", 1, False))
    s_mate = lax.ppermute(to_mate, "gy", pairs("gy", 0))
    wide = (lat_cells + 2 * rim, width, LANES)
    faces = pl.pallas_call(
        functools.partial(faces_kernel, lat_cells, lon_cells, lat_cells * count_y),
        out_shape=[jax.ShapeDtypeStruct(wide, f32)] * 2,
        in_specs=[VMEM] + [ANY] * 4 + [VMEM] * 2,
        out_specs=[VMEM] * 2,
        scratch_shapes=[
            pltpu.VMEM(wide, f32),
            pltpu.VMEM(tile_ends.shape, f32),
            pltpu.VMEM(tile_ends.shape, f32),
            pltpu.VMEM((2, *tile_ends.shape), f32),
            pltpu.SemaphoreType.DMA((4,)),
        ],
        compiler_params=params(4 << 20),
        cost_estimate=cost(2),
    )(rates, r_next, r_mate, r_first, r_second, s_west, s_east)
    steps = pl.pallas_call(
        functools.partial(inner_kernel, lat_cells, lon_cells),
        out_shape=[jax.ShapeDtypeStruct((lat_cells, width, LANES), f32)] * (ITERS + 1),
        in_specs=[VMEM] * 5,
        out_specs=[VMEM] * (ITERS + 1),
        compiler_params=params(2 << 20),
        cost_estimate=cost(2),
    )(state, s_west, s_east, *faces)
    out_shape = (row_width, lat_cells, lon_cells)
    out = pl.pallas_call(
        functools.partial(outer_kernel, lat_cells, lon_cells),
        out_shape=jax.ShapeDtypeStruct(out_shape, f32),
        in_specs=[VMEM] * (4 + ITERS + 1),
        out_specs=HBM,
        scratch_shapes=[pltpu.VMEM((ITERS, rim, width, LANES), f32)] * 2
        + [pltpu.VMEM(out_shape, f32), pltpu.SemaphoreType.DMA((2,))],
        compiler_params=params(6 << 20),
        cost_estimate=cost(3),
    )(s_next, s_mate, *faces, *steps)
    return out.reshape(variables, levels, lat_cells, lon_cells)


def solution(mesh):
    placed = (
        P(("gx", "gy"), None),
        P(("gx", "gy"), None),
        P(("gx", "gy")),
        P(None, "gy", "gx"),
        P(None, "gy", "gx"),
        P(None, "gy", "gx"),
    )
    return jax.shard_map(
        on_device, mesh=mesh, in_specs=placed, out_specs=P(None, None, "gy", "gx"), check_vma=False
    )
```
